256 devices in a mesh: dom: 64 (over y, x, z_hi, core), row: 4 (over z_lo).
Axes of the slice: x: 4, y: 4, z: 8 (z_hi: 2, z_lo: 4; z = z_hi * 4 + z_lo), core: 2. Of those that a mesh axis runs over, the one named last changes fastest.
Arguments:
- state: float32 [3, 64, 64, 4096], P(None, 'dom', 'row'), may hold values from -1.5 to 3, as said below
- rain: float32 [64, 64, 4096], P('dom', 'row'), may hold values from 0 to 0.5
- ground: float32 [64, 4096], P('row'), may hold values from 0 to 1
- counts: int32 [64], replicated, may hold values from 0 to 16, as said below
- slot_map: int32 [64], replicated, may hold values from 0 to 63, each once
Outputs:
- resampled: float32 [3, 64, 64, 4096], P(None, 'dom', 'row')
The draws below stay inside these ranges and needn't reach their ends.
Inputs may be any that keep to these rules, and one draw needn't show every extreme that they name: `state`: depth (component 0) lies in 0.5 to 3; both momenta (components 1 and 2) lie in -1.5 to 1.5. counts sum to 64; one particle gets exactly 16 copies, others at most 2, many none. `slot_map`: each slot appears once.
All inputs are finite; a program needn't handle non-finite values.
Results may differ from the reference program's by a relative error of at most 0.00002.
Values sent between devices are 32-bit elements; how exact they have to be, the bound alone decides.
No kernel may reach another device: no remote copies, remote signals or barrier semaphores. Data moves between devices by JAX's collectives and lax.ppermute only.
A program may use at most 192 MiB of HBM per device.

```python
import jax
import jax.numpy as jnp
from jax import lax

COLS = 4096
ROWS = 64
PARTICLES = 64


def draw_state(key, part):
    key_d, key_a, key_b = jax.random.split(jax.random.fold_in(key, 11), 3)
    shape = (PARTICLES, ROWS, COLS)
    depth = jax.random.uniform(key_d, shape, jnp.float32, 0.5, 3.0)
    flow_a = jnp.clip(0.5 * jax.random.normal(key_a, shape, jnp.float32), -1.5, 1.5)
    flow_b = jnp.clip(0.5 * jax.random.normal(key_b, shape, jnp.float32), -1.5, 1.5)
    return jnp.stack([depth, flow_a, flow_b]).astype(jnp.float32)


def draw_counts(key, part):
    key_a, key_c = jax.random.split(jax.random.fold_in(key, 23), 2)
    heavy = PARTICLES // 4
    places = jnp.arange(PARTICLES, dtype=jnp.int32)
    mixed = jax.random.permutation(key_a, 2 * (PARTICLES - 1)).astype(jnp.int32)
    rest = 1 + mixed[:PARTICLES] // 2
    picks = jnp.where(places < heavy, 0, rest).astype(jnp.int32)
    order = jax.random.permutation(key_c, PARTICLES).astype(jnp.int32)
    picks = order[picks]
    return jnp.sum((picks[:, None] == places[None, :]).astype(jnp.int32), axis=0).astype(jnp.int32)


def levels(stream_key, shape, pieces, low, high):
    loudness, own = 1.0, jax.random.fold_in(stream_key, 6)
    for position, parts in pieces:
        heights = jnp.exp(jax.random.uniform(jax.random.fold_in(own, position), (parts,), jnp.float32, low / len(pieces), high / len(pieces)))
        loudness = loudness * jnp.repeat(heights, shape[position] // parts).reshape([-1 if axis == position else 1 for axis in range(len(shape))])
    return loudness


def setup_inputs(seed: int = 0) -> dict:
    seeds = jax.random.split(jax.random.key(seed), 6)
    return {
        "state": draw_state(jax.random.fold_in(seeds[5], 71), 0),
        "rain": jnp.clip(0.5 * jax.random.uniform(seeds[1], (PARTICLES, ROWS, COLS), jnp.float32) ** levels(seeds[1], (PARTICLES, ROWS, COLS), ((0, 64), (1, 4)), -0.2, 0.2), 0.0, 0.5),
        "ground": jnp.clip(1.0 * jax.random.uniform(seeds[2], (ROWS, COLS), jnp.float32) ** levels(seeds[2], (ROWS, COLS), ((0, 4),), -0.2, 0.2), 0.0, 1.0),
        "counts": draw_counts(jax.random.fold_in(seeds[5], 71), 0),
        "slot_map": jax.random.permutation(seeds[4], PARTICLES).astype(jnp.int32),
    }


gravity = 9.81
courant = 0.04

def hll_flux(depth_l, norm_l, tang_l, depth_r, norm_r, tang_r):
    vel_l = norm_l / depth_l
    vel_r = norm_r / depth_r
    cel_l = jnp.sqrt(gravity * depth_l)
    cel_r = jnp.sqrt(gravity * depth_r)
    lower = jnp.minimum(jnp.minimum(vel_l - cel_l, vel_r - cel_r), 0.0)
    upper = jnp.maximum(jnp.maximum(vel_l + cel_l, vel_r + cel_r), 0.0)
    scale = 1.0 / (upper - lower)
    left_f = (norm_l, norm_l * vel_l + 0.5 * gravity * depth_l * depth_l, tang_l * vel_l)
    right_f = (norm_r, norm_r * vel_r + 0.5 * gravity * depth_r * depth_r, tang_r * vel_r)
    left_u = (depth_l, norm_l, tang_l)
    right_u = (depth_r, norm_r, tang_r)
    return tuple(((upper * fl - lower * fr + upper * lower * (ur - ul)) * scale for fl, fr, ul, ur in zip(left_f, right_f, left_u, right_u)))

def wall_cols(field, sign):
    return jnp.concatenate([field[:, :1] * sign, field, field[:, -1:] * sign], axis=1)

def advance(padded, rain_now):
    depth = wall_cols(padded[0], 1.0)
    flow_a = wall_cols(padded[1], 1.0)
    flow_b = wall_cols(padded[2], -1.0)
    bed = wall_cols(padded[3], 1.0)
    row_f = hll_flux(depth[:-1, 1:-1], flow_a[:-1, 1:-1], flow_b[:-1, 1:-1], depth[1:, 1:-1], flow_a[1:, 1:-1], flow_b[1:, 1:-1])
    col_f = hll_flux(depth[1:-1, :-1], flow_b[1:-1, :-1], flow_a[1:-1, :-1], depth[1:-1, 1:], flow_b[1:-1, 1:], flow_a[1:-1, 1:])
    depth_c = depth[1:-1, 1:-1]
    new_depth = depth_c - courant * (row_f[0][1:] - row_f[0][:-1]) - courant * (col_f[0][:, 1:] - col_f[0][:, :-1]) + rain_now
    new_a = flow_a[1:-1, 1:-1] - courant * (row_f[1][1:] - row_f[1][:-1]) - courant * (col_f[2][:, 1:] - col_f[2][:, :-1]) - courant * gravity * depth_c * (bed[2:, 1:-1] - bed[:-2, 1:-1]) * 0.5
    new_b = flow_b[1:-1, 1:-1] - courant * (row_f[2][1:] - row_f[2][:-1]) - courant * (col_f[1][:, 1:] - col_f[1][:, :-1]) - courant * gravity * depth_c * (bed[1:-1, 2:] - bed[1:-1, :-2]) * 0.5
    return jnp.stack([new_depth, new_a, new_b])

def ancestors_of(counts, slot_map):
    total = counts.shape[0]
    places = jnp.arange(total, dtype=jnp.int32)
    cumul = jnp.cumsum(counts).astype(jnp.int32)
    ordered = lax.optimization_barrier(jnp.sum((cumul[None, :] <= places[:, None]).astype(jnp.int32), axis=1))
    hits = (slot_map[None, :] == places[:, None]).astype(jnp.int32)
    return lax.optimization_barrier(jnp.sum(hits * ordered[None, :], axis=1)).astype(jnp.int32)

def reference(state, rain, ground, counts, slot_map):
    signs = jnp.array([1.0, -1.0, 1.0, 1.0], jnp.float32)[:, None, None]

    def one_particle(items):
        fields, rain_now = items
        stacked = jnp.concatenate([fields, ground[None]], axis=0)
        padded = jnp.concatenate([stacked[:, :1] * signs, stacked, stacked[:, -1:] * signs], axis=1)
        return advance(padded, rain_now)
    stepped = lax.map(one_particle, (jnp.moveaxis(state, 1, 0), rain))
    ancestor = ancestors_of(counts, slot_map)
    return jnp.moveaxis(stepped[ancestor], 0, 1)
```

```python
import functools

import jax
import jax.numpy as jnp
from jax import lax
from jax.experimental import pallas as pl
from jax.experimental.pallas import tpu as pltpu
from jax.sharding import Mesh, PartitionSpec as P

gravity = 9.81
courant = 0.04
LANES = 128
SUBLANES = 8


def cell_terms(depth, norm, tang):
    vel = norm / depth
    cel = jnp.sqrt(gravity * depth)
    press = 0.5 * gravity * depth * depth
    return depth, norm, tang, norm * vel + press, tang * vel, vel - cel, vel + cel


def interface(left, right):
    depth_l, norm_l, tang_l, fnorm_l, ftang_l, slow_l, fast_l = left
    depth_r, norm_r, tang_r, fnorm_r, ftang_r, slow_r, fast_r = right
    lower = jnp.minimum(jnp.minimum(slow_l, slow_r), 0.0)
    upper = jnp.maximum(jnp.maximum(fast_l, fast_r), 0.0)
    scale = 1.0 / (upper - lower)
    both = upper * lower
    return (
        (upper * norm_l - lower * norm_r + both * (depth_r - depth_l)) * scale,
        (upper * fnorm_l - lower * fnorm_r + both * (norm_r - norm_l)) * scale,
        (upper * ftang_l - lower * ftang_r + both * (tang_r - tang_l)) * scale,
    )


def both_ways(depth, flow_a, flow_b):
    inverse = 1.0 / depth
    cel = jnp.sqrt(gravity * depth)
    press = (0.5 * gravity) * depth * depth
    vel_a = flow_a * inverse
    vel_b = flow_b * inverse
    cross = flow_a * vel_b
    by_row = (depth, flow_a, flow_b, flow_a * vel_a + press, cross, vel_a - cel, vel_a + cel)
    by_col = (depth, flow_b, flow_a, flow_b * vel_b + press, cross, vel_b - cel, vel_b + cel)
    return by_row, by_col


def step_kernel(state_ref, rain_ref, ground_ref, out_ref):
    rows, width = ground_ref.shape
    tiles = width // LANES
    shape = (rows, LANES)
    lane = lax.broadcasted_iota(jnp.int32, shape, 1)
    row = lax.broadcasted_iota(jnp.int32, shape, 0)
    first_lane, last_lane = lane == 0, lane == LANES - 1
    first_row, last_row = row == 0, row == rows - 1

    def load(tile):
        at = pl.ds(pl.multiple_of(tile * LANES, LANES), LANES)
        return state_ref[0, 0, :, at], state_ref[1, 0, :, at], state_ref[2, 0, :, at], ground_ref[:, at]

    def rolled(terms):
        return tuple(pltpu.roll(term, LANES - 1, 1) for term in terms)

    def one(tile, carry):
        cells, bed, cells_r, bed_r, flux_before, bed_before = carry
        depth, flow_a, flow_b = cells[0]
        by_row, by_col = cells[1], cells[2]
        nxt = jnp.minimum(tile + 1, tiles - 1)
        n_depth, n_a, n_b, n_bed = load(nxt)
        n_row, n_col = both_ways(n_depth, n_a, n_b)
        n_rolled = rolled(n_col)
        n_bed_r = pltpu.roll(n_bed, LANES - 1, 1)
        right = tuple(jnp.where(last_lane, n, c) for n, c in zip(n_rolled, cells_r))
        at_wall = tile == tiles - 1
        ghost = jnp.logical_and(last_lane, at_wall)
        g_depth, g_norm, g_tang, g_fnorm, g_ftang, g_slow, g_fast = by_col
        mirror = (g_depth, -g_norm, g_tang, g_fnorm, -g_ftang, -g_fast, -g_slow)
        right = tuple(jnp.where(ghost, m, r) for m, r in zip(mirror, right))
        bed_next = jnp.where(ghost, bed, jnp.where(last_lane, n_bed_r, bed_r))
        flux = interface(by_col, right)
        flux_r = tuple(pltpu.roll(f, 1, 1) for f in flux)
        flux_left = tuple(jnp.where(first_lane, b, f) for b, f in zip(flux_before, flux_r))
        bed_rolled = pltpu.roll(bed, 1, 1)
        bed_left = jnp.where(first_lane, bed_before, bed_rolled)

        above = tuple(pltpu.roll(term, 1, 0) for term in by_row)
        inner = interface(above, by_row)
        inner = tuple(jnp.where(first_row, 0.0, f) for f in inner)
        below = tuple(pltpu.roll(f, rows - 1, 0) for f in inner)
        bed_up = jnp.where(first_row, 0.0, pltpu.roll(bed, 1, 0))
        bed_down = jnp.where(last_row, 0.0, pltpu.roll(bed, rows - 1, 0))

        pull = (0.5 * courant * gravity) * depth
        at = pl.ds(pl.multiple_of(tile * LANES, LANES), LANES)
        new_depth = depth - courant * ((below[0] - inner[0]) + (flux[0] - flux_left[0])) + rain_ref[0, :, at]
        new_a = flow_a - courant * ((below[1] - inner[1]) + (flux[2] - flux_left[2])) - pull * (bed_down - bed_up)
        new_b = flow_b - courant * ((below[2] - inner[2]) + (flux[1] - flux_left[1])) - pull * (bed_next - bed_left)
        for part, value in enumerate((new_depth, new_a, new_b)):
            for top in range(rows // SUBLANES):
                out_ref[tile, top, part] = value[top * SUBLANES : (top + 1) * SUBLANES]
        return ((n_depth, n_a, n_b), n_row, n_col), n_bed, n_rolled, n_bed_r, flux_r, bed_rolled

    depth, flow_a, flow_b, bed = load(0)
    by_row, by_col = both_ways(depth, flow_a, flow_b)
    g_depth, g_norm, g_tang, g_fnorm, g_ftang, g_slow, g_fast = by_col
    mirror = (g_depth, -g_norm, g_tang, g_fnorm, -g_ftang, -g_fast, -g_slow)
    start = (
        ((depth, flow_a, flow_b), by_row, by_col),
        bed,
        rolled(by_col),
        pltpu.roll(bed, LANES - 1, 1),
        interface(mirror, by_col),
        bed,
    )
    lax.fori_loop(0, tiles, one, start)


def edge_kernel(strip_ref, first_ref, last_ref, top_ref, low_ref, part_ref, out_ref, top_sc, low_sc, *, strips):
    strip = strip_ref[0]

    def fluxes(inside, outside, at_wall, upward):
        own = tuple(inside[i] for i in range(4))
        far = tuple(outside[i] for i in range(4))
        depth = jnp.where(at_wall, own[0], far[0])
        norm = jnp.where(at_wall, -own[1], far[1])
        tang = jnp.where(at_wall, own[2], far[2])
        bed = jnp.where(at_wall, own[3], far[3])
        mine = cell_terms(*own[:3])
        other = cell_terms(depth, norm, tang)
        flux = interface(other, mine) if upward else interface(mine, other)
        sign = courant if upward else -courant
        pull = (0.5 * courant * gravity) * own[0] * bed
        return (
            sign * flux[0],
            sign * flux[1] + (pull if upward else -pull),
            sign * flux[2],
        )

    for part, value in enumerate(fluxes(first_ref, top_ref, strip == 0, True)):
        top_sc[part] = value
    for part, value in enumerate(fluxes(last_ref, low_ref, strip == strips - 1, False)):
        low_sc[part] = value
    tiles = out_ref.shape[0]
    tops = out_ref.shape[1]
    out_ref[...] = part_ref[...]
    for tile in range(tiles):
        for part in range(3):
            out_ref[tile, 0, part, 0:1, :] = part_ref[tile, 0, part, 0:1, :] + top_sc[part, tile : tile + 1, :]
            out_ref[tile, tops - 1, part, SUBLANES - 1 : SUBLANES, :] = (
                part_ref[tile, tops - 1, part, SUBLANES - 1 : SUBLANES, :] + low_sc[part, tile : tile + 1, :]
            )


def place_kernel(tiles_ref, out_ref):
    tiles, tops = tiles_ref.shape[:2]
    for tile in range(tiles):
        for top in range(tops):
            for part in range(3):
                out_ref[part, 0, top * SUBLANES : (top + 1) * SUBLANES, tile * LANES : (tile + 1) * LANES] = tiles_ref[
                    tile, top, part
                ]


def whole(count):
    return [pl.BlockSpec(memory_space=pltpu.VMEM)] * count


def params(moved):
    return dict(
        compiler_params=pltpu.CompilerParams(vmem_limit_bytes=16 * 1024 * 1024),
        cost_estimate=pl.CostEstimate(flops=moved * 40, bytes_accessed=moved, transcendentals=0),
    )


def ancestors_of(counts, slot_map):
    total = counts.shape[0]
    places = jnp.arange(total, dtype=jnp.int32)
    upto = (places[None, :] <= places[:, None]).astype(jnp.int32)
    cumul = jnp.sum(upto * counts[None, :], axis=1)
    ordered = jnp.sum((cumul[None, :] <= places[:, None]).astype(jnp.int32), axis=1)
    hits = (slot_map[None, :] == places[:, None]).astype(jnp.int32)
    return jnp.sum(hits * ordered[None, :], axis=1)


def stepped_tiles(state, rain, ground):
    rows, width = ground.shape
    tiles, tops = width // LANES, rows // SUBLANES
    strips = lax.axis_size("row")
    edges = [
        jnp.concatenate([state[:, 0, at], ground[None, at]], axis=0).reshape(4, tiles, LANES) for at in (0, rows - 1)
    ]
    forward = [(i, i + 1) for i in range(strips - 1)]
    backward = [(target, source) for source, target in forward]
    top = lax.ppermute(edges[1], "row", forward)
    low = lax.ppermute(edges[0], "row", backward)
    shape = jax.ShapeDtypeStruct((tiles, tops, 3, SUBLANES, LANES), jnp.float32)
    partial = pl.pallas_call(
        step_kernel, out_shape=shape, in_specs=whole(3), out_specs=whole(1)[0], name="step", **params(2 << 20)
    )(state, rain, ground)
    strip = lax.axis_index("row").astype(jnp.int32).reshape(1)

    return pl.pallas_call(
        functools.partial(edge_kernel, strips=strips),
        out_shape=shape,
        in_specs=[pl.BlockSpec(memory_space=pltpu.SMEM)] + whole(5),
        out_specs=whole(1)[0],
        scratch_shapes=[pltpu.VMEM((3, tiles, LANES), jnp.float32)] * 2,
        input_output_aliases={5: 0},
        name="edges",
        **params(1 << 20),
    )(strip, edges[0], edges[1], top, low, partial)


def placed_strip(block, rows, width):
    return pl.pallas_call(
        place_kernel,
        out_shape=jax.ShapeDtypeStruct((3, 1, rows, width), jnp.float32),
        in_specs=whole(1),
        out_specs=whole(1)[0],
        name="place",
        **params(2 << 20),
    )(block)


def on_device(state, rain, ground, counts, slot_map):
    rows, width = ground.shape
    ancestor = ancestors_of(counts, slot_map)
    block = stepped_tiles(state, rain, ground)
    shape = block.shape
    outgoing = block.reshape((lax.axis_size("dom"), -1) + shape[2:])
    received = lax.all_to_all(outgoing, "dom", split_axis=0, concat_axis=0, tiled=True)
    chosen = jnp.take(received, ancestor, axis=0, mode="clip")
    returned = lax.all_to_all(chosen, "dom", split_axis=0, concat_axis=0, tiled=True)
    return placed_strip(returned.reshape(shape), rows, width)


def solution(mesh):
    placed = (P(None, "dom", "row", None), P("dom", "row", None), P("row", None), P(), P())
    return jax.shard_map(
        on_device,
        mesh=mesh,
        in_specs=placed,
        out_specs=P(None, "dom", "row", None),
        check_vma=False,
    )
```

```python
import functools

import jax
import jax.numpy as jnp
from jax import lax
from jax.experimental import pallas as pl
from jax.experimental.pallas import tpu as pltpu
from jax.sharding import Mesh, PartitionSpec as P

gravity = 9.81
courant = 0.04
LANES = 128
SUBLANES = 8


def cell_terms(depth, norm, tang):
    vel = norm / depth
    cel = jnp.sqrt(gravity * depth)
    press = 0.5 * gravity * depth * depth
    return depth, norm, tang, norm * vel + press, tang * vel, vel - cel, vel + cel


def interface(left, right):
    depth_l, norm_l, tang_l, fnorm_l, ftang_l, slow_l, fast_l = left
    depth_r, norm_r, tang_r, fnorm_r, ftang_r, slow_r, fast_r = right
    lower = jnp.minimum(jnp.minimum(slow_l, slow_r), 0.0)
    upper = jnp.maximum(jnp.maximum(fast_l, fast_r), 0.0)
    scale = 1.0 / (upper - lower)
    both = upper * lower
    return (
        (upper * norm_l - lower * norm_r + both * (depth_r - depth_l)) * scale,
        (upper * fnorm_l - lower * fnorm_r + both * (norm_r - norm_l)) * scale,
        (upper * ftang_l - lower * ftang_r + both * (tang_r - tang_l)) * scale,
    )


def both_ways(depth, flow_a, flow_b):
    inverse = 1.0 / depth
    cel = jnp.sqrt(gravity * depth)
    press = (0.5 * gravity) * depth * depth
    vel_a = flow_a * inverse
    vel_b = flow_b * inverse
    cross = flow_a * vel_b
    by_row = (depth, flow_a, flow_b, flow_a * vel_a + press, cross, vel_a - cel, vel_a + cel)
    by_col = (depth, flow_b, flow_a, flow_b * vel_b + press, cross, vel_b - cel, vel_b + cel)
    return by_row, by_col


def pack_kernel(state_ref, ground_ref, first_ref, last_ref, sems):
    rows = ground_ref.shape[0]
    copies = []
    for side, (row, out_ref) in enumerate(((rows - 1, last_ref), (0, first_ref))):
        at = pl.ds(row, 1)
        for part in range(3):
            copies.append(pltpu.make_async_copy(state_ref.at[part, 0, at], out_ref.at[part], sems.at[side, part]))
        copies.append(pltpu.make_async_copy(ground_ref.at[at], out_ref.at[3], sems.at[side, 3]))
    for copy in copies:
        copy.start()
    for copy in copies:
        copy.wait()


def step_kernel(state_ref, rain_ref, ground_ref, out_ref, *, unroll):
    rows, width = ground_ref.shape
    tiles = width // LANES
    shape = (rows, LANES)
    lane = lax.broadcasted_iota(jnp.int32, shape, 1)
    row = lax.broadcasted_iota(jnp.int32, shape, 0)
    first_lane, last_lane = lane == 0, lane == LANES - 1
    first_row, last_row = row == 0, row == rows - 1

    def columns(tile):
        start = tile * LANES
        return pl.ds(start if isinstance(tile, int) else pl.multiple_of(start, LANES), LANES)

    def load(tile):
        at = columns(tile)
        return state_ref[0, 0, :, at], state_ref[1, 0, :, at], state_ref[2, 0, :, at], ground_ref[:, at]

    def rolled(terms):
        return tuple(pltpu.roll(term, LANES - 1, 1) for term in terms)

    def mirrored(terms):
        depth, norm, tang, fnorm, ftang, slow, fast = terms
        return depth, -norm, tang, fnorm, -ftang, -fast, -slow

    def one(tile, carry, last=False):
        by_row, by_col, bed, cells_r, bed_r, flux_before, bed_before = carry
        depth, flow_a, flow_b = by_row[:3]
        if last:
            n_row, n_col, n_bed = by_row, by_col, bed
            n_rolled, n_bed_r = mirrored(by_col), bed
        else:
            n_depth, n_a, n_b, n_bed = load(tile + 1)
            n_row, n_col = both_ways(n_depth, n_a, n_b)
            n_rolled = rolled(n_col)
            n_bed_r = pltpu.roll(n_bed, LANES - 1, 1)
        right = tuple(jnp.where(last_lane, n, c) for n, c in zip(n_rolled, cells_r))
        bed_next = jnp.where(last_lane, n_bed_r, bed_r)
        flux = interface(by_col, right)
        flux_r = tuple(pltpu.roll(f, 1, 1) for f in flux)
        flux_left = tuple(jnp.where(first_lane, b, f) for b, f in zip(flux_before, flux_r))
        bed_rolled = pltpu.roll(bed, 1, 1)
        bed_left = jnp.where(first_lane, bed_before, bed_rolled)

        above = tuple(pltpu.roll(term, 1, 0) for term in by_row)
        inner = interface(above, by_row)
        inner = tuple(jnp.where(first_row, 0.0, f) for f in inner)
        below = tuple(pltpu.roll(f, rows - 1, 0) for f in inner)
        bed_up = jnp.where(first_row, 0.0, pltpu.roll(bed, 1, 0))
        bed_down = jnp.where(last_row, 0.0, pltpu.roll(bed, rows - 1, 0))

        pull = (0.5 * courant * gravity) * depth
        new_depth = depth - courant * ((below[0] - inner[0]) + (flux[0] - flux_left[0])) + rain_ref[0, :, columns(tile)]
        new_a = flow_a - courant * ((below[1] - inner[1]) + (flux[2] - flux_left[2])) - pull * (bed_down - bed_up)
        new_b = flow_b - courant * ((below[2] - inner[2]) + (flux[1] - flux_left[1])) - pull * (bed_next - bed_left)
        for part, value in enumerate((new_depth, new_a, new_b)):
            for top in range(rows // SUBLANES):
                out_ref[tile, top, part] = value[top * SUBLANES : (top + 1) * SUBLANES]
        return n_row, n_col, n_bed, n_rolled, n_bed_r, flux_r, bed_rolled

    depth, flow_a, flow_b, bed = load(0)
    by_row, by_col = both_ways(depth, flow_a, flow_b)
    edge = interface(mirrored(by_col), by_col)
    carry = (by_row, by_col, bed, rolled(by_col), pltpu.roll(bed, LANES - 1, 1), edge, bed)
    steps = (tiles - 1) // unroll

    def some(i, carry):
        for k in range(unroll):
            carry = one(i * unroll + k, carry)
        return carry

    carry = lax.fori_loop(0, steps, some, carry)
    for tile in range(steps * unroll, tiles):
        carry = one(tile, carry, tile == tiles - 1)


def edge_kernel(strip_ref, first_ref, last_ref, top_ref, low_ref, part_ref, out_ref, top_sc, low_sc, *, strips):
    strip = strip_ref[0]

    def fluxes(inside, outside, at_wall, upward):
        own = tuple(inside[i] for i in range(4))
        far = tuple(outside[i] for i in range(4))
        depth = jnp.where(at_wall, own[0], far[0])
        norm = jnp.where(at_wall, -own[1], far[1])
        tang = jnp.where(at_wall, own[2], far[2])
        bed = jnp.where(at_wall, own[3], far[3])
        mine = cell_terms(*own[:3])
        other = cell_terms(depth, norm, tang)
        flux = interface(other, mine) if upward else interface(mine, other)
        sign = courant if upward else -courant
        pull = (0.5 * courant * gravity) * own[0] * bed
        return (
            sign * flux[0],
            sign * flux[1] + (pull if upward else -pull),
            sign * flux[2],
        )

    for part, value in enumerate(fluxes(first_ref, top_ref, strip == 0, True)):
        top_sc[part] = value
    for part, value in enumerate(fluxes(last_ref, low_ref, strip == strips - 1, False)):
        low_sc[part] = value
    tiles = out_ref.shape[0]
    tops = out_ref.shape[1]
    out_ref[...] = part_ref[...]
    for tile in range(tiles):
        for part in range(3):
            out_ref[tile, 0, part, 0:1, :] = part_ref[tile, 0, part, 0:1, :] + top_sc[part, tile : tile + 1, :]
            out_ref[tile, tops - 1, part, SUBLANES - 1 : SUBLANES, :] = (
                part_ref[tile, tops - 1, part, SUBLANES - 1 : SUBLANES, :] + low_sc[part, tile : tile + 1, :]
            )


def choose_kernel(index_ref, from_ref, out_ref):
    for slot in range(out_ref.shape[0]):
        out_ref[slot] = from_ref[index_ref[slot]]


def place_kernel(tiles_ref, out_ref):
    tiles, tops = tiles_ref.shape[:2]
    for tile in range(tiles):
        for top in range(tops):
            for part in range(3):
                out_ref[part, 0, top * SUBLANES : (top + 1) * SUBLANES, tile * LANES : (tile + 1) * LANES] = tiles_ref[
                    tile, top, part
                ]


def whole(count):
    return [pl.BlockSpec(memory_space=pltpu.VMEM)] * count


def params(moved):
    return dict(
        compiler_params=pltpu.CompilerParams(vmem_limit_bytes=16 * 1024 * 1024),
        cost_estimate=pl.CostEstimate(flops=moved * 40, bytes_accessed=moved, transcendentals=0),
    )


def ancestors_of(counts, slot_map):
    total = counts.shape[0]
    places = jnp.arange(total, dtype=jnp.int32)
    upto = (places[None, :] <= places[:, None]).astype(jnp.int32)
    cumul = jnp.sum(upto * counts[None, :], axis=1)
    ordered = jnp.sum((cumul[None, :] <= places[:, None]).astype(jnp.int32), axis=1)
    hits = (slot_map[None, :] == places[:, None]).astype(jnp.int32)
    return jnp.sum(hits * ordered[None, :], axis=1)


UNROLL = 4
HBM = pl.BlockSpec(memory_space=pltpu.HBM)


def packed_edges(state, ground):
    rows, width = ground.shape
    shape = pltpu.VMEM((4, 1, width), jnp.float32)
    return pl.pallas_call(
        pack_kernel,
        out_shape=(shape, shape),
        in_specs=[HBM, HBM],
        out_specs=whole(2),
        scratch_shapes=[pltpu.SemaphoreType.DMA((2, 4))],
        name="pack",
        **params(1 << 18),
    )(*(pltpu.with_memory_space_constraint(x, pltpu.HBM) for x in (state, ground)))


def partial_step(state, rain, ground, unroll=UNROLL):
    rows, width = ground.shape
    tiles, tops = width // LANES, rows // SUBLANES
    return pl.pallas_call(
        functools.partial(step_kernel, unroll=unroll),
        out_shape=pltpu.VMEM((tiles, tops, 3, SUBLANES, LANES), jnp.float32),
        in_specs=whole(3),
        out_specs=whole(1)[0],
        name="step",
        **params(8 << 20),
    )(state, rain, ground)


def stepped_tiles(state, rain, ground):
    rows, width = ground.shape
    tiles = width // LANES
    strips = lax.axis_size("row")
    first, last = packed_edges(state, ground)
    forward = [(i, i + 1) for i in range(strips - 1)]
    backward = [(target, source) for source, target in forward]
    top = lax.ppermute(last, "row", forward)
    low = lax.ppermute(first, "row", backward)
    partial = partial_step(state, rain, ground)
    strip = lax.axis_index("row").astype(jnp.int32).reshape(1)
    square = (4, tiles, LANES)
    return pl.pallas_call(
        functools.partial(edge_kernel, strips=strips),
        out_shape=pltpu.VMEM(partial.shape, jnp.float32),
        in_specs=[pl.BlockSpec(memory_space=pltpu.SMEM)] + whole(5),
        out_specs=whole(1)[0],
        scratch_shapes=[pltpu.VMEM((3, tiles, LANES), jnp.float32)] * 2,
        name="edges",
        **params(1 << 20),
    )(strip, first.reshape(square), last.reshape(square), top.reshape(square), low.reshape(square), partial)


def chosen_blocks(index, blocks):
    return pl.pallas_call(
        choose_kernel,
        out_shape=jax.ShapeDtypeStruct(index.shape + blocks.shape[1:], jnp.float32),
        in_specs=[pl.BlockSpec(memory_space=pltpu.SMEM)] + whole(1),
        out_specs=whole(1)[0],
        name="choose",
        **params(2 << 20),
    )(index, blocks)


def placed_strip(block, rows, width):
    return pl.pallas_call(
        place_kernel,
        out_shape=jax.ShapeDtypeStruct((3, 1, rows, width), jnp.float32),
        in_specs=whole(1),
        out_specs=whole(1)[0],
        name="place",
        **params(2 << 20),
    )(block)


def on_device(state, rain, ground, counts, slot_map):
    rows, width = ground.shape
    ancestor = ancestors_of(counts, slot_map)
    block, ancestor = lax.optimization_barrier((stepped_tiles(state, rain, ground), ancestor))
    shape = block.shape
    outgoing = block.reshape((lax.axis_size("dom"), -1) + shape[2:])
    received = lax.all_to_all(outgoing, "dom", split_axis=0, concat_axis=0, tiled=True)
    chosen = chosen_blocks(ancestor, received)
    returned = lax.all_to_all(chosen, "dom", split_axis=0, concat_axis=0, tiled=True)
    return placed_strip(returned.reshape(shape), rows, width)


def solution(mesh):
    placed = (P(None, "dom", "row", None), P("dom", "row", None), P("row", None), P(), P())
    return jax.shard_map(
        on_device,
        mesh=mesh,
        in_specs=placed,
        out_specs=P(None, "dom", "row", None),
        check_vma=False,
    )
```

```python
import functools

import jax
import jax.numpy as jnp
from jax import lax
from jax.experimental import pallas as pl
from jax.experimental.pallas import tpu as pltpu
from jax.sharding import Mesh, PartitionSpec as P

gravity = 9.81
courant = 0.04
LANES = 128
SUBLANES = 8


def cell_terms(depth, norm, tang):
    vel = norm / depth
    cel = jnp.sqrt(gravity * depth)
    press = 0.5 * gravity * depth * depth
    return depth, norm, tang, norm * vel + press, tang * vel, vel - cel, vel + cel


def interface(left, right):
    depth_l, norm_l, tang_l, fnorm_l, ftang_l, slow_l, fast_l = left
    depth_r, norm_r, tang_r, fnorm_r, ftang_r, slow_r, fast_r = right
    lower = jnp.minimum(jnp.minimum(slow_l, slow_r), 0.0)
    upper = jnp.maximum(jnp.maximum(fast_l, fast_r), 0.0)
    scale = 1.0 / (upper - lower)
    both = upper * lower
    return (
        (upper * norm_l - lower * norm_r + both * (depth_r - depth_l)) * scale,
        (upper * fnorm_l - lower * fnorm_r + both * (norm_r - norm_l)) * scale,
        (upper * ftang_l - lower * ftang_r + both * (tang_r - tang_l)) * scale,
    )


def both_ways(depth, flow_a, flow_b):
    inverse = 1.0 / depth
    cel = jnp.sqrt(gravity * depth)
    press = (0.5 * gravity) * depth * depth
    vel_a = flow_a * inverse
    vel_b = flow_b * inverse
    cross = flow_a * vel_b
    by_row = (depth, flow_a, flow_b, flow_a * vel_a + press, cross, vel_a - cel, vel_a + cel)
    by_col = (depth, flow_b, flow_a, flow_b * vel_b + press, cross, vel_b - cel, vel_b + cel)
    return by_row, by_col


def pack_kernel(state_ref, ground_ref, first_ref, last_ref, sems):
    rows = ground_ref.shape[0]
    copies = []
    for side, (row, out_ref) in enumerate(((rows - 1, last_ref), (0, first_ref))):
        at = pl.ds(row, 1)
        for part in range(3):
            copies.append(pltpu.make_async_copy(state_ref.at[part, 0, at], out_ref.at[part], sems.at[side, part]))
        copies.append(pltpu.make_async_copy(ground_ref.at[at], out_ref.at[3], sems.at[side, 3]))
    for copy in copies:
        copy.start()
    for copy in copies:
        copy.wait()


def step_kernel(state_ref, rain_ref, ground_ref, out_ref, *, unroll):
    rows, width = ground_ref.shape
    tiles = width // LANES
    shape = (rows, LANES)
    lane = lax.broadcasted_iota(jnp.int32, shape, 1)
    row = lax.broadcasted_iota(jnp.int32, shape, 0)
    first_lane, last_lane = lane == 0, lane == LANES - 1
    first_row, last_row = row == 0, row == rows - 1

    def columns(tile):
        start = tile * LANES
        return pl.ds(start if isinstance(tile, int) else pl.multiple_of(start, LANES), LANES)

    def load(tile):
        at = columns(tile)
        return state_ref[0, 0, :, at], state_ref[1, 0, :, at], state_ref[2, 0, :, at], ground_ref[:, at]

    def rolled(terms):
        return tuple(pltpu.roll(term, LANES - 1, 1) for term in terms)

    def mirrored(terms):
        depth, norm, tang, fnorm, ftang, slow, fast = terms
        return depth, -norm, tang, fnorm, -ftang, -fast, -slow

    def one(tile, carry, last=False):
        by_row, by_col, bed, cells_r, bed_r, flux_before, bed_before = carry
        depth, flow_a, flow_b = by_row[:3]
        if last:
            n_row, n_col, n_bed = by_row, by_col, bed
            n_rolled, n_bed_r = mirrored(by_col), bed
        else:
            n_depth, n_a, n_b, n_bed = load(tile + 1)
            n_row, n_col = both_ways(n_depth, n_a, n_b)
            n_rolled = rolled(n_col)
            n_bed_r = pltpu.roll(n_bed, LANES - 1, 1)
        right = tuple(jnp.where(last_lane, n, c) for n, c in zip(n_rolled, cells_r))
        bed_next = jnp.where(last_lane, n_bed_r, bed_r)
        flux = interface(by_col, right)
        flux_r = tuple(pltpu.roll(f, 1, 1) for f in flux)
        flux_left = tuple(jnp.where(first_lane, b, f) for b, f in zip(flux_before, flux_r))
        bed_rolled = pltpu.roll(bed, 1, 1)
        bed_left = jnp.where(first_lane, bed_before, bed_rolled)

        above = tuple(pltpu.roll(term, 1, 0) for term in by_row)
        inner = interface(above, by_row)
        inner = tuple(jnp.where(first_row, 0.0, f) for f in inner)
        below = tuple(pltpu.roll(f, rows - 1, 0) for f in inner)
        bed_up = jnp.where(first_row, 0.0, pltpu.roll(bed, 1, 0))
        bed_down = jnp.where(last_row, 0.0, pltpu.roll(bed, rows - 1, 0))

        pull = (0.5 * courant * gravity) * depth
        new_depth = depth - courant * ((below[0] - inner[0]) + (flux[0] - flux_left[0])) + rain_ref[0, :, columns(tile)]
        new_a = flow_a - courant * ((below[1] - inner[1]) + (flux[2] - flux_left[2])) - pull * (bed_down - bed_up)
        new_b = flow_b - courant * ((below[2] - inner[2]) + (flux[1] - flux_left[1])) - pull * (bed_next - bed_left)
        for part, value in enumerate((new_depth, new_a, new_b)):
            for top in range(rows // SUBLANES):
                out_ref[tile, top, part] = value[top * SUBLANES : (top + 1) * SUBLANES]
        return n_row, n_col, n_bed, n_rolled, n_bed_r, flux_r, bed_rolled

    depth, flow_a, flow_b, bed = load(0)
    by_row, by_col = both_ways(depth, flow_a, flow_b)
    edge = interface(mirrored(by_col), by_col)
    carry = (by_row, by_col, bed, rolled(by_col), pltpu.roll(bed, LANES - 1, 1), edge, bed)
    steps = (tiles - 1) // unroll

    def some(i, carry):
        for k in range(unroll):
            carry = one(i * unroll + k, carry)
        return carry

    carry = lax.fori_loop(0, steps, some, carry)
    for tile in range(steps * unroll, tiles):
        carry = one(tile, carry, tile == tiles - 1)


def edge_kernel(strip_ref, first_ref, last_ref, top_ref, low_ref, part_ref, out_ref, top_sc, low_sc, *, strips):
    strip = strip_ref[0]

    def fluxes(inside, outside, at_wall, upward):
        own = tuple(inside[i] for i in range(4))
        far = tuple(outside[i] for i in range(4))
        depth = jnp.where(at_wall, own[0], far[0])
        norm = jnp.where(at_wall, -own[1], far[1])
        tang = jnp.where(at_wall, own[2], far[2])
        bed = jnp.where(at_wall, own[3], far[3])
        mine = cell_terms(*own[:3])
        other = cell_terms(depth, norm, tang)
        flux = interface(other, mine) if upward else interface(mine, other)
        sign = courant if upward else -courant
        pull = (0.5 * courant * gravity) * own[0] * bed
        return (
            sign * flux[0],
            sign * flux[1] + (pull if upward else -pull),
            sign * flux[2],
        )

    for part, value in enumerate(fluxes(first_ref, top_ref, strip == 0, True)):
        top_sc[part] = value
    for part, value in enumerate(fluxes(last_ref, low_ref, strip == strips - 1, False)):
        low_sc[part] = value
    tiles = out_ref.shape[0]
    tops = out_ref.shape[1]
    out_ref[...] = part_ref[...]
    for tile in range(tiles):
        for part in range(3):
            out_ref[tile, 0, part, 0:1, :] = part_ref[tile, 0, part, 0:1, :] + top_sc[part, tile : tile + 1, :]
            out_ref[tile, tops - 1, part, SUBLANES - 1 : SUBLANES, :] = (
                part_ref[tile, tops - 1, part, SUBLANES - 1 : SUBLANES, :] + low_sc[part, tile : tile + 1, :]
            )


def plan_kernel(zh_ref, core_ref, counts_ref, slot_ref, plan_ref, level_ref, *, sizes):
    zh, core = zh_ref[0], core_ref[0]
    total = counts_ref.shape[1]
    square = (total, total)
    i = lax.broadcasted_iota(jnp.int32, square, 0)
    j = lax.broadcasted_iota(jnp.int32, square, 1)

    def over_lanes(values):
        return jnp.sum(values, axis=1, keepdims=True)

    def over_rows(values):
        return jnp.sum(values, axis=0, keepdims=True)

    def half(places):
        return jnp.bitwise_and(jnp.right_shift(places, 1), 1)

    counts, slots = counts_ref[...], slot_ref[...]
    cumul = over_lanes(jnp.where(j <= i, counts, 0))
    ordered = over_rows((cumul <= j).astype(jnp.int32))
    ancestor = over_lanes(jnp.where(slots == i, ordered, 0))
    crossing = jnp.logical_and(ancestor == j, half(i) != half(j))
    needed = (over_rows(crossing.astype(jnp.int32)) > 0).astype(jnp.int32)
    needed_col = over_lanes(jnp.where(i == j, needed, 0))
    earlier = jnp.logical_and(i < j, half(i) == half(j))
    rank = over_rows(jnp.where(earlier, needed_col, 0))
    rank_col = over_lanes(jnp.where(i == j, rank, 0))
    home = jnp.where(jnp.bitwise_and(i, 1) == core, 0, total) + jnp.right_shift(i, 2)
    mine = jnp.logical_and(half(i) == zh, jnp.logical_and(needed_col > 0, rank_col == j))
    send = over_rows(jnp.where(mine, home, 0))
    rank_of = over_lanes(jnp.where(ancestor == j, rank, 0))
    here = jnp.where(jnp.bitwise_and(ancestor, 1) == core, 0, total) + jnp.right_shift(ancestor, 2)
    source = jnp.where(half(ancestor) == zh, here, 2 * total + rank_of)
    find = over_rows(jnp.where(i == 4 * j + 2 * zh + core, source, 0))
    plan_ref[0:1, :] = send
    plan_ref[1:2, :] = find
    lower = jnp.sum(jnp.where(half(j[0:1]) == 0, needed, 0))
    most = jnp.maximum(lower, jnp.sum(needed) - lower)
    level_ref[0] = sum((most > size).astype(jnp.int32) for size in sizes[:-1])


def outgoing_kernel(core_ref, plan_ref, own_ref, other_ref, out_ref):
    core = core_ref[0]
    for k in range(out_ref.shape[0]):
        code = plan_ref[0, k]

        @pl.when(code < 64)
        def _():
            out_ref[k] = own_ref[code, core]

        @pl.when(code >= 64)
        def _():
            out_ref[k] = other_ref[code - 64, core]


def slots_kernel(core_ref, plan_ref, own_ref, other_ref, crossed_ref, crossed_other_ref, out_ref):
    core = core_ref[0]
    for slot in range(out_ref.shape[0]):
        code = plan_ref[1, slot]

        @pl.when(code < 64)
        def _():
            out_ref[slot] = own_ref[code]

        @pl.when(jnp.logical_and(code >= 64, code < 128))
        def _():
            out_ref[slot] = other_ref[code - 64]

        @pl.when(code >= 128)
        def _():
            out_ref[slot, core] = crossed_ref[code - 128]
            out_ref[slot, 1 - core] = crossed_other_ref[code - 128]


def place_kernel(tiles_ref, out_ref):
    tiles, tops = tiles_ref.shape[:2]
    for tile in range(tiles):
        for top in range(tops):
            for part in range(3):
                out_ref[part, 0, top * SUBLANES : (top + 1) * SUBLANES, tile * LANES : (tile + 1) * LANES] = tiles_ref[
                    tile, top, part
                ]


def whole(count):
    return [pl.BlockSpec(memory_space=pltpu.VMEM)] * count


def params(moved):
    return dict(
        compiler_params=pltpu.CompilerParams(vmem_limit_bytes=16 * 1024 * 1024),
        cost_estimate=pl.CostEstimate(flops=moved * 40, bytes_accessed=moved, transcendentals=0),
    )


UNROLL = 4
HBM = pl.BlockSpec(memory_space=pltpu.HBM)


def packed_edges(state, ground):
    rows, width = ground.shape
    shape = pltpu.VMEM((4, 1, width), jnp.float32)
    return pl.pallas_call(
        pack_kernel,
        out_shape=(shape, shape),
        in_specs=[HBM, HBM],
        out_specs=whole(2),
        scratch_shapes=[pltpu.SemaphoreType.DMA((2, 4))],
        name="pack",
        **params(1 << 18),
    )(*(pltpu.with_memory_space_constraint(x, pltpu.HBM) for x in (state, ground)))


def partial_step(state, rain, ground, unroll=UNROLL):
    rows, width = ground.shape
    tiles, tops = width // LANES, rows // SUBLANES
    return pl.pallas_call(
        functools.partial(step_kernel, unroll=unroll),
        out_shape=pltpu.VMEM((tiles, tops, 3, SUBLANES, LANES), jnp.float32),
        in_specs=whole(3),
        out_specs=whole(1)[0],
        name="step",
        **params(8 << 20),
    )(state, rain, ground)


def stepped_tiles(state, rain, ground):
    rows, width = ground.shape
    tiles = width // LANES
    strips = lax.axis_size("row")
    first, last = packed_edges(state, ground)
    forward = [(i, i + 1) for i in range(strips - 1)]
    backward = [(target, source) for source, target in forward]
    top = lax.ppermute(last, "row", forward)
    low = lax.ppermute(first, "row", backward)
    partial = partial_step(state, rain, ground)
    strip = lax.axis_index("row").astype(jnp.int32).reshape(1)
    square = (4, tiles, LANES)
    return pl.pallas_call(
        functools.partial(edge_kernel, strips=strips),
        out_shape=pltpu.VMEM(partial.shape, jnp.float32),
        in_specs=[pl.BlockSpec(memory_space=pltpu.SMEM)] + whole(5),
        out_specs=whole(1)[0],
        scratch_shapes=[pltpu.VMEM((3, tiles, LANES), jnp.float32)] * 2,
        name="edges",
        **params(1 << 20),
    )(strip, first.reshape(square), last.reshape(square), top.reshape(square), low.reshape(square), partial)


SMEM = pl.BlockSpec(memory_space=pltpu.SMEM)
SWAP = [(0, 1), (1, 0)]


def transfer_plan(zh, core, counts, slot_map):
    total = counts.shape[0]
    return pl.pallas_call(
        functools.partial(plan_kernel, sizes=SIZES),
        out_shape=(jax.ShapeDtypeStruct((2, total), jnp.int32), jax.ShapeDtypeStruct((1,), jnp.int32)),
        in_specs=[SMEM, SMEM] + whole(2),
        out_specs=(whole(1)[0], SMEM),
        name="plan",
        **params(1 << 16),
    )(zh, core, counts.reshape(1, total), slot_map.reshape(1, total))


def blocks_for_slots(core, plan, own, other, most):
    outgoing = pl.pallas_call(
        outgoing_kernel,
        out_shape=jax.ShapeDtypeStruct((most,) + own.shape[2:], jnp.float32),
        in_specs=[SMEM, SMEM] + whole(2),
        out_specs=whole(1)[0],
        name="outgoing",
        **params(1 << 20),
    )(core, plan, own, other)
    crossed = lax.ppermute(outgoing, "zh", SWAP)
    crossed_other = lax.ppermute(crossed, "core", SWAP)
    return pl.pallas_call(
        slots_kernel,
        out_shape=jax.ShapeDtypeStruct(own.shape, jnp.float32),
        in_specs=[SMEM, SMEM] + whole(4),
        out_specs=whole(1)[0],
        name="slots",
        **params(2 << 20),
    )(core, plan, own, other, crossed, crossed_other)


def placed_strip(block, rows, width):
    return pl.pallas_call(
        place_kernel,
        out_shape=jax.ShapeDtypeStruct((3, 1, rows, width), jnp.float32),
        in_specs=whole(1),
        out_specs=whole(1)[0],
        name="place",
        **params(2 << 20),
    )(block)


PLANE = ("y", "x")
SIZES = (8, 10, 12, 14, 16, 18, 20, 24, 32)


def on_device(state, rain, ground, counts, slot_map):
    rows, width = ground.shape
    zh = lax.axis_index("zh").astype(jnp.int32).reshape(1)
    core = lax.axis_index("core").astype(jnp.int32).reshape(1)
    plan, level = transfer_plan(zh, core, counts, slot_map)
    block, plan, level = lax.optimization_barrier((stepped_tiles(state, rain, ground), plan, level))
    shape = block.shape
    spread = lax.axis_size("y") * lax.axis_size("x")
    outgoing = block.reshape((spread, 2, -1) + shape[2:])
    own = lax.all_to_all(outgoing, PLANE, split_axis=0, concat_axis=0, tiled=True)
    other = lax.ppermute(own, "core", SWAP)
    chosen = lax.switch(
        level[0], [functools.partial(blocks_for_slots, most=size) for size in SIZES], core, plan, own, other
    )
    returned = lax.all_to_all(chosen, PLANE, split_axis=0, concat_axis=0, tiled=True)
    return placed_strip(returned.reshape(shape), rows, width)


def solution(mesh):
    fine = Mesh(mesh.devices.reshape(4, 4, 2, 2, 4), ("y", "x", "zh", "core", "row"))
    dom = ("y", "x", "zh", "core")
    placed = (P(None, dom, "row", None), P(dom, "row", None), P("row", None), P(), P())
    return jax.shard_map(
        on_device,
        mesh=fine,
        in_specs=placed,
        out_specs=P(None, dom, "row", None),
        check_vma=False,
    )
```

```python
import functools

import jax
import jax.numpy as jnp
from jax import lax
from jax.experimental import pallas as pl
from jax.experimental.pallas import tpu as pltpu
from jax.sharding import Mesh, PartitionSpec as P

gravity = 9.81
courant = 0.04
LANES = 128
SUBLANES = 8


def cell_terms(depth, norm, tang):
    vel = norm / depth
    cel = jnp.sqrt(gravity * depth)
    press = 0.5 * gravity * depth * depth
    return depth, norm, tang, norm * vel + press, tang * vel, vel - cel, vel + cel


def interface(left, right):
    depth_l, norm_l, tang_l, fnorm_l, ftang_l, slow_l, fast_l = left
    depth_r, norm_r, tang_r, fnorm_r, ftang_r, slow_r, fast_r = right
    lower = jnp.minimum(jnp.minimum(slow_l, slow_r), 0.0)
    upper = jnp.maximum(jnp.maximum(fast_l, fast_r), 0.0)
    scale = 1.0 / (upper - lower)
    both = upper * lower
    return (
        (upper * norm_l - lower * norm_r + both * (depth_r - depth_l)) * scale,
        (upper * fnorm_l - lower * fnorm_r + both * (norm_r - norm_l)) * scale,
        (upper * ftang_l - lower * ftang_r + both * (tang_r - tang_l)) * scale,
    )


def both_ways(depth, flow_a, flow_b):
    inverse = 1.0 / depth
    cel = jnp.sqrt(gravity * depth)
    press = (0.5 * gravity) * depth * depth
    vel_a = flow_a * inverse
    vel_b = flow_b * inverse
    cross = flow_a * vel_b
    by_row = (depth, flow_a, flow_b, flow_a * vel_a + press, cross, vel_a - cel, vel_a + cel)
    by_col = (depth, flow_b, flow_a, flow_b * vel_b + press, cross, vel_b - cel, vel_b + cel)
    return by_row, by_col


def pack_kernel(state_ref, ground_ref, first_ref, last_ref, sems):
    rows = ground_ref.shape[0]
    copies = []
    for side, (row, out_ref) in enumerate(((rows - 1, last_ref), (0, first_ref))):
        at = pl.ds(row, 1)
        for part in range(3):
            copies.append(pltpu.make_async_copy(state_ref.at[part, 0, at], out_ref.at[part], sems.at[side, part]))
        copies.append(pltpu.make_async_copy(ground_ref.at[at], out_ref.at[3], sems.at[side, 3]))
    for copy in copies:
        copy.start()
    for copy in copies:
        copy.wait()


def write_plan(zh, counts, slots, plan_ref, level_ref, sizes):
    total = counts.shape[1]
    square = (total, total)
    i = lax.broadcasted_iota(jnp.int32, square, 0)
    j = lax.broadcasted_iota(jnp.int32, square, 1)

    def over_lanes(values):
        return jnp.sum(values, axis=1, keepdims=True)

    def over_rows(values):
        return jnp.sum(values, axis=0, keepdims=True)

    def half(places):
        return jnp.bitwise_and(jnp.right_shift(places, 1), 1)

    def place(places):
        return 2 * jnp.right_shift(places, 2) + jnp.bitwise_and(places, 1)

    cumul = over_lanes(jnp.where(j <= i, counts, 0))
    ordered = over_rows((cumul <= j).astype(jnp.int32))
    ancestor = over_lanes(jnp.where(slots == i, ordered, 0))
    crossing = jnp.logical_and(ancestor == j, half(i) != half(j))
    needed = (over_rows(crossing.astype(jnp.int32)) > 0).astype(jnp.int32)
    needed_col = over_lanes(jnp.where(i == j, needed, 0))
    earlier = jnp.logical_and(i < j, half(i) == half(j))
    rank = over_rows(jnp.where(earlier, needed_col, 0))
    rank_col = over_lanes(jnp.where(i == j, rank, 0))
    mine = jnp.logical_and(half(i) == zh, jnp.logical_and(needed_col > 0, rank_col == j))
    plan_ref[0:1, :] = over_rows(jnp.where(mine, place(i), 0))
    rank_of = over_lanes(jnp.where(ancestor == j, rank, 0))
    source = jnp.where(half(ancestor) == zh, place(ancestor), total // 2 + rank_of)
    here = jnp.logical_and(half(i) == zh, place(i) == j)
    plan_ref[1:2, :] = over_rows(jnp.where(here, source, 0))
    lower = jnp.sum(jnp.where(half(j[0:1]) == 0, needed, 0))
    most = jnp.maximum(lower, jnp.sum(needed) - lower)
    level_ref[0] = sum((most > size).astype(jnp.int32) for size in sizes[:-1])


def step_kernel(
    zh_ref, state_ref, ground_ref, rain_hbm, counts_hbm, slots_hbm,
    out_ref, plan_ref, level_ref, rain_ref, counts_ref, slots_ref, sems, *, unroll, sizes
):
    rows, width = ground_ref.shape
    copies = [
        pltpu.make_async_copy(counts_hbm, counts_ref, sems.at[0]),
        pltpu.make_async_copy(slots_hbm, slots_ref, sems.at[1]),
        pltpu.make_async_copy(rain_hbm, rain_ref, sems.at[2]),
    ]
    for copy in copies:
        copy.start()
    tiles = width // LANES
    shape = (rows, LANES)
    lane = lax.broadcasted_iota(jnp.int32, shape, 1)
    row = lax.broadcasted_iota(jnp.int32, shape, 0)
    first_lane, last_lane = lane == 0, lane == LANES - 1
    first_row, last_row = row == 0, row == rows - 1

    def columns(tile):
        start = tile * LANES
        return pl.ds(start if isinstance(tile, int) else pl.multiple_of(start, LANES), LANES)

    def load(tile):
        at = columns(tile)
        return state_ref[0, 0, :, at], state_ref[1, 0, :, at], state_ref[2, 0, :, at], ground_ref[:, at]

    def rolled(terms):
        return tuple(pltpu.roll(term, LANES - 1, 1) for term in terms)

    def mirrored(terms):
        depth, norm, tang, fnorm, ftang, slow, fast = terms
        return depth, -norm, tang, fnorm, -ftang, -fast, -slow

    def one(tile, carry, last=False):
        by_row, by_col, bed, cells_r, bed_r, flux_before, bed_before = carry
        depth, flow_a, flow_b = by_row[:3]
        if last:
            n_row, n_col, n_bed = by_row, by_col, bed
            n_rolled, n_bed_r = mirrored(by_col), bed
        else:
            n_depth, n_a, n_b, n_bed = load(tile + 1)
            n_row, n_col = both_ways(n_depth, n_a, n_b)
            n_rolled = rolled(n_col)
            n_bed_r = pltpu.roll(n_bed, LANES - 1, 1)
        right = tuple(jnp.where(last_lane, n, c) for n, c in zip(n_rolled, cells_r))
        bed_next = jnp.where(last_lane, n_bed_r, bed_r)
        flux = interface(by_col, right)
        flux_r = tuple(pltpu.roll(f, 1, 1) for f in flux)
        flux_left = tuple(jnp.where(first_lane, b, f) for b, f in zip(flux_before, flux_r))
        bed_rolled = pltpu.roll(bed, 1, 1)
        bed_left = jnp.where(first_lane, bed_before, bed_rolled)

        above = tuple(pltpu.roll(term, 1, 0) for term in by_row)
        inner = interface(above, by_row)
        inner = tuple(jnp.where(first_row, 0.0, f) for f in inner)
        below = tuple(pltpu.roll(f, rows - 1, 0) for f in inner)
        bed_up = jnp.where(first_row, 0.0, pltpu.roll(bed, 1, 0))
        bed_down = jnp.where(last_row, 0.0, pltpu.roll(bed, rows - 1, 0))

        pull = (0.5 * courant * gravity) * depth
        new_depth = depth - courant * ((below[0] - inner[0]) + (flux[0] - flux_left[0]))
        new_a = flow_a - courant * ((below[1] - inner[1]) + (flux[2] - flux_left[2])) - pull * (bed_down - bed_up)
        new_b = flow_b - courant * ((below[2] - inner[2]) + (flux[1] - flux_left[1])) - pull * (bed_next - bed_left)
        for part, value in enumerate((new_depth, new_a, new_b)):
            for top in range(rows // SUBLANES):
                out_ref[tile, top, part] = value[top * SUBLANES : (top + 1) * SUBLANES]
        return n_row, n_col, n_bed, n_rolled, n_bed_r, flux_r, bed_rolled

    depth, flow_a, flow_b, bed = load(0)
    by_row, by_col = both_ways(depth, flow_a, flow_b)
    edge = interface(mirrored(by_col), by_col)
    carry = (by_row, by_col, bed, rolled(by_col), pltpu.roll(bed, LANES - 1, 1), edge, bed)
    steps = (tiles - 1) // unroll

    def some(i, carry):
        for k in range(unroll):
            carry = one(i * unroll + k, carry)
        return carry

    carry = lax.fori_loop(0, steps, some, carry)
    for copy in copies:
        copy.wait()
    write_plan(zh_ref[0], counts_ref[...], slots_ref[...], plan_ref, level_ref, sizes)
    for tile in range(steps * unroll, tiles):
        carry = one(tile, carry, tile == tiles - 1)
    for tile in range(tiles):
        for top in range(rows // SUBLANES):
            at = slice(top * SUBLANES, (top + 1) * SUBLANES)
            out_ref[tile, top, 0] += rain_ref[0, at, columns(tile)]


def edge_kernel(strip_ref, first_ref, last_ref, top_ref, low_ref, part_ref, out_ref, top_sc, low_sc, *, strips):
    strip = strip_ref[0]

    def fluxes(inside, outside, at_wall, upward):
        own = tuple(inside[i] for i in range(4))
        far = tuple(outside[i] for i in range(4))
        depth = jnp.where(at_wall, own[0], far[0])
        norm = jnp.where(at_wall, -own[1], far[1])
        tang = jnp.where(at_wall, own[2], far[2])
        bed = jnp.where(at_wall, own[3], far[3])
        mine = cell_terms(*own[:3])
        other = cell_terms(depth, norm, tang)
        flux = interface(other, mine) if upward else interface(mine, other)
        sign = courant if upward else -courant
        pull = (0.5 * courant * gravity) * own[0] * bed
        return (
            sign * flux[0],
            sign * flux[1] + (pull if upward else -pull),
            sign * flux[2],
        )

    for part, value in enumerate(fluxes(first_ref, top_ref, strip == 0, True)):
        top_sc[part] = value
    for part, value in enumerate(fluxes(last_ref, low_ref, strip == strips - 1, False)):
        low_sc[part] = value
    tiles = out_ref.shape[0]
    tops = out_ref.shape[1]
    out_ref[...] = part_ref[...]
    for tile in range(tiles):
        for part in range(3):
            out_ref[tile, 0, part, 0:1, :] = part_ref[tile, 0, part, 0:1, :] + top_sc[part, tile : tile + 1, :]
            out_ref[tile, tops - 1, part, SUBLANES - 1 : SUBLANES, :] = (
                part_ref[tile, tops - 1, part, SUBLANES - 1 : SUBLANES, :] + low_sc[part, tile : tile + 1, :]
            )


def outgoing_kernel(plan_ref, held_ref, out_ref):
    for k in range(out_ref.shape[0]):
        out_ref[k] = held_ref[plan_ref[0, k]]


def slots_kernel(plan_ref, held_ref, crossed_ref, out_ref):
    held = held_ref.shape[0]
    for slot in range(out_ref.shape[0]):
        code = plan_ref[1, slot]

        @pl.when(code < held)
        def _():
            out_ref[slot] = held_ref[code]

        @pl.when(code >= held)
        def _():
            out_ref[slot] = crossed_ref[code - held]


def place_kernel(tiles_ref, out_ref):
    tiles, tops = tiles_ref.shape[:2]
    for tile in range(tiles):
        for top in range(tops):
            for part in range(3):
                out_ref[part, 0, top * SUBLANES : (top + 1) * SUBLANES, tile * LANES : (tile + 1) * LANES] = tiles_ref[
                    tile, top, part
                ]


def whole(count):
    return [pl.BlockSpec(memory_space=pltpu.VMEM)] * count


def params(moved):
    return dict(
        compiler_params=pltpu.CompilerParams(vmem_limit_bytes=16 * 1024 * 1024),
        cost_estimate=pl.CostEstimate(flops=moved * 40, bytes_accessed=moved, transcendentals=0),
    )


UNROLL = 4
HBM = pl.BlockSpec(memory_space=pltpu.HBM)
SMEM = pl.BlockSpec(memory_space=pltpu.SMEM)


def packed_edges(state, ground):
    rows, width = ground.shape
    shape = pltpu.VMEM((4, 1, width), jnp.float32)
    return pl.pallas_call(
        pack_kernel,
        out_shape=(shape, shape),
        in_specs=[HBM, HBM],
        out_specs=whole(2),
        scratch_shapes=[pltpu.SemaphoreType.DMA((2, 4))],
        name="pack",
        **params(1 << 18),
    )(*in_hbm(state, ground))


def in_hbm(*arrays):
    return [pltpu.with_memory_space_constraint(array, pltpu.HBM) for array in arrays]


def partial_step(zh, state, rain, ground, counts, slot_map, sizes, unroll=UNROLL):
    rows, width = ground.shape
    tiles, tops = width // LANES, rows // SUBLANES
    row = (1, counts.shape[0])
    return pl.pallas_call(
        functools.partial(step_kernel, unroll=unroll, sizes=sizes),
        out_shape=(
            jax.ShapeDtypeStruct((tiles, tops, 3, SUBLANES, LANES), jnp.float32),
            jax.ShapeDtypeStruct((2, row[1]), jnp.int32),
            jax.ShapeDtypeStruct((1,), jnp.int32),
        ),
        in_specs=[SMEM] + whole(2) + [HBM] * 3,
        out_specs=whole(2) + [SMEM],
        scratch_shapes=[
            pltpu.VMEM(rain.shape, jnp.float32),
            pltpu.VMEM(row, jnp.int32),
            pltpu.VMEM(row, jnp.int32),
            pltpu.SemaphoreType.DMA((3,)),
        ],
        name="step",
        **params(8 << 20),
    )(zh, state, ground, *in_hbm(rain, counts.reshape(row), slot_map.reshape(row)))


def stepped_tiles(zh, state, rain, ground, counts, slot_map, sizes):
    rows, width = ground.shape
    tiles = width // LANES
    strips = lax.axis_size("row")
    first, last = packed_edges(state, ground)
    forward = [(i, i + 1) for i in range(strips - 1)]
    backward = [(target, source) for source, target in forward]
    top = lax.ppermute(last, "row", forward)
    low = lax.ppermute(first, "row", backward)
    partial, plan, level = partial_step(zh, state, rain, ground, counts, slot_map, sizes)
    strip = lax.axis_index("row").astype(jnp.int32).reshape(1)
    square = (4, tiles, LANES)
    block = pl.pallas_call(
        functools.partial(edge_kernel, strips=strips),
        out_shape=pltpu.VMEM(partial.shape, jnp.float32),
        in_specs=[SMEM] + whole(5),
        out_specs=whole(1)[0],
        scratch_shapes=[pltpu.VMEM((3, tiles, LANES), jnp.float32)] * 2,
        name="edges",
        **params(1 << 20),
    )(strip, first.reshape(square), last.reshape(square), top.reshape(square), low.reshape(square), partial)
    return block, plan, level


SWAP = [(0, 1), (1, 0)]


def blocks_for_slots(plan, held, most):
    outgoing = pl.pallas_call(
        outgoing_kernel,
        out_shape=jax.ShapeDtypeStruct((most,) + held.shape[1:], jnp.float32),
        in_specs=[SMEM] + whole(1),
        out_specs=whole(1)[0],
        name="outgoing",
        **params(1 << 20),
    )(plan, held)
    crossed = lax.ppermute(outgoing, "zh", SWAP)
    return pl.pallas_call(
        slots_kernel,
        out_shape=jax.ShapeDtypeStruct(held.shape, jnp.float32),
        in_specs=[SMEM] + whole(2),
        out_specs=whole(1)[0],
        name="slots",
        **params(2 << 20),
    )(plan, held, crossed)


def placed_strip(block, rows, width):
    return pl.pallas_call(
        place_kernel,
        out_shape=jax.ShapeDtypeStruct((3, 1, rows, width), jnp.float32),
        in_specs=whole(1),
        out_specs=whole(1)[0],
        name="place",
        **params(2 << 20),
    )(block)


PLANE = ("y", "x", "core")
SIZES = (8, 9, 10, 11, 12, 13, 14, 15, 16, 17, 18, 20, 24, 32)


def on_device(state, rain, ground, counts, slot_map):
    rows, width = ground.shape
    zh = lax.axis_index("zh").astype(jnp.int32).reshape(1)
    block, plan, level = stepped_tiles(zh, state, rain, ground, counts, slot_map, SIZES)
    shape = block.shape
    outgoing = block.reshape((lax.axis_size(PLANE), -1) + shape[2:])
    held = lax.all_to_all(outgoing, PLANE, split_axis=0, concat_axis=0, tiled=True)
    held, level = lax.optimization_barrier((held, level))
    chosen = lax.switch(level[0], [functools.partial(blocks_for_slots, most=size) for size in SIZES], plan, held)
    returned = lax.all_to_all(chosen, PLANE, split_axis=0, concat_axis=0, tiled=True)
    return placed_strip(returned.reshape(shape), rows, width)


def solution(mesh):
    fine = Mesh(mesh.devices.reshape(4, 4, 2, 2, 4), ("y", "x", "zh", "core", "row"))
    dom = ("y", "x", "zh", "core")
    placed = (P(None, dom, "row", None), P(dom, "row", None), P("row", None), P(), P())
    return jax.shard_map(
        on_device,
        mesh=fine,
        in_specs=placed,
        out_specs=P(None, dom, "row", None),
        check_vma=False,
    )
```

```python
import functools

import jax
import jax.numpy as jnp
from jax import lax
from jax.experimental import pallas as pl
from jax.experimental.pallas import tpu as pltpu
from jax.sharding import Mesh, PartitionSpec as P

gravity = 9.81
courant = 0.04
LANES = 128
SUBLANES = 8


def cell_terms(depth, norm, tang):
    vel = norm / depth
    cel = jnp.sqrt(gravity * depth)
    press = 0.5 * gravity * depth * depth
    return depth, norm, tang, norm * vel + press, tang * vel, vel - cel, vel + cel


def interface(left, right):
    depth_l, norm_l, tang_l, fnorm_l, ftang_l, slow_l, fast_l = left
    depth_r, norm_r, tang_r, fnorm_r, ftang_r, slow_r, fast_r = right
    lower = jnp.minimum(jnp.minimum(slow_l, slow_r), 0.0)
    upper = jnp.maximum(jnp.maximum(fast_l, fast_r), 0.0)
    scale = 1.0 / (upper - lower)
    both = upper * lower
    return (
        (upper * norm_l - lower * norm_r + both * (depth_r - depth_l)) * scale,
        (upper * fnorm_l - lower * fnorm_r + both * (norm_r - norm_l)) * scale,
        (upper * ftang_l - lower * ftang_r + both * (tang_r - tang_l)) * scale,
    )


def both_ways(depth, flow_a, flow_b):
    inverse = 1.0 / depth
    cel = jnp.sqrt(gravity * depth)
    press = (0.5 * gravity) * depth * depth
    vel_a = flow_a * inverse
    vel_b = flow_b * inverse
    cross = flow_a * vel_b
    by_row = (depth, flow_a, flow_b, flow_a * vel_a + press, cross, vel_a - cel, vel_a + cel)
    by_col = (depth, flow_b, flow_a, flow_b * vel_b + press, cross, vel_b - cel, vel_b + cel)
    return by_row, by_col


def pack_kernel(state_ref, ground_ref, first_ref, last_ref, sems):
    rows = ground_ref.shape[0]
    copies = []
    for side, (row, out_ref) in enumerate(((rows - 1, last_ref), (0, first_ref))):
        at = pl.ds(row, 1)
        for part in range(3):
            copies.append(pltpu.make_async_copy(state_ref.at[part, 0, at], out_ref.at[part], sems.at[side, part]))
        copies.append(pltpu.make_async_copy(ground_ref.at[at], out_ref.at[3], sems.at[side, 3]))
    for copy in copies:
        copy.start()
    for copy in copies:
        copy.wait()


def write_plan(zh, counts, slots, plan_ref, level_ref, sizes):
    total = counts.shape[1]
    square = (total, total)
    i = lax.broadcasted_iota(jnp.int32, square, 0)
    j = lax.broadcasted_iota(jnp.int32, square, 1)

    def over_lanes(values):
        return jnp.sum(values, axis=1, keepdims=True)

    def over_rows(values):
        return jnp.sum(values, axis=0, keepdims=True)

    def half(places):
        return jnp.bitwise_and(jnp.right_shift(places, 1), 1)

    def place(places):
        return 2 * jnp.right_shift(places, 2) + jnp.bitwise_and(places, 1)

    cumul = over_lanes(jnp.where(j <= i, counts, 0))
    ordered = over_rows((cumul <= j).astype(jnp.int32))
    ancestor = over_lanes(jnp.where(slots == i, ordered, 0))
    crossing = jnp.logical_and(ancestor == j, half(i) != half(j))
    needed = (over_rows(crossing.astype(jnp.int32)) > 0).astype(jnp.int32)
    needed_col = over_lanes(jnp.where(i == j, needed, 0))
    earlier = jnp.logical_and(i < j, half(i) == half(j))
    rank = over_rows(jnp.where(earlier, needed_col, 0))
    rank_col = over_lanes(jnp.where(i == j, rank, 0))
    mine = jnp.logical_and(half(i) == zh, jnp.logical_and(needed_col > 0, rank_col == j))
    plan_ref[0:1, :] = over_rows(jnp.where(mine, place(i), 0))
    rank_of = over_lanes(jnp.where(ancestor == j, rank, 0))
    source = jnp.where(half(ancestor) == zh, place(ancestor), total // 2 + rank_of)
    here = jnp.logical_and(half(i) == zh, place(i) == j)
    plan_ref[1:2, :] = over_rows(jnp.where(here, source, 0))
    lower = jnp.sum(jnp.where(half(j[0:1]) == 0, needed, 0))
    most = jnp.maximum(lower, jnp.sum(needed) - lower)
    level_ref[0] = sum((most > size).astype(jnp.int32) for size in sizes[:-1])


def step_kernel(
    zh_ref, state_ref, ground_ref, rain_hbm, counts_hbm, slots_hbm,
    out_ref, plan_ref, level_ref, rain_ref, counts_ref, slots_ref, sems, *, unroll, sizes
):
    rows, width = ground_ref.shape
    copies = [
        pltpu.make_async_copy(counts_hbm, counts_ref, sems.at[0]),
        pltpu.make_async_copy(slots_hbm, slots_ref, sems.at[1]),
        pltpu.make_async_copy(rain_hbm, rain_ref, sems.at[2]),
    ]
    for copy in copies:
        copy.start()
    tiles = width // LANES
    shape = (rows, LANES)
    lane = lax.broadcasted_iota(jnp.int32, shape, 1)
    row = lax.broadcasted_iota(jnp.int32, shape, 0)
    first_lane, last_lane = lane == 0, lane == LANES - 1
    first_row, last_row = row == 0, row == rows - 1

    def columns(tile):
        start = tile * LANES
        return pl.ds(start if isinstance(tile, int) else pl.multiple_of(start, LANES), LANES)

    def load(tile):
        at = columns(tile)
        return state_ref[0, 0, :, at], state_ref[1, 0, :, at], state_ref[2, 0, :, at], ground_ref[:, at]

    def rolled(terms):
        return tuple(pltpu.roll(term, LANES - 1, 1) for term in terms)

    def mirrored(terms):
        depth, norm, tang, fnorm, ftang, slow, fast = terms
        return depth, -norm, tang, fnorm, -ftang, -fast, -slow

    def one(tile, carry, last=False):
        by_row, by_col, bed, cells_r, bed_r, flux_before, bed_before = carry
        depth, flow_a, flow_b = by_row[:3]
        if last:
            n_row, n_col, n_bed = by_row, by_col, bed
            n_rolled, n_bed_r = mirrored(by_col), bed
        else:
            n_depth, n_a, n_b, n_bed = load(tile + 1)
            n_row, n_col = both_ways(n_depth, n_a, n_b)
            n_rolled = rolled(n_col)
            n_bed_r = pltpu.roll(n_bed, LANES - 1, 1)
        right = tuple(jnp.where(last_lane, n, c) for n, c in zip(n_rolled, cells_r))
        bed_next = jnp.where(last_lane, n_bed_r, bed_r)
        flux = interface(by_col, right)
        flux_r = tuple(pltpu.roll(f, 1, 1) for f in flux)
        flux_left = tuple(jnp.where(first_lane, b, f) for b, f in zip(flux_before, flux_r))
        bed_rolled = pltpu.roll(bed, 1, 1)
        bed_left = jnp.where(first_lane, bed_before, bed_rolled)

        above = tuple(pltpu.roll(term, 1, 0) for term in by_row)
        inner = interface(above, by_row)
        inner = tuple(jnp.where(first_row, 0.0, f) for f in inner)
        below = tuple(pltpu.roll(f, rows - 1, 0) for f in inner)
        bed_up = jnp.where(first_row, 0.0, pltpu.roll(bed, 1, 0))
        bed_down = jnp.where(last_row, 0.0, pltpu.roll(bed, rows - 1, 0))

        pull = (0.5 * courant * gravity) * depth
        new_depth = depth - courant * ((below[0] - inner[0]) + (flux[0] - flux_left[0]))
        new_a = flow_a - courant * ((below[1] - inner[1]) + (flux[2] - flux_left[2])) - pull * (bed_down - bed_up)
        new_b = flow_b - courant * ((below[2] - inner[2]) + (flux[1] - flux_left[1])) - pull * (bed_next - bed_left)
        for part, value in enumerate((new_depth, new_a, new_b)):
            for top in range(rows // SUBLANES):
                out_ref[tile, top, part] = value[top * SUBLANES : (top + 1) * SUBLANES]
        return n_row, n_col, n_bed, n_rolled, n_bed_r, flux_r, bed_rolled

    depth, flow_a, flow_b, bed = load(0)
    by_row, by_col = both_ways(depth, flow_a, flow_b)
    edge = interface(mirrored(by_col), by_col)
    carry = (by_row, by_col, bed, rolled(by_col), pltpu.roll(bed, LANES - 1, 1), edge, bed)
    steps = (tiles - 1) // unroll

    def some(i, carry):
        for k in range(unroll):
            carry = one(i * unroll + k, carry)
        return carry

    carry = lax.fori_loop(0, steps, some, carry)
    for copy in copies:
        copy.wait()
    write_plan(zh_ref[0], counts_ref[...], slots_ref[...], plan_ref, level_ref, sizes)
    for tile in range(steps * unroll, tiles):
        carry = one(tile, carry, tile == tiles - 1)
    for tile in range(tiles):
        for top in range(rows // SUBLANES):
            at = slice(top * SUBLANES, (top + 1) * SUBLANES)
            out_ref[tile, top, 0] += rain_ref[0, at, columns(tile)]


def edge_kernel(strip_ref, first_ref, last_ref, top_ref, low_ref, part_ref, out_ref, top_sc, low_sc, *, strips):
    strip = strip_ref[0]

    def fluxes(inside, outside, at_wall, upward):
        own = tuple(inside[i] for i in range(4))
        far = tuple(outside[i] for i in range(4))
        depth = jnp.where(at_wall, own[0], far[0])
        norm = jnp.where(at_wall, -own[1], far[1])
        tang = jnp.where(at_wall, own[2], far[2])
        bed = jnp.where(at_wall, own[3], far[3])
        mine = cell_terms(*own[:3])
        other = cell_terms(depth, norm, tang)
        flux = interface(other, mine) if upward else interface(mine, other)
        sign = courant if upward else -courant
        pull = (0.5 * courant * gravity) * own[0] * bed
        return (
            sign * flux[0],
            sign * flux[1] + (pull if upward else -pull),
            sign * flux[2],
        )

    for part, value in enumerate(fluxes(first_ref, top_ref, strip == 0, True)):
        top_sc[part] = value
    for part, value in enumerate(fluxes(last_ref, low_ref, strip == strips - 1, False)):
        low_sc[part] = value
    tiles = out_ref.shape[0]
    tops = out_ref.shape[1]
    out_ref[...] = part_ref[...]
    for tile in range(tiles):
        for part in range(3):
            out_ref[tile, 0, part, 0:1, :] = part_ref[tile, 0, part, 0:1, :] + top_sc[part, tile : tile + 1, :]
            out_ref[tile, tops - 1, part, SUBLANES - 1 : SUBLANES, :] = (
                part_ref[tile, tops - 1, part, SUBLANES - 1 : SUBLANES, :] + low_sc[part, tile : tile + 1, :]
            )


def outgoing_kernel(plan_ref, held_ref, out_ref):
    for k in range(out_ref.shape[0]):
        out_ref[k] = held_ref[plan_ref[0, k]]


def slots_kernel(plan_ref, held_ref, crossed_ref, out_ref):
    held = held_ref.shape[0]
    for slot in range(out_ref.shape[0]):
        code = plan_ref[1, slot]

        @pl.when(code < held)
        def _():
            out_ref[slot] = held_ref[code]

        @pl.when(code >= held)
        def _():
            out_ref[slot] = crossed_ref[code - held]


def place_kernel(tiles_ref, out_ref):
    tiles, tops = tiles_ref.shape[:2]
    for tile in range(tiles):
        for top in range(tops):
            for part in range(3):
                out_ref[part, 0, top * SUBLANES : (top + 1) * SUBLANES, tile * LANES : (tile + 1) * LANES] = tiles_ref[
                    tile, top, part
                ]


def whole(count):
    return [pl.BlockSpec(memory_space=pltpu.VMEM)] * count


def params(moved):
    return dict(
        compiler_params=pltpu.CompilerParams(vmem_limit_bytes=16 * 1024 * 1024),
        cost_estimate=pl.CostEstimate(flops=moved * 40, bytes_accessed=moved, transcendentals=0),
    )


UNROLL = 4
HBM = pl.BlockSpec(memory_space=pltpu.HBM)
SMEM = pl.BlockSpec(memory_space=pltpu.SMEM)


def packed_edges(state, ground):
    rows, width = ground.shape
    shape = pltpu.VMEM((4, 1, width), jnp.float32)
    return pl.pallas_call(
        pack_kernel,
        out_shape=(shape, shape),
        in_specs=[HBM, HBM],
        out_specs=whole(2),
        scratch_shapes=[pltpu.SemaphoreType.DMA((2, 4))],
        name="pack",
        **params(1 << 18),
    )(*in_hbm(state, ground))


def in_hbm(*arrays):
    return [pltpu.with_memory_space_constraint(array, pltpu.HBM) for array in arrays]


def partial_step(zh, state, rain, ground, counts, slot_map, sizes, unroll=UNROLL):
    rows, width = ground.shape
    tiles, tops = width // LANES, rows // SUBLANES
    row = (1, counts.shape[0])
    return pl.pallas_call(
        functools.partial(step_kernel, unroll=unroll, sizes=sizes),
        out_shape=(
            jax.ShapeDtypeStruct((tiles, tops, 3, SUBLANES, LANES), jnp.float32),
            jax.ShapeDtypeStruct((2, row[1]), jnp.int32),
            jax.ShapeDtypeStruct((1,), jnp.int32),
        ),
        in_specs=[SMEM] + whole(2) + [HBM] * 3,
        out_specs=whole(2) + [SMEM],
        scratch_shapes=[
            pltpu.VMEM(rain.shape, jnp.float32),
            pltpu.VMEM(row, jnp.int32),
            pltpu.VMEM(row, jnp.int32),
            pltpu.SemaphoreType.DMA((3,)),
        ],
        name="step",
        **params(8 << 20),
    )(zh, state, ground, *in_hbm(rain, counts.reshape(row), slot_map.reshape(row)))


def stepped_tiles(zh, state, rain, ground, counts, slot_map, sizes):
    rows, width = ground.shape
    tiles = width // LANES
    strips = lax.axis_size("row")
    first, last = packed_edges(state, ground)
    forward = [(i, (i + 1) % strips) for i in range(strips)]
    backward = [(target, source) for source, target in forward]
    top = lax.ppermute(last, "row", forward)
    low = lax.ppermute(first, "row", backward)
    partial, plan, level = partial_step(zh, state, rain, ground, counts, slot_map, sizes)
    strip = lax.axis_index("row").astype(jnp.int32).reshape(1)
    square = (4, tiles, LANES)
    block = pl.pallas_call(
        functools.partial(edge_kernel, strips=strips),
        out_shape=pltpu.VMEM(partial.shape, jnp.float32),
        in_specs=[SMEM] + whole(5),
        out_specs=whole(1)[0],
        scratch_shapes=[pltpu.VMEM((3, tiles, LANES), jnp.float32)] * 2,
        name="edges",
        **params(1 << 20),
    )(strip, first.reshape(square), last.reshape(square), top.reshape(square), low.reshape(square), partial)
    return block, plan, level


SWAP = [(0, 1), (1, 0)]


def blocks_for_slots(plan, block, most):
    held = lax.all_to_all(block, PLANE, split_axis=0, concat_axis=0, tiled=True)
    outgoing = pl.pallas_call(
        outgoing_kernel,
        out_shape=jax.ShapeDtypeStruct((most,) + held.shape[1:], jnp.float32),
        in_specs=[SMEM] + whole(1),
        out_specs=whole(1)[0],
        name="outgoing",
        **params(1 << 20),
    )(plan, held)
    crossed = lax.ppermute(outgoing, "zh", SWAP)
    return pl.pallas_call(
        slots_kernel,
        out_shape=jax.ShapeDtypeStruct(held.shape, jnp.float32),
        in_specs=[SMEM] + whole(2),
        out_specs=whole(1)[0],
        name="slots",
        **params(2 << 20),
    )(plan, held, crossed)


def placed_strip(block, rows, width):
    return pl.pallas_call(
        place_kernel,
        out_shape=jax.ShapeDtypeStruct((3, 1, rows, width), jnp.float32),
        in_specs=whole(1),
        out_specs=whole(1)[0],
        name="place",
        **params(2 << 20),
    )(block)


PLANE = ("y", "x", "core")
SIZES = (8, 9, 10, 11, 12, 13, 14, 15, 16, 17, 18, 20, 24, 32)


def on_device(state, rain, ground, counts, slot_map):
    rows, width = ground.shape
    zh = lax.axis_index("zh").astype(jnp.int32).reshape(1)
    block, plan, level = stepped_tiles(zh, state, rain, ground, counts, slot_map, SIZES)
    shape = block.shape
    outgoing = block.reshape((lax.axis_size(PLANE), -1) + shape[2:])
    chosen = lax.switch(level[0], [functools.partial(blocks_for_slots, most=size) for size in SIZES], plan, outgoing)
    returned = lax.all_to_all(chosen, PLANE, split_axis=0, concat_axis=0, tiled=True)
    return placed_strip(returned.reshape(shape), rows, width)


def solution(mesh):
    fine = Mesh(mesh.devices.reshape(4, 4, 2, 2, 4), ("y", "x", "zh", "core", "row"))
    dom = ("y", "x", "zh", "core")
    placed = (P(None, dom, "row", None), P(dom, "row", None), P("row", None), P(), P())
    return jax.shard_map(
        on_device,
        mesh=fine,
        in_specs=placed,
        out_specs=P(None, dom, "row", None),
        check_vma=False,
    )
```

```python
import functools

import jax
import jax.numpy as jnp
from jax import lax
from jax.experimental import pallas as pl
from jax.experimental.pallas import tpu as pltpu
from jax.sharding import Mesh, PartitionSpec as P

gravity = 9.81
courant = 0.04
LANES = 128
SUBLANES = 8


def cell_terms(depth, norm, tang):
    vel = norm / depth
    cel = jnp.sqrt(gravity * depth)
    press = 0.5 * gravity * depth * depth
    return depth, norm, tang, norm * vel + press, tang * vel, vel - cel, vel + cel


def interface(left, right):
    depth_l, norm_l, tang_l, fnorm_l, ftang_l, slow_l, fast_l = left
    depth_r, norm_r, tang_r, fnorm_r, ftang_r, slow_r, fast_r = right
    lower = jnp.minimum(jnp.minimum(slow_l, slow_r), 0.0)
    upper = jnp.maximum(jnp.maximum(fast_l, fast_r), 0.0)
    scale = 1.0 / (upper - lower)
    both = upper * lower
    return (
        (upper * norm_l - lower * norm_r + both * (depth_r - depth_l)) * scale,
        (upper * fnorm_l - lower * fnorm_r + both * (norm_r - norm_l)) * scale,
        (upper * ftang_l - lower * ftang_r + both * (tang_r - tang_l)) * scale,
    )


def both_ways(depth, flow_a, flow_b):
    inverse = 1.0 / depth
    cel = jnp.sqrt(gravity * depth)
    press = (0.5 * gravity) * depth * depth
    vel_a = flow_a * inverse
    vel_b = flow_b * inverse
    cross = flow_a * vel_b
    by_row = (depth, flow_a, flow_b, flow_a * vel_a + press, cross, vel_a - cel, vel_a + cel)
    by_col = (depth, flow_b, flow_a, flow_b * vel_b + press, cross, vel_b - cel, vel_b + cel)
    return by_row, by_col


def pack_kernel(state_ref, ground_ref, first_ref, last_ref, sems):
    rows = ground_ref.shape[0]
    copies = []
    for side, (row, out_ref) in enumerate(((rows - 1, last_ref), (0, first_ref))):
        at = pl.ds(row, 1)
        for part in range(3):
            copies.append(pltpu.make_async_copy(state_ref.at[part, 0, at], out_ref.at[part], sems.at[side, part]))
        copies.append(pltpu.make_async_copy(ground_ref.at[at], out_ref.at[3], sems.at[side, 3]))
    for copy in copies:
        copy.start()
    for copy in copies:
        copy.wait()


def write_plan(zh, counts, slots, plan_ref, level_ref, sizes):
    total = counts.shape[1]
    square = (total, total)
    i = lax.broadcasted_iota(jnp.int32, square, 0)
    j = lax.broadcasted_iota(jnp.int32, square, 1)

    def over_lanes(values):
        return jnp.sum(values, axis=1, keepdims=True)

    def over_rows(values):
        return jnp.sum(values, axis=0, keepdims=True)

    def half(places):
        return jnp.bitwise_and(jnp.right_shift(places, 1), 1)

    def place(places):
        return 2 * jnp.right_shift(places, 2) + jnp.bitwise_and(places, 1)

    cumul = over_lanes(jnp.where(j <= i, counts, 0))
    ordered = over_rows((cumul <= j).astype(jnp.int32))
    ancestor = over_lanes(jnp.where(slots == i, ordered, 0))
    crossing = jnp.logical_and(ancestor == j, half(i) != half(j))
    needed = (over_rows(crossing.astype(jnp.int32)) > 0).astype(jnp.int32)
    needed_col = over_lanes(jnp.where(i == j, needed, 0))
    earlier = jnp.logical_and(i < j, half(i) == half(j))
    rank = over_rows(jnp.where(earlier, needed_col, 0))
    rank_col = over_lanes(jnp.where(i == j, rank, 0))
    mine = jnp.logical_and(half(i) == zh, jnp.logical_and(needed_col > 0, rank_col == j))
    plan_ref[0:1, :] = over_rows(jnp.where(mine, place(i), 0))
    rank_of = over_lanes(jnp.where(ancestor == j, rank, 0))
    source = jnp.where(half(ancestor) == zh, place(ancestor), total // 2 + rank_of)
    here = jnp.logical_and(half(i) == zh, place(i) == j)
    plan_ref[1:2, :] = over_rows(jnp.where(here, source, 0))
    lower = jnp.sum(jnp.where(half(j[0:1]) == 0, needed, 0))
    most = jnp.maximum(lower, jnp.sum(needed) - lower)
    level_ref[0] = sum((most > size).astype(jnp.int32) for size in sizes[:-1])


def step_kernel(
    zh_ref, state_ref, ground_ref, rain_hbm, counts_hbm, slots_hbm,
    out_ref, plan_smem, level_ref, rain_ref, counts_ref, slots_ref, plan_ref, sems, *, unroll, tail, sizes
):
    rows, width = ground_ref.shape
    copies = [
        pltpu.make_async_copy(counts_hbm, counts_ref, sems.at[0]),
        pltpu.make_async_copy(slots_hbm, slots_ref, sems.at[1]),
        pltpu.make_async_copy(rain_hbm, rain_ref, sems.at[2]),
    ]
    for copy in copies:
        copy.start()
    tiles = width // LANES
    shape = (rows, LANES)
    lane = lax.broadcasted_iota(jnp.int32, shape, 1)
    row = lax.broadcasted_iota(jnp.int32, shape, 0)
    first_lane, last_lane = lane == 0, lane == LANES - 1
    first_row, last_row = row == 0, row == rows - 1

    def columns(tile):
        start = tile * LANES
        return pl.ds(start if isinstance(tile, int) else pl.multiple_of(start, LANES), LANES)

    def load(tile):
        at = columns(tile)
        return state_ref[0, 0, :, at], state_ref[1, 0, :, at], state_ref[2, 0, :, at], ground_ref[:, at]

    def rolled(terms):
        return tuple(pltpu.roll(term, LANES - 1, 1) for term in terms)

    def mirrored(terms):
        depth, norm, tang, fnorm, ftang, slow, fast = terms
        return depth, -norm, tang, fnorm, -ftang, -fast, -slow

    def one(tile, carry, last=False):
        by_row, by_col, bed, cells_r, bed_r, flux_before, bed_before = carry
        depth, flow_a, flow_b = by_row[:3]
        if last:
            n_row, n_col, n_bed = by_row, by_col, bed
            n_rolled, n_bed_r = mirrored(by_col), bed
        else:
            n_depth, n_a, n_b, n_bed = load(tile + 1)
            n_row, n_col = both_ways(n_depth, n_a, n_b)
            n_rolled = rolled(n_col)
            n_bed_r = pltpu.roll(n_bed, LANES - 1, 1)
        right = tuple(jnp.where(last_lane, n, c) for n, c in zip(n_rolled, cells_r))
        bed_next = jnp.where(last_lane, n_bed_r, bed_r)
        flux = interface(by_col, right)
        flux_r = tuple(pltpu.roll(f, 1, 1) for f in flux)
        flux_left = tuple(jnp.where(first_lane, b, f) for b, f in zip(flux_before, flux_r))
        bed_rolled = pltpu.roll(bed, 1, 1)
        bed_left = jnp.where(first_lane, bed_before, bed_rolled)

        above = tuple(pltpu.roll(term, 1, 0) for term in by_row)
        inner = interface(above, by_row)
        inner = tuple(jnp.where(first_row, 0.0, f) for f in inner)
        below = tuple(pltpu.roll(f, rows - 1, 0) for f in inner)
        bed_up = jnp.where(first_row, 0.0, pltpu.roll(bed, 1, 0))
        bed_down = jnp.where(last_row, 0.0, pltpu.roll(bed, rows - 1, 0))

        pull = (0.5 * courant * gravity) * depth
        new_depth = depth - courant * ((below[0] - inner[0]) + (flux[0] - flux_left[0]))
        new_a = flow_a - courant * ((below[1] - inner[1]) + (flux[2] - flux_left[2])) - pull * (bed_down - bed_up)
        new_b = flow_b - courant * ((below[2] - inner[2]) + (flux[1] - flux_left[1])) - pull * (bed_next - bed_left)
        for part, value in enumerate((new_depth, new_a, new_b)):
            for top in range(rows // SUBLANES):
                out_ref[tile, top, part] = value[top * SUBLANES : (top + 1) * SUBLANES]
        return n_row, n_col, n_bed, n_rolled, n_bed_r, flux_r, bed_rolled

    depth, flow_a, flow_b, bed = load(0)
    by_row, by_col = both_ways(depth, flow_a, flow_b)
    edge = interface(mirrored(by_col), by_col)
    carry = (by_row, by_col, bed, rolled(by_col), pltpu.roll(bed, LANES - 1, 1), edge, bed)
    steps = (tiles - max(1, min(tail, tiles))) // unroll

    def some(i, carry):
        for k in range(unroll):
            carry = one(i * unroll + k, carry)
        return carry

    carry = lax.fori_loop(0, steps, some, carry)
    for copy in copies:
        copy.wait()
    write_plan(zh_ref[0], counts_ref[...], slots_ref[...], plan_ref, level_ref, sizes)
    to_scalars = pltpu.make_async_copy(plan_ref, plan_smem, sems.at[3])
    to_scalars.start()
    for tile in range(steps * unroll, tiles):
        carry = one(tile, carry, tile == tiles - 1)
    for tile in range(tiles):
        for top in range(rows // SUBLANES):
            at = slice(top * SUBLANES, (top + 1) * SUBLANES)
            out_ref[tile, top, 0] += rain_ref[0, at, columns(tile)]
    to_scalars.wait()


def edge_kernel(strip_ref, first_ref, last_ref, top_ref, low_ref, part_ref, out_ref, top_sc, low_sc, *, strips):
    strip = strip_ref[0]

    def fluxes(inside, outside, at_wall, upward):
        own = tuple(inside[i] for i in range(4))
        far = tuple(outside[i] for i in range(4))
        depth = jnp.where(at_wall, own[0], far[0])
        norm = jnp.where(at_wall, -own[1], far[1])
        tang = jnp.where(at_wall, own[2], far[2])
        bed = jnp.where(at_wall, own[3], far[3])
        mine = cell_terms(*own[:3])
        other = cell_terms(depth, norm, tang)
        flux = interface(other, mine) if upward else interface(mine, other)
        sign = courant if upward else -courant
        pull = (0.5 * courant * gravity) * own[0] * bed
        return (
            sign * flux[0],
            sign * flux[1] + (pull if upward else -pull),
            sign * flux[2],
        )

    for part, value in enumerate(fluxes(first_ref, top_ref, strip == 0, True)):
        top_sc[part] = value
    for part, value in enumerate(fluxes(last_ref, low_ref, strip == strips - 1, False)):
        low_sc[part] = value
    tiles = out_ref.shape[0]
    tops = out_ref.shape[1]
    out_ref[...] = part_ref[...]
    for tile in range(tiles):
        for part in range(3):
            out_ref[tile, 0, part, 0:1, :] = part_ref[tile, 0, part, 0:1, :] + top_sc[part, tile : tile + 1, :]
            out_ref[tile, tops - 1, part, SUBLANES - 1 : SUBLANES, :] = (
                part_ref[tile, tops - 1, part, SUBLANES - 1 : SUBLANES, :] + low_sc[part, tile : tile + 1, :]
            )


def outgoing_kernel(plan_ref, held_ref, out_ref):
    for k in range(out_ref.shape[0]):
        out_ref[k] = held_ref[plan_ref[0, k]]


def slots_kernel(plan_ref, held_ref, crossed_ref, out_ref):
    held, most = held_ref.shape[0], crossed_ref.shape[0]
    for slot in range(out_ref.shape[0]):
        code = plan_ref[1, slot]
        near = held_ref[jnp.minimum(code, held - 1)]
        far = crossed_ref[jnp.clip(code - held, 0, most - 1)]
        out_ref[slot] = jnp.where(code < held, near, far)


def place_kernel(tiles_ref, out_hbm, rows_ref, sems):
    tiles, tops, parts = tiles_ref.shape[:3]
    copies = []
    for part in range(parts):
        for top in range(tops):
            at = pl.ds(top * SUBLANES, SUBLANES)
            for tile in range(tiles):
                rows_ref[part, at, tile * LANES : (tile + 1) * LANES] = tiles_ref[tile, top, part]
            copies.append(
                pltpu.make_async_copy(rows_ref.at[part, at], out_hbm.at[part, 0, at], sems.at[part, top])
            )
            copies[-1].start()
    for copy in copies:
        copy.wait()


def whole(count):
    return [pl.BlockSpec(memory_space=pltpu.VMEM)] * count


def params(moved):
    return dict(
        compiler_params=pltpu.CompilerParams(vmem_limit_bytes=16 * 1024 * 1024),
        cost_estimate=pl.CostEstimate(flops=moved * 40, bytes_accessed=moved, transcendentals=0),
    )


UNROLL = 8
TAIL = 16
HBM = pl.BlockSpec(memory_space=pltpu.HBM)
SMEM = pl.BlockSpec(memory_space=pltpu.SMEM)


def packed_edges(state, ground):
    rows, width = ground.shape
    shape = pltpu.VMEM((4, 1, width), jnp.float32)
    return pl.pallas_call(
        pack_kernel,
        out_shape=(shape, shape),
        in_specs=[HBM, HBM],
        out_specs=whole(2),
        scratch_shapes=[pltpu.SemaphoreType.DMA((2, 4))],
        name="pack",
        **params(1 << 18),
    )(*in_hbm(state, ground))


def in_hbm(*arrays):
    return [pltpu.with_memory_space_constraint(array, pltpu.HBM) for array in arrays]


def partial_step(zh, state, rain, ground, counts, slot_map, sizes, unroll=UNROLL, tail=TAIL):
    rows, width = ground.shape
    tiles, tops = width // LANES, rows // SUBLANES
    row = (1, counts.shape[0])
    return pl.pallas_call(
        functools.partial(step_kernel, unroll=unroll, tail=tail, sizes=sizes),
        out_shape=(
            jax.ShapeDtypeStruct((tiles, tops, 3, SUBLANES, LANES), jnp.float32),
            pltpu.SMEM((2, row[1]), jnp.int32),
            pltpu.SMEM((1,), jnp.int32),
        ),
        in_specs=[SMEM] + whole(2) + [HBM] * 3,
        out_specs=whole(1) + [SMEM] * 2,
        scratch_shapes=[
            pltpu.VMEM(rain.shape, jnp.float32),
            pltpu.VMEM(row, jnp.int32),
            pltpu.VMEM(row, jnp.int32),
            pltpu.VMEM((2, row[1]), jnp.int32),
            pltpu.SemaphoreType.DMA((4,)),
        ],
        name="step",
        **params(8 << 20),
    )(zh, state, ground, *in_hbm(rain, counts.reshape(row), slot_map.reshape(row)))


def stepped_tiles(zh, state, rain, ground, counts, slot_map, sizes):
    rows, width = ground.shape
    tiles = width // LANES
    strips = lax.axis_size("row")
    first, last = packed_edges(state, ground)
    forward = [(i, (i + 1) % strips) for i in range(strips)]
    backward = [(target, source) for source, target in forward]
    top = lax.ppermute(last, "row", forward)
    low = lax.ppermute(first, "row", backward)
    partial, plan, level = partial_step(zh, state, rain, ground, counts, slot_map, sizes)
    strip = lax.axis_index("row").astype(jnp.int32).reshape(1)
    square = (4, tiles, LANES)
    block = pl.pallas_call(
        functools.partial(edge_kernel, strips=strips),
        out_shape=pltpu.VMEM(partial.shape, jnp.float32),
        in_specs=[SMEM] + whole(5),
        out_specs=whole(1)[0],
        scratch_shapes=[pltpu.VMEM((3, tiles, LANES), jnp.float32)] * 2,
        name="edges",
        **params(1 << 20),
    )(strip, first.reshape(square), last.reshape(square), top.reshape(square), low.reshape(square), partial)
    return block, plan, level


SWAP = [(0, 1), (1, 0)]


def blocks_for_slots(plan, block, most):
    held = lax.all_to_all(block, PLANE, split_axis=0, concat_axis=0, tiled=True)
    outgoing = pl.pallas_call(
        outgoing_kernel,
        out_shape=jax.ShapeDtypeStruct((most,) + held.shape[1:], jnp.float32),
        in_specs=[SMEM] + whole(1),
        out_specs=whole(1)[0],
        name="outgoing",
        **params(1 << 20),
    )(plan, held)
    crossed = lax.ppermute(outgoing, "zh", SWAP)
    return pl.pallas_call(
        slots_kernel,
        out_shape=jax.ShapeDtypeStruct(held.shape, jnp.float32),
        in_specs=[SMEM] + whole(2),
        out_specs=whole(1)[0],
        name="slots",
        **params(2 << 20),
    )(plan, held, crossed)


def placed_strip(block, rows, width):
    return pl.pallas_call(
        place_kernel,
        out_shape=jax.ShapeDtypeStruct((3, 1, rows, width), jnp.float32),
        in_specs=whole(1),
        out_specs=HBM,
        scratch_shapes=[
            pltpu.VMEM((3, rows, width), jnp.float32),
            pltpu.SemaphoreType.DMA((3, rows // SUBLANES)),
        ],
        name="place",
        **params(2 << 20),
    )(block)


PLANE = ("y", "x", "core")
SIZES = (8, 9, 10, 11, 12, 13, 14, 15, 16, 17, 18, 20, 24, 32)


def on_device(state, rain, ground, counts, slot_map):
    rows, width = ground.shape
    zh = lax.axis_index("zh").astype(jnp.int32).reshape(1)
    block, plan, level = stepped_tiles(zh, state, rain, ground, counts, slot_map, SIZES)
    shape = block.shape
    outgoing = block.reshape((lax.axis_size(PLANE), -1) + shape[2:])
    chosen = lax.switch(level[0], [functools.partial(blocks_for_slots, most=size) for size in SIZES], plan, outgoing)
    returned = lax.all_to_all(chosen, PLANE, split_axis=0, concat_axis=0, tiled=True)
    return placed_strip(returned.reshape(shape), rows, width)


def solution(mesh):
    fine = Mesh(mesh.devices.reshape(4, 4, 2, 2, 4), ("y", "x", "zh", "core", "row"))
    dom = ("y", "x", "zh", "core")
    placed = (P(None, dom, "row", None), P(dom, "row", None), P("row", None), P(), P())
    return jax.shard_map(
        on_device,
        mesh=fine,
        in_specs=placed,
        out_specs=P(None, dom, "row", None),
        check_vma=False,
    )
```

```python
import functools

import jax
import jax.numpy as jnp
from jax import lax
from jax.experimental import pallas as pl
from jax.experimental.pallas import tpu as pltpu
from jax.sharding import Mesh, PartitionSpec as P

gravity = 9.81
courant = 0.04
LANES = 128
SUBLANES = 8


def cell_terms(depth, norm, tang):
    vel = norm / depth
    cel = jnp.sqrt(gravity * depth)
    press = 0.5 * gravity * depth * depth
    return depth, norm, tang, norm * vel + press, tang * vel, vel - cel, vel + cel


def interface(left, right):
    depth_l, norm_l, tang_l, fnorm_l, ftang_l, slow_l, fast_l = left
    depth_r, norm_r, tang_r, fnorm_r, ftang_r, slow_r, fast_r = right
    lower = jnp.minimum(jnp.minimum(slow_l, slow_r), 0.0)
    upper = jnp.maximum(jnp.maximum(fast_l, fast_r), 0.0)
    scale = 1.0 / (upper - lower)
    both = upper * lower
    return (
        (upper * norm_l - lower * norm_r + both * (depth_r - depth_l)) * scale,
        (upper * fnorm_l - lower * fnorm_r + both * (norm_r - norm_l)) * scale,
        (upper * ftang_l - lower * ftang_r + both * (tang_r - tang_l)) * scale,
    )


def both_ways(depth, flow_a, flow_b):
    inverse = 1.0 / depth
    cel = jnp.sqrt(gravity * depth)
    press = (0.5 * gravity) * depth * depth
    vel_a = flow_a * inverse
    vel_b = flow_b * inverse
    cross = flow_a * vel_b
    by_row = (depth, flow_a, flow_b, flow_a * vel_a + press, cross, vel_a - cel, vel_a + cel)
    by_col = (depth, flow_b, flow_a, flow_b * vel_b + press, cross, vel_b - cel, vel_b + cel)
    return by_row, by_col


def pack_kernel(state_ref, ground_ref, first_ref, last_ref, sems):
    rows = ground_ref.shape[0]
    copies = []
    for side, (row, out_ref) in enumerate(((rows - 1, last_ref), (0, first_ref))):
        at = pl.ds(row, 1)
        for part in range(3):
            copies.append(pltpu.make_async_copy(state_ref.at[part, 0, at], out_ref.at[part], sems.at[side, part]))
        copies.append(pltpu.make_async_copy(ground_ref.at[at], out_ref.at[3], sems.at[side, 3]))
    for copy in copies:
        copy.start()
    for copy in copies:
        copy.wait()


def write_plan(zh, counts, slots, plan_ref, level_ref, sizes):
    total = counts.shape[1]
    square = (total, total)
    i = lax.broadcasted_iota(jnp.int32, square, 0)
    j = lax.broadcasted_iota(jnp.int32, square, 1)

    def over_lanes(values):
        return jnp.sum(values, axis=1, keepdims=True)

    def over_rows(values):
        return jnp.sum(values, axis=0, keepdims=True)

    def half(places):
        return jnp.bitwise_and(jnp.right_shift(places, 1), 1)

    def place(places):
        return 2 * jnp.right_shift(places, 2) + jnp.bitwise_and(places, 1)

    cumul = over_lanes(jnp.where(j <= i, counts, 0))
    ordered = over_rows((cumul <= j).astype(jnp.int32))
    ancestor = over_lanes(jnp.where(slots == i, ordered, 0))
    crossing = jnp.logical_and(ancestor == j, half(i) != half(j))
    needed = (over_rows(crossing.astype(jnp.int32)) > 0).astype(jnp.int32)
    needed_col = over_lanes(jnp.where(i == j, needed, 0))
    earlier = jnp.logical_and(i < j, half(i) == half(j))
    rank = over_rows(jnp.where(earlier, needed_col, 0))
    rank_col = over_lanes(jnp.where(i == j, rank, 0))
    mine = jnp.logical_and(half(i) == zh, jnp.logical_and(needed_col > 0, rank_col == j))
    plan_ref[0:1, :] = over_rows(jnp.where(mine, place(i), 0))
    rank_of = over_lanes(jnp.where(ancestor == j, rank, 0))
    source = jnp.where(half(ancestor) == zh, place(ancestor), total // 2 + rank_of)
    here = jnp.logical_and(half(i) == zh, place(i) == j)
    plan_ref[1:2, :] = over_rows(jnp.where(here, source, 0))
    lower = jnp.sum(jnp.where(half(j[0:1]) == 0, needed, 0))
    most = jnp.maximum(lower, jnp.sum(needed) - lower)
    level_ref[0] = sum((most > size).astype(jnp.int32) for size in sizes[:-1])


def step_kernel(
    zh_ref, state_ref, ground_ref, rain_hbm, counts_hbm, slots_hbm,
    out_ref, plan_smem, level_ref, rain_ref, counts_ref, slots_ref, plan_ref, sems, *, unroll, tail, sizes
):
    rows, width = ground_ref.shape
    copies = [
        pltpu.make_async_copy(counts_hbm, counts_ref, sems.at[0]),
        pltpu.make_async_copy(slots_hbm, slots_ref, sems.at[1]),
        pltpu.make_async_copy(rain_hbm, rain_ref, sems.at[2]),
    ]
    for copy in copies:
        copy.start()
    tiles = width // LANES
    shape = (rows, LANES)
    lane = lax.broadcasted_iota(jnp.int32, shape, 1)
    row = lax.broadcasted_iota(jnp.int32, shape, 0)
    first_lane, last_lane = lane == 0, lane == LANES - 1
    first_row, last_row = row == 0, row == rows - 1

    def columns(tile):
        start = tile * LANES
        return pl.ds(start if isinstance(tile, int) else pl.multiple_of(start, LANES), LANES)

    def load(tile):
        at = columns(tile)
        return state_ref[0, 0, :, at], state_ref[1, 0, :, at], state_ref[2, 0, :, at], ground_ref[:, at]

    def rolled(terms):
        return tuple(pltpu.roll(term, LANES - 1, 1) for term in terms)

    def mirrored(terms):
        depth, norm, tang, fnorm, ftang, slow, fast = terms
        return depth, -norm, tang, fnorm, -ftang, -fast, -slow

    def one(tile, carry, last=False):
        by_row, by_col, bed, cells_r, bed_r, flux_before, bed_before = carry
        depth, flow_a, flow_b = by_row[:3]
        if last:
            n_row, n_col, n_bed = by_row, by_col, bed
            n_rolled, n_bed_r = mirrored(by_col), bed
        else:
            n_depth, n_a, n_b, n_bed = load(tile + 1)
            n_row, n_col = both_ways(n_depth, n_a, n_b)
            n_rolled = rolled(n_col)
            n_bed_r = pltpu.roll(n_bed, LANES - 1, 1)
        right = tuple(jnp.where(last_lane, n, c) for n, c in zip(n_rolled, cells_r))
        bed_next = jnp.where(last_lane, n_bed_r, bed_r)
        flux = interface(by_col, right)
        flux_r = tuple(pltpu.roll(f, 1, 1) for f in flux)
        flux_left = tuple(jnp.where(first_lane, b, f) for b, f in zip(flux_before, flux_r))
        bed_rolled = pltpu.roll(bed, 1, 1)
        bed_left = jnp.where(first_lane, bed_before, bed_rolled)

        above = tuple(pltpu.roll(term, 1, 0) for term in by_row)
        inner = interface(above, by_row)
        inner = tuple(jnp.where(first_row, 0.0, f) for f in inner)
        below = tuple(pltpu.roll(f, rows - 1, 0) for f in inner)
        bed_up = jnp.where(first_row, 0.0, pltpu.roll(bed, 1, 0))
        bed_down = jnp.where(last_row, 0.0, pltpu.roll(bed, rows - 1, 0))

        pull = (0.5 * courant * gravity) * depth
        new_depth = depth - courant * ((below[0] - inner[0]) + (flux[0] - flux_left[0]))
        new_a = flow_a - courant * ((below[1] - inner[1]) + (flux[2] - flux_left[2])) - pull * (bed_down - bed_up)
        new_b = flow_b - courant * ((below[2] - inner[2]) + (flux[1] - flux_left[1])) - pull * (bed_next - bed_left)
        for part, value in enumerate((new_depth, new_a, new_b)):
            for top in range(rows // SUBLANES):
                out_ref[tile, top, part] = value[top * SUBLANES : (top + 1) * SUBLANES]
        return n_row, n_col, n_bed, n_rolled, n_bed_r, flux_r, bed_rolled

    depth, flow_a, flow_b, bed = load(0)
    by_row, by_col = both_ways(depth, flow_a, flow_b)
    edge = interface(mirrored(by_col), by_col)
    carry = (by_row, by_col, bed, rolled(by_col), pltpu.roll(bed, LANES - 1, 1), edge, bed)
    steps = (tiles - max(1, min(tail, tiles))) // unroll

    def some(i, carry):
        for k in range(unroll):
            carry = one(i * unroll + k, carry)
        return carry

    carry = lax.fori_loop(0, steps, some, carry)
    for copy in copies:
        copy.wait()
    write_plan(zh_ref[0], counts_ref[...], slots_ref[...], plan_ref, level_ref, sizes)
    to_scalars = pltpu.make_async_copy(plan_ref, plan_smem, sems.at[3])
    to_scalars.start()
    for tile in range(steps * unroll, tiles):
        carry = one(tile, carry, tile == tiles - 1)
    for tile in range(tiles):
        for top in range(rows // SUBLANES):
            at = slice(top * SUBLANES, (top + 1) * SUBLANES)
            out_ref[tile, top, 0] += rain_ref[0, at, columns(tile)]
    to_scalars.wait()


def edge_kernel(strip_ref, first_ref, last_ref, top_ref, low_ref, part_ref, out_ref, top_sc, low_sc, *, strips):
    strip = strip_ref[0]

    def fluxes(inside, outside, at_wall, upward):
        own = tuple(inside[i] for i in range(4))
        far = tuple(outside[i] for i in range(4))
        depth = jnp.where(at_wall, own[0], far[0])
        norm = jnp.where(at_wall, -own[1], far[1])
        tang = jnp.where(at_wall, own[2], far[2])
        bed = jnp.where(at_wall, own[3], far[3])
        mine = cell_terms(*own[:3])
        other = cell_terms(depth, norm, tang)
        flux = interface(other, mine) if upward else interface(mine, other)
        sign = courant if upward else -courant
        pull = (0.5 * courant * gravity) * own[0] * bed
        return (
            sign * flux[0],
            sign * flux[1] + (pull if upward else -pull),
            sign * flux[2],
        )

    for part, value in enumerate(fluxes(first_ref, top_ref, strip == 0, True)):
        top_sc[part] = value
    for part, value in enumerate(fluxes(last_ref, low_ref, strip == strips - 1, False)):
        low_sc[part] = value
    tiles = out_ref.shape[0]
    tops = out_ref.shape[1]
    out_ref[...] = part_ref[...]
    for tile in range(tiles):
        for part in range(3):
            out_ref[tile, 0, part, 0:1, :] = part_ref[tile, 0, part, 0:1, :] + top_sc[part, tile : tile + 1, :]
            out_ref[tile, tops - 1, part, SUBLANES - 1 : SUBLANES, :] = (
                part_ref[tile, tops - 1, part, SUBLANES - 1 : SUBLANES, :] + low_sc[part, tile : tile + 1, :]
            )


def outgoing_kernel(plan_ref, held_ref, out_ref):
    for k in range(out_ref.shape[0]):
        out_ref[k] = held_ref[plan_ref[0, k]]


def slots_kernel(plan_ref, held_ref, crossed_ref, out_ref):
    held, most = held_ref.shape[0], crossed_ref.shape[0]
    for slot in range(out_ref.shape[0]):
        code = plan_ref[1, slot]
        near = held_ref[jnp.minimum(code, held - 1)]
        far = crossed_ref[jnp.clip(code - held, 0, most - 1)]
        out_ref[slot] = jnp.where(code < held, near, far)


def place_kernel(tiles_ref, out_hbm, rows_ref, sems):
    tiles, tops, parts = tiles_ref.shape[:3]
    copies = []
    for part in range(parts):
        for top in range(tops):
            at = pl.ds(top * SUBLANES, SUBLANES)
            for tile in range(tiles):
                rows_ref[part, at, tile * LANES : (tile + 1) * LANES] = tiles_ref[tile, top, part]
            copies.append(
                pltpu.make_async_copy(rows_ref.at[part, at], out_hbm.at[part, 0, at], sems.at[part, top])
            )
            copies[-1].start()
    for copy in copies:
        copy.wait()


def whole(count):
    return [pl.BlockSpec(memory_space=pltpu.VMEM)] * count


def params(moved):
    return dict(
        compiler_params=pltpu.CompilerParams(vmem_limit_bytes=16 * 1024 * 1024),
        cost_estimate=pl.CostEstimate(flops=moved * 40, bytes_accessed=moved, transcendentals=0),
    )


COLUMN = ("zh", "row")
UNROLL = 8
TAIL = 16
HBM = pl.BlockSpec(memory_space=pltpu.HBM)
SMEM = pl.BlockSpec(memory_space=pltpu.SMEM)


def packed_edges(state, ground):
    rows, width = ground.shape
    shape = pltpu.VMEM((4, 1, width), jnp.float32)
    return pl.pallas_call(
        pack_kernel,
        out_shape=(shape, shape),
        in_specs=[HBM, HBM],
        out_specs=whole(2),
        scratch_shapes=[pltpu.SemaphoreType.DMA((2, 4))],
        name="pack",
        **params(1 << 18),
    )(*in_hbm(state, ground))


def in_hbm(*arrays):
    return [pltpu.with_memory_space_constraint(array, pltpu.HBM) for array in arrays]


def partial_step(zh, state, rain, ground, counts, slot_map, sizes, unroll=UNROLL, tail=TAIL):
    rows, width = ground.shape
    tiles, tops = width // LANES, rows // SUBLANES
    row = (1, counts.shape[0])
    return pl.pallas_call(
        functools.partial(step_kernel, unroll=unroll, tail=tail, sizes=sizes),
        out_shape=(
            jax.ShapeDtypeStruct((tiles, tops, 3, SUBLANES, LANES), jnp.float32),
            pltpu.SMEM((2, row[1]), jnp.int32),
            pltpu.SMEM((1,), jnp.int32),
        ),
        in_specs=[SMEM] + whole(2) + [HBM] * 3,
        out_specs=whole(1) + [SMEM] * 2,
        scratch_shapes=[
            pltpu.VMEM(rain.shape, jnp.float32),
            pltpu.VMEM(row, jnp.int32),
            pltpu.VMEM(row, jnp.int32),
            pltpu.VMEM((2, row[1]), jnp.int32),
            pltpu.SemaphoreType.DMA((4,)),
        ],
        name="step",
        **params(8 << 20),
    )(zh, state, ground, *in_hbm(rain, counts.reshape(row), slot_map.reshape(row)))


def stepped_tiles(zh, state, rain, ground, counts, slot_map, sizes):
    rows, width = ground.shape
    tiles = width // LANES
    strips = lax.axis_size("row")
    first, last = packed_edges(state, ground)
    count = lax.axis_size(COLUMN)
    forward = [(i, (i + 1) % count) for i in range(count)]
    backward = [(target, source) for source, target in forward]
    top = lax.ppermute(last, COLUMN, forward)
    low = lax.ppermute(first, COLUMN, backward)
    partial, plan, level = partial_step(zh, state, rain, ground, counts, slot_map, sizes)
    strip = lax.axis_index("row").astype(jnp.int32).reshape(1)
    square = (4, tiles, LANES)
    block = pl.pallas_call(
        functools.partial(edge_kernel, strips=strips),
        out_shape=pltpu.VMEM(partial.shape, jnp.float32),
        in_specs=[SMEM] + whole(5),
        out_specs=whole(1)[0],
        scratch_shapes=[pltpu.VMEM((3, tiles, LANES), jnp.float32)] * 2,
        name="edges",
        **params(1 << 20),
    )(strip, first.reshape(square), last.reshape(square), top.reshape(square), low.reshape(square), partial)
    return block, plan, level


SWAP = [(0, 1), (1, 0)]


def blocks_for_slots(plan, block, most):
    held = lax.all_to_all(block, PLANE, split_axis=0, concat_axis=0, tiled=True)
    outgoing = pl.pallas_call(
        outgoing_kernel,
        out_shape=jax.ShapeDtypeStruct((most,) + held.shape[1:], jnp.float32),
        in_specs=[SMEM] + whole(1),
        out_specs=whole(1)[0],
        name="outgoing",
        **params(1 << 20),
    )(plan, held)
    crossed = lax.ppermute(outgoing, "zh", SWAP)
    return pl.pallas_call(
        slots_kernel,
        out_shape=jax.ShapeDtypeStruct(held.shape, jnp.float32),
        in_specs=[SMEM] + whole(2),
        out_specs=whole(1)[0],
        name="slots",
        **params(2 << 20),
    )(plan, held, crossed)


def placed_strip(block, rows, width):
    return pl.pallas_call(
        place_kernel,
        out_shape=jax.ShapeDtypeStruct((3, 1, rows, width), jnp.float32),
        in_specs=whole(1),
        out_specs=HBM,
        scratch_shapes=[
            pltpu.VMEM((3, rows, width), jnp.float32),
            pltpu.SemaphoreType.DMA((3, rows // SUBLANES)),
        ],
        name="place",
        **params(2 << 20),
    )(block)


PLANE = ("y", "x", "core")
SIZES = (8, 9, 10, 11, 12, 13, 14, 15, 16, 17, 18, 20, 24, 32)


def on_device(state, rain, ground, counts, slot_map):
    rows, width = ground.shape
    zh = lax.axis_index("zh").astype(jnp.int32).reshape(1)
    block, plan, level = stepped_tiles(zh, state, rain, ground, counts, slot_map, SIZES)
    shape = block.shape
    outgoing = block.reshape((lax.axis_size(PLANE), -1) + shape[2:])
    chosen = lax.switch(level[0], [functools.partial(blocks_for_slots, most=size) for size in SIZES], plan, outgoing)
    returned = lax.all_to_all(chosen, PLANE, split_axis=0, concat_axis=0, tiled=True)
    return placed_strip(returned.reshape(shape), rows, width)


def solution(mesh):
    fine = Mesh(mesh.devices.reshape(4, 4, 2, 2, 4), ("y", "x", "zh", "core", "row"))
    dom = ("y", "x", "zh", "core")
    placed = (P(None, dom, "row", None), P(dom, "row", None), P("row", None), P(), P())
    return jax.shard_map(
        on_device,
        mesh=fine,
        in_specs=placed,
        out_specs=P(None, dom, "row", None),
        check_vma=False,
    )
```

```python
import functools

import jax
import jax.numpy as jnp
from jax import lax
from jax.experimental import pallas as pl
from jax.experimental.pallas import tpu as pltpu
from jax.sharding import Mesh, PartitionSpec as P

gravity = 9.81
courant = 0.04
LANES = 128
SUBLANES = 8


def cell_terms(depth, norm, tang):
    vel = norm / depth
    cel = jnp.sqrt(gravity * depth)
    press = 0.5 * gravity * depth * depth
    return depth, norm, tang, norm * vel + press, tang * vel, vel - cel, vel + cel


def interface(left, right):
    depth_l, norm_l, tang_l, fnorm_l, ftang_l, slow_l, fast_l = left
    depth_r, norm_r, tang_r, fnorm_r, ftang_r, slow_r, fast_r = right
    lower = jnp.minimum(jnp.minimum(slow_l, slow_r), 0.0)
    upper = jnp.maximum(jnp.maximum(fast_l, fast_r), 0.0)
    scale = 1.0 / (upper - lower)
    both = upper * lower
    return (
        (upper * norm_l - lower * norm_r + both * (depth_r - depth_l)) * scale,
        (upper * fnorm_l - lower * fnorm_r + both * (norm_r - norm_l)) * scale,
        (upper * ftang_l - lower * ftang_r + both * (tang_r - tang_l)) * scale,
    )


def both_ways(depth, flow_a, flow_b):
    inverse = 1.0 / depth
    cel = jnp.sqrt(gravity * depth)
    press = (0.5 * gravity) * depth * depth
    vel_a = flow_a * inverse
    vel_b = flow_b * inverse
    cross = flow_a * vel_b
    by_row = (depth, flow_a, flow_b, flow_a * vel_a + press, cross, vel_a - cel, vel_a + cel)
    by_col = (depth, flow_b, flow_a, flow_b * vel_b + press, cross, vel_b - cel, vel_b + cel)
    return by_row, by_col


def pack_kernel(state_ref, ground_ref, first_ref, last_ref, sems):
    rows = ground_ref.shape[0]
    copies = []
    for side, (row, out_ref) in enumerate(((rows - 1, last_ref), (0, first_ref))):
        at = pl.ds(row, 1)
        for part in range(3):
            copies.append(pltpu.make_async_copy(state_ref.at[part, 0, at], out_ref.at[part], sems.at[side, part]))
        copies.append(pltpu.make_async_copy(ground_ref.at[at], out_ref.at[3], sems.at[side, 3]))
    for copy in copies:
        copy.start()
    for copy in copies:
        copy.wait()


def write_plan(zh, counts, slots, plan_ref, level_ref, sizes):
    total = counts.shape[1]
    square = (total, total)
    i = lax.broadcasted_iota(jnp.int32, square, 0)
    j = lax.broadcasted_iota(jnp.int32, square, 1)

    def over_lanes(values):
        return jnp.sum(values, axis=1, keepdims=True)

    def over_rows(values):
        return jnp.sum(values, axis=0, keepdims=True)

    def half(places):
        return jnp.bitwise_and(jnp.right_shift(places, 1), 1)

    def place(places):
        return 2 * jnp.right_shift(places, 2) + jnp.bitwise_and(places, 1)

    cumul = over_lanes(jnp.where(j <= i, counts, 0))
    ordered = over_rows((cumul <= j).astype(jnp.int32))
    ancestor = over_lanes(jnp.where(slots == i, ordered, 0))
    crossing = jnp.logical_and(ancestor == j, half(i) != half(j))
    needed = (over_rows(crossing.astype(jnp.int32)) > 0).astype(jnp.int32)
    needed_col = over_lanes(jnp.where(i == j, needed, 0))
    earlier = jnp.logical_and(i < j, half(i) == half(j))
    rank = over_rows(jnp.where(earlier, needed_col, 0))
    rank_col = over_lanes(jnp.where(i == j, rank, 0))
    mine = jnp.logical_and(half(i) == zh, jnp.logical_and(needed_col > 0, rank_col == j))
    plan_ref[0:1, :] = over_rows(jnp.where(mine, place(i), 0))
    rank_of = over_lanes(jnp.where(ancestor == j, rank, 0))
    source = jnp.where(half(ancestor) == zh, place(ancestor), total // 2 + rank_of)
    here = jnp.logical_and(half(i) == zh, place(i) == j)
    plan_ref[1:2, :] = over_rows(jnp.where(here, source, 0))
    lower = jnp.sum(jnp.where(half(j[0:1]) == 0, needed, 0))
    most = jnp.maximum(lower, jnp.sum(needed) - lower)
    level_ref[0] = sum((most > size).astype(jnp.int32) for size in sizes[:-1])


def step_kernel(
    zh_ref, state_ref, ground_ref, rain_hbm, counts_hbm, slots_hbm,
    out_ref, plan_smem, level_ref, rain_ref, counts_ref, slots_ref, plan_ref, sems, *, unroll, tail, sizes
):
    rows, width = ground_ref.shape
    copies = [
        pltpu.make_async_copy(counts_hbm, counts_ref, sems.at[0]),
        pltpu.make_async_copy(slots_hbm, slots_ref, sems.at[1]),
        pltpu.make_async_copy(rain_hbm, rain_ref, sems.at[2]),
    ]
    for copy in copies:
        copy.start()
    tiles = width // LANES
    shape = (rows, LANES)
    lane = lax.broadcasted_iota(jnp.int32, shape, 1)
    row = lax.broadcasted_iota(jnp.int32, shape, 0)
    first_lane, last_lane = lane == 0, lane == LANES - 1
    first_row, last_row = row == 0, row == rows - 1

    def columns(tile):
        start = tile * LANES
        return pl.ds(start if isinstance(tile, int) else pl.multiple_of(start, LANES), LANES)

    def load(tile):
        at = columns(tile)
        return state_ref[0, 0, :, at], state_ref[1, 0, :, at], state_ref[2, 0, :, at], ground_ref[:, at]

    def rolled(terms):
        return tuple(pltpu.roll(term, LANES - 1, 1) for term in terms)

    def mirrored(terms):
        depth, norm, tang, fnorm, ftang, slow, fast = terms
        return depth, -norm, tang, fnorm, -ftang, -fast, -slow

    def one(tile, carry, last=False):
        by_row, by_col, bed, cells_r, bed_r, flux_before, bed_before = carry
        depth, flow_a, flow_b = by_row[:3]
        if last:
            n_row, n_col, n_bed = by_row, by_col, bed
            n_rolled, n_bed_r = mirrored(by_col), bed
        else:
            n_depth, n_a, n_b, n_bed = load(tile + 1)
            n_row, n_col = both_ways(n_depth, n_a, n_b)
            n_rolled = rolled(n_col)
            n_bed_r = pltpu.roll(n_bed, LANES - 1, 1)
        right = tuple(jnp.where(last_lane, n, c) for n, c in zip(n_rolled, cells_r))
        bed_next = jnp.where(last_lane, n_bed_r, bed_r)
        flux = interface(by_col, right)
        flux_r = tuple(pltpu.roll(f, 1, 1) for f in flux)
        flux_left = tuple(jnp.where(first_lane, b, f) for b, f in zip(flux_before, flux_r))
        bed_rolled = pltpu.roll(bed, 1, 1)
        bed_left = jnp.where(first_lane, bed_before, bed_rolled)

        above = tuple(pltpu.roll(term, 1, 0) for term in by_row)
        inner = interface(above, by_row)
        inner = tuple(jnp.where(first_row, 0.0, f) for f in inner)
        below = tuple(pltpu.roll(f, rows - 1, 0) for f in inner)
        bed_up = jnp.where(first_row, 0.0, pltpu.roll(bed, 1, 0))
        bed_down = jnp.where(last_row, 0.0, pltpu.roll(bed, rows - 1, 0))

        pull = (0.5 * courant * gravity) * depth
        new_depth = depth - courant * ((below[0] - inner[0]) + (flux[0] - flux_left[0]))
        new_a = flow_a - courant * ((below[1] - inner[1]) + (flux[2] - flux_left[2])) - pull * (bed_down - bed_up)
        new_b = flow_b - courant * ((below[2] - inner[2]) + (flux[1] - flux_left[1])) - pull * (bed_next - bed_left)
        for part, value in enumerate((new_depth, new_a, new_b)):
            for top in range(rows // SUBLANES):
                out_ref[tile, top, part] = value[top * SUBLANES : (top + 1) * SUBLANES]
        return n_row, n_col, n_bed, n_rolled, n_bed_r, flux_r, bed_rolled

    depth, flow_a, flow_b, bed = load(0)
    by_row, by_col = both_ways(depth, flow_a, flow_b)
    edge = interface(mirrored(by_col), by_col)
    carry = (by_row, by_col, bed, rolled(by_col), pltpu.roll(bed, LANES - 1, 1), edge, bed)
    steps = (tiles - max(1, min(tail, tiles))) // unroll

    def some(i, carry):
        for k in range(unroll):
            carry = one(i * unroll + k, carry)
        return carry

    carry = lax.fori_loop(0, steps, some, carry)
    for copy in copies:
        copy.wait()
    write_plan(zh_ref[0], counts_ref[...], slots_ref[...], plan_ref, level_ref, sizes)
    to_scalars = pltpu.make_async_copy(plan_ref, plan_smem, sems.at[3])
    to_scalars.start()
    for tile in range(steps * unroll, tiles):
        carry = one(tile, carry, tile == tiles - 1)
    for tile in range(tiles):
        for top in range(rows // SUBLANES):
            at = slice(top * SUBLANES, (top + 1) * SUBLANES)
            out_ref[tile, top, 0] += rain_ref[0, at, columns(tile)]
    to_scalars.wait()


def edge_kernel(strip_ref, first_ref, last_ref, top_ref, low_ref, part_ref, out_ref, top_sc, low_sc, *, strips):
    strip = strip_ref[0]

    def fluxes(inside, outside, at_wall, upward):
        own = tuple(inside[i] for i in range(4))
        far = tuple(outside[i] for i in range(4))
        depth = jnp.where(at_wall, own[0], far[0])
        norm = jnp.where(at_wall, -own[1], far[1])
        tang = jnp.where(at_wall, own[2], far[2])
        bed = jnp.where(at_wall, own[3], far[3])
        mine = cell_terms(*own[:3])
        other = cell_terms(depth, norm, tang)
        flux = interface(other, mine) if upward else interface(mine, other)
        sign = courant if upward else -courant
        pull = (0.5 * courant * gravity) * own[0] * bed
        return (
            sign * flux[0],
            sign * flux[1] + (pull if upward else -pull),
            sign * flux[2],
        )

    for part, value in enumerate(fluxes(first_ref, top_ref, strip == 0, True)):
        top_sc[part] = value
    for part, value in enumerate(fluxes(last_ref, low_ref, strip == strips - 1, False)):
        low_sc[part] = value
    tiles = out_ref.shape[0]
    tops = out_ref.shape[1]
    out_ref[...] = part_ref[...]
    for tile in range(tiles):
        for part in range(3):
            out_ref[tile, 0, part, 0:1, :] = part_ref[tile, 0, part, 0:1, :] + top_sc[part, tile : tile + 1, :]
            out_ref[tile, tops - 1, part, SUBLANES - 1 : SUBLANES, :] = (
                part_ref[tile, tops - 1, part, SUBLANES - 1 : SUBLANES, :] + low_sc[part, tile : tile + 1, :]
            )


def outgoing_kernel(plan_ref, held_ref, out_ref):
    for k in range(out_ref.shape[0]):
        out_ref[k] = held_ref[plan_ref[0, k]]


def slots_kernel(plan_ref, held_ref, crossed_ref, out_ref):
    held, most = held_ref.shape[0], crossed_ref.shape[0]
    for slot in range(out_ref.shape[0]):
        code = plan_ref[1, slot]
        near = held_ref[jnp.minimum(code, held - 1)]
        far = crossed_ref[jnp.clip(code - held, 0, most - 1)]
        out_ref[slot] = jnp.where(code < held, near, far)


def place_kernel(tiles_ref, out_hbm, sems):
    tops, parts = tiles_ref.shape[1:3]
    copies = [
        pltpu.make_async_copy(tiles_ref.at[:, top, part], out_hbm.at[part, top], sems.at[part, top])
        for part in range(parts)
        for top in range(tops)
    ]
    for copy in copies:
        copy.start()
    for copy in copies:
        copy.wait()


def whole(count):
    return [pl.BlockSpec(memory_space=pltpu.VMEM)] * count


def params(moved):
    return dict(
        compiler_params=pltpu.CompilerParams(vmem_limit_bytes=16 * 1024 * 1024),
        cost_estimate=pl.CostEstimate(flops=moved * 40, bytes_accessed=moved, transcendentals=0),
    )


COLUMN = ("zh", "row")
UNROLL = 8
TAIL = 16
HBM = pl.BlockSpec(memory_space=pltpu.HBM)
SMEM = pl.BlockSpec(memory_space=pltpu.SMEM)


def packed_edges(state, ground):
    rows, width = ground.shape
    shape = pltpu.VMEM((4, 1, width), jnp.float32)
    return pl.pallas_call(
        pack_kernel,
        out_shape=(shape, shape),
        in_specs=[HBM, HBM],
        out_specs=whole(2),
        scratch_shapes=[pltpu.SemaphoreType.DMA((2, 4))],
        name="pack",
        **params(1 << 18),
    )(*in_hbm(state, ground))


def in_hbm(*arrays):
    return [pltpu.with_memory_space_constraint(array, pltpu.HBM) for array in arrays]


def partial_step(zh, state, rain, ground, counts, slot_map, sizes, unroll=UNROLL, tail=TAIL):
    rows, width = ground.shape
    tiles, tops = width // LANES, rows // SUBLANES
    row = (1, counts.shape[0])
    return pl.pallas_call(
        functools.partial(step_kernel, unroll=unroll, tail=tail, sizes=sizes),
        out_shape=(
            jax.ShapeDtypeStruct((tiles, tops, 3, SUBLANES, LANES), jnp.float32),
            pltpu.SMEM((2, row[1]), jnp.int32),
            pltpu.SMEM((1,), jnp.int32),
        ),
        in_specs=[SMEM] + whole(2) + [HBM] * 3,
        out_specs=whole(1) + [SMEM] * 2,
        scratch_shapes=[
            pltpu.VMEM(rain.shape, jnp.float32),
            pltpu.VMEM(row, jnp.int32),
            pltpu.VMEM(row, jnp.int32),
            pltpu.VMEM((2, row[1]), jnp.int32),
            pltpu.SemaphoreType.DMA((4,)),
        ],
        name="step",
        **params(8 << 20),
    )(zh, state, ground, *in_hbm(rain, counts.reshape(row), slot_map.reshape(row)))


def stepped_tiles(zh, state, rain, ground, counts, slot_map, sizes):
    rows, width = ground.shape
    tiles = width // LANES
    strips = lax.axis_size("row")
    first, last = packed_edges(state, ground)
    count = lax.axis_size(COLUMN)
    forward = [(i, (i + 1) % count) for i in range(count)]
    backward = [(target, source) for source, target in forward]
    top = lax.ppermute(last, COLUMN, forward)
    low = lax.ppermute(first, COLUMN, backward)
    partial, plan, level = partial_step(zh, state, rain, ground, counts, slot_map, sizes)
    strip = lax.axis_index("row").astype(jnp.int32).reshape(1)
    square = (4, tiles, LANES)
    block = pl.pallas_call(
        functools.partial(edge_kernel, strips=strips),
        out_shape=pltpu.VMEM(partial.shape, jnp.float32),
        in_specs=[SMEM] + whole(5),
        out_specs=whole(1)[0],
        scratch_shapes=[pltpu.VMEM((3, tiles, LANES), jnp.float32)] * 2,
        name="edges",
        **params(1 << 20),
    )(strip, first.reshape(square), last.reshape(square), top.reshape(square), low.reshape(square), partial)
    return block, plan, level


SWAP = [(0, 1), (1, 0)]


def blocks_for_slots(plan, block, most):
    held = lax.all_to_all(block, PLANE, split_axis=0, concat_axis=0, tiled=True)
    outgoing = pl.pallas_call(
        outgoing_kernel,
        out_shape=jax.ShapeDtypeStruct((most,) + held.shape[1:], jnp.float32),
        in_specs=[SMEM] + whole(1),
        out_specs=whole(1)[0],
        name="outgoing",
        **params(1 << 20),
    )(plan, held)
    crossed = lax.ppermute(outgoing, "zh", SWAP)
    return pl.pallas_call(
        slots_kernel,
        out_shape=jax.ShapeDtypeStruct(held.shape, jnp.float32),
        in_specs=[SMEM] + whole(2),
        out_specs=whole(1)[0],
        name="slots",
        **params(2 << 20),
    )(plan, held, crossed)


def placed_strip(block, rows, width):
    tiles, tops = block.shape[:2]
    placed = pl.pallas_call(
        place_kernel,
        out_shape=jax.ShapeDtypeStruct((3, tops, tiles, SUBLANES, LANES), jnp.float32),
        in_specs=whole(1),
        out_specs=HBM,
        scratch_shapes=[pltpu.SemaphoreType.DMA((3, tops))],
        name="place",
        **params(2 << 20),
    )(block)
    return placed.transpose(0, 1, 3, 2, 4).reshape(3, 1, rows, width)


PLANE = ("y", "x", "core")
SIZES = (8, 9, 10, 11, 12, 13, 14, 15, 16, 17, 18, 20, 24, 32)


def on_device(state, rain, ground, counts, slot_map):
    rows, width = ground.shape
    zh = lax.axis_index("zh").astype(jnp.int32).reshape(1)
    block, plan, level = stepped_tiles(zh, state, rain, ground, counts, slot_map, SIZES)
    shape = block.shape
    outgoing = block.reshape((lax.axis_size(PLANE), -1) + shape[2:])
    chosen = lax.switch(level[0], [functools.partial(blocks_for_slots, most=size) for size in SIZES], plan, outgoing)
    returned = lax.all_to_all(chosen, PLANE, split_axis=0, concat_axis=0, tiled=True)
    return placed_strip(returned.reshape(shape), rows, width)


def solution(mesh):
    fine = Mesh(mesh.devices.reshape(4, 4, 2, 2, 4), ("y", "x", "zh", "core", "row"))
    dom = ("y", "x", "zh", "core")
    placed = (P(None, dom, "row", None), P(dom, "row", None), P("row", None), P(), P())
    return jax.shard_map(
        on_device,
        mesh=fine,
        in_specs=placed,
        out_specs=P(None, dom, "row", None),
        check_vma=False,
    )
```

```python
import functools

import jax
import jax.numpy as jnp
from jax import lax
from jax.experimental import pallas as pl
from jax.experimental.pallas import tpu as pltpu
from jax.sharding import Mesh, PartitionSpec as P

gravity = 9.81
courant = 0.04
LANES = 128
SUBLANES = 8


def cell_terms(depth, norm, tang):
    vel = norm / depth
    cel = jnp.sqrt(gravity * depth)
    press = 0.5 * gravity * depth * depth
    return depth, norm, tang, norm * vel + press, tang * vel, vel - cel, vel + cel


def interface(left, right):
    depth_l, norm_l, tang_l, fnorm_l, ftang_l, slow_l, fast_l = left
    depth_r, norm_r, tang_r, fnorm_r, ftang_r, slow_r, fast_r = right
    lower = jnp.minimum(jnp.minimum(slow_l, slow_r), 0.0)
    upper = jnp.maximum(jnp.maximum(fast_l, fast_r), 0.0)
    scale = 1.0 / (upper - lower)
    both = upper * lower
    return (
        (upper * norm_l - lower * norm_r + both * (depth_r - depth_l)) * scale,
        (upper * fnorm_l - lower * fnorm_r + both * (norm_r - norm_l)) * scale,
        (upper * ftang_l - lower * ftang_r + both * (tang_r - tang_l)) * scale,
    )


def both_ways(depth, flow_a, flow_b):
    inverse = 1.0 / depth
    cel = jnp.sqrt(gravity * depth)
    press = (0.5 * gravity) * depth * depth
    vel_a = flow_a * inverse
    vel_b = flow_b * inverse
    cross = flow_a * vel_b
    by_row = (depth, flow_a, flow_b, flow_a * vel_a + press, cross, vel_a - cel, vel_a + cel)
    by_col = (depth, flow_b, flow_a, flow_b * vel_b + press, cross, vel_b - cel, vel_b + cel)
    return by_row, by_col


def pack_kernel(state_ref, ground_ref, first_ref, last_ref, sems):
    tops = ground_ref.shape[0]
    copies = []
    for side, (top, row, out_ref) in enumerate(((tops - 1, SUBLANES - 1, last_ref), (0, 0, first_ref))):
        copies.append(pltpu.make_async_copy(state_ref.at[:, top, :, row], out_ref.at[0:3], sems.at[side, 0]))
        copies.append(pltpu.make_async_copy(ground_ref.at[top, :, row], out_ref.at[3], sems.at[side, 1]))
    for copy in copies:
        copy.start()
    for copy in copies:
        copy.wait()


def write_plan(zh, counts, slots, plan_ref, level_ref, sizes):
    total = counts.shape[1]
    square = (total, total)
    i = lax.broadcasted_iota(jnp.int32, square, 0)
    j = lax.broadcasted_iota(jnp.int32, square, 1)

    def over_lanes(values):
        return jnp.sum(values, axis=1, keepdims=True)

    def over_rows(values):
        return jnp.sum(values, axis=0, keepdims=True)

    def half(places):
        return jnp.bitwise_and(jnp.right_shift(places, 1), 1)

    def place(places):
        return 2 * jnp.right_shift(places, 2) + jnp.bitwise_and(places, 1)

    cumul = over_lanes(jnp.where(j <= i, counts, 0))
    ordered = over_rows((cumul <= j).astype(jnp.int32))
    ancestor = over_lanes(jnp.where(slots == i, ordered, 0))
    crossing = jnp.logical_and(ancestor == j, half(i) != half(j))
    needed = (over_rows(crossing.astype(jnp.int32)) > 0).astype(jnp.int32)
    needed_col = over_lanes(jnp.where(i == j, needed, 0))
    earlier = jnp.logical_and(i < j, half(i) == half(j))
    rank = over_rows(jnp.where(earlier, needed_col, 0))
    rank_col = over_lanes(jnp.where(i == j, rank, 0))
    mine = jnp.logical_and(half(i) == zh, jnp.logical_and(needed_col > 0, rank_col == j))
    plan_ref[0:1, :] = over_rows(jnp.where(mine, place(i), 0))
    rank_of = over_lanes(jnp.where(ancestor == j, rank, 0))
    source = jnp.where(half(ancestor) == zh, place(ancestor), total // 2 + rank_of)
    here = jnp.logical_and(half(i) == zh, place(i) == j)
    plan_ref[1:2, :] = over_rows(jnp.where(here, source, 0))
    lower = jnp.sum(jnp.where(half(j[0:1]) == 0, needed, 0))
    most = jnp.maximum(lower, jnp.sum(needed) - lower)
    level_ref[0] = sum((most > size).astype(jnp.int32) for size in sizes[:-1])


def step_kernel(
    zh_ref, state_ref, ground_ref, rain_hbm, counts_hbm, slots_hbm,
    out_ref, plan_smem, level_ref, rain_ref, counts_ref, slots_ref, plan_ref, sems, *, unroll, tail, sizes
):
    rows, width = ground_ref.shape
    copies = [
        pltpu.make_async_copy(counts_hbm, counts_ref, sems.at[0]),
        pltpu.make_async_copy(slots_hbm, slots_ref, sems.at[1]),
        pltpu.make_async_copy(rain_hbm, rain_ref, sems.at[2]),
    ]
    for copy in copies:
        copy.start()
    tiles = width // LANES
    shape = (rows, LANES)
    lane = lax.broadcasted_iota(jnp.int32, shape, 1)
    row = lax.broadcasted_iota(jnp.int32, shape, 0)
    first_lane, last_lane = lane == 0, lane == LANES - 1
    first_row, last_row = row == 0, row == rows - 1

    def columns(tile):
        start = tile * LANES
        return pl.ds(start if isinstance(tile, int) else pl.multiple_of(start, LANES), LANES)

    def load(tile):
        at = columns(tile)
        return state_ref[0, 0, :, at], state_ref[1, 0, :, at], state_ref[2, 0, :, at], ground_ref[:, at]

    def rolled(terms):
        return tuple(pltpu.roll(term, LANES - 1, 1) for term in terms)

    def mirrored(terms):
        depth, norm, tang, fnorm, ftang, slow, fast = terms
        return depth, -norm, tang, fnorm, -ftang, -fast, -slow

    def one(tile, carry, last=False):
        by_row, by_col, bed, cells_r, bed_r, flux_before, bed_before = carry
        depth, flow_a, flow_b = by_row[:3]
        if last:
            n_row, n_col, n_bed = by_row, by_col, bed
            n_rolled, n_bed_r = mirrored(by_col), bed
        else:
            n_depth, n_a, n_b, n_bed = load(tile + 1)
            n_row, n_col = both_ways(n_depth, n_a, n_b)
            n_rolled = rolled(n_col)
            n_bed_r = pltpu.roll(n_bed, LANES - 1, 1)
        right = tuple(jnp.where(last_lane, n, c) for n, c in zip(n_rolled, cells_r))
        bed_next = jnp.where(last_lane, n_bed_r, bed_r)
        flux = interface(by_col, right)
        flux_r = tuple(pltpu.roll(f, 1, 1) for f in flux)
        flux_left = tuple(jnp.where(first_lane, b, f) for b, f in zip(flux_before, flux_r))
        bed_rolled = pltpu.roll(bed, 1, 1)
        bed_left = jnp.where(first_lane, bed_before, bed_rolled)

        above = tuple(pltpu.roll(term, 1, 0) for term in by_row)
        inner = interface(above, by_row)
        inner = tuple(jnp.where(first_row, 0.0, f) for f in inner)
        below = tuple(pltpu.roll(f, rows - 1, 0) for f in inner)
        bed_up = jnp.where(first_row, 0.0, pltpu.roll(bed, 1, 0))
        bed_down = jnp.where(last_row, 0.0, pltpu.roll(bed, rows - 1, 0))

        pull = (0.5 * courant * gravity) * depth
        new_depth = depth - courant * ((below[0] - inner[0]) + (flux[0] - flux_left[0]))
        new_a = flow_a - courant * ((below[1] - inner[1]) + (flux[2] - flux_left[2])) - pull * (bed_down - bed_up)
        new_b = flow_b - courant * ((below[2] - inner[2]) + (flux[1] - flux_left[1])) - pull * (bed_next - bed_left)
        for part, value in enumerate((new_depth, new_a, new_b)):
            for top in range(rows // SUBLANES):
                out_ref[tile, top, part] = value[top * SUBLANES : (top + 1) * SUBLANES]
        return n_row, n_col, n_bed, n_rolled, n_bed_r, flux_r, bed_rolled

    depth, flow_a, flow_b, bed = load(0)
    by_row, by_col = both_ways(depth, flow_a, flow_b)
    edge = interface(mirrored(by_col), by_col)
    carry = (by_row, by_col, bed, rolled(by_col), pltpu.roll(bed, LANES - 1, 1), edge, bed)
    steps = (tiles - max(1, min(tail, tiles))) // unroll

    def some(i, carry):
        for k in range(unroll):
            carry = one(i * unroll + k, carry)
        return carry

    carry = lax.fori_loop(0, steps, some, carry)
    for copy in copies:
        copy.wait()
    write_plan(zh_ref[0], counts_ref[...], slots_ref[...], plan_ref, level_ref, sizes)
    to_scalars = pltpu.make_async_copy(plan_ref, plan_smem, sems.at[3])
    to_scalars.start()
    for tile in range(steps * unroll, tiles):
        carry = one(tile, carry, tile == tiles - 1)
    for tile in range(tiles):
        for top in range(rows // SUBLANES):
            at = slice(top * SUBLANES, (top + 1) * SUBLANES)
            out_ref[tile, top, 0] += rain_ref[0, at, columns(tile)]
    to_scalars.wait()


def edge_kernel(strip_ref, first_ref, last_ref, top_ref, low_ref, part_ref, out_ref, top_sc, low_sc, *, strips):
    strip = strip_ref[0]

    def fluxes(inside, outside, at_wall, upward):
        own = tuple(inside[i] for i in range(4))
        far = tuple(outside[i] for i in range(4))
        depth = jnp.where(at_wall, own[0], far[0])
        norm = jnp.where(at_wall, -own[1], far[1])
        tang = jnp.where(at_wall, own[2], far[2])
        bed = jnp.where(at_wall, own[3], far[3])
        mine = cell_terms(*own[:3])
        other = cell_terms(depth, norm, tang)
        flux = interface(other, mine) if upward else interface(mine, other)
        sign = courant if upward else -courant
        pull = (0.5 * courant * gravity) * own[0] * bed
        return (
            sign * flux[0],
            sign * flux[1] + (pull if upward else -pull),
            sign * flux[2],
        )

    for part, value in enumerate(fluxes(first_ref, top_ref, strip == 0, True)):
        top_sc[part] = value
    for part, value in enumerate(fluxes(last_ref, low_ref, strip == strips - 1, False)):
        low_sc[part] = value
    tiles = out_ref.shape[0]
    tops = out_ref.shape[1]
    out_ref[...] = part_ref[...]
    for tile in range(tiles):
        for part in range(3):
            out_ref[tile, 0, part, 0:1, :] = part_ref[tile, 0, part, 0:1, :] + top_sc[part, tile : tile + 1, :]
            out_ref[tile, tops - 1, part, SUBLANES - 1 : SUBLANES, :] = (
                part_ref[tile, tops - 1, part, SUBLANES - 1 : SUBLANES, :] + low_sc[part, tile : tile + 1, :]
            )


def outgoing_kernel(plan_ref, held_ref, out_ref):
    for k in range(out_ref.shape[0]):
        out_ref[k] = held_ref[plan_ref[0, k]]


def slots_kernel(plan_ref, held_ref, crossed_ref, out_ref):
    held, most = held_ref.shape[0], crossed_ref.shape[0]
    for slot in range(out_ref.shape[0]):
        code = plan_ref[1, slot]
        near = held_ref[jnp.minimum(code, held - 1)]
        far = crossed_ref[jnp.clip(code - held, 0, most - 1)]
        out_ref[slot] = jnp.where(code < held, near, far)


def place_kernel(tiles_ref, out_hbm, sems):
    tops, parts = tiles_ref.shape[1:3]
    copies = [
        pltpu.make_async_copy(tiles_ref.at[:, top, part], out_hbm.at[part, top], sems.at[part, top])
        for part in range(parts)
        for top in range(tops)
    ]
    for copy in copies:
        copy.start()
    for copy in copies:
        copy.wait()


def whole(count):
    return [pl.BlockSpec(memory_space=pltpu.VMEM)] * count


def params(moved):
    return dict(
        compiler_params=pltpu.CompilerParams(vmem_limit_bytes=16 * 1024 * 1024),
        cost_estimate=pl.CostEstimate(flops=moved * 40, bytes_accessed=moved, transcendentals=0),
    )


COLUMN = ("zh", "row")
UNROLL = 8
TAIL = 16
HBM = pl.BlockSpec(memory_space=pltpu.HBM)
SMEM = pl.BlockSpec(memory_space=pltpu.SMEM)


def packed_edges(state, ground):
    rows, width = ground.shape
    tops, tiles = rows // SUBLANES, width // LANES
    shape = pltpu.VMEM((4, tiles, LANES), jnp.float32)
    state = state.reshape(3, tops, SUBLANES, tiles, LANES).transpose(0, 1, 3, 2, 4)
    ground = ground.reshape(tops, SUBLANES, tiles, LANES).transpose(0, 2, 1, 3)
    return pl.pallas_call(
        pack_kernel,
        out_shape=(shape, shape),
        in_specs=[HBM, HBM],
        out_specs=whole(2),
        scratch_shapes=[pltpu.SemaphoreType.DMA((2, 2))],
        name="pack",
        **params(1 << 18),
    )(*in_hbm(state, ground))


def in_hbm(*arrays):
    return [pltpu.with_memory_space_constraint(array, pltpu.HBM) for array in arrays]


def partial_step(zh, state, rain, ground, counts, slot_map, sizes, unroll=UNROLL, tail=TAIL):
    rows, width = ground.shape
    tiles, tops = width // LANES, rows // SUBLANES
    row = (1, counts.shape[0])
    return pl.pallas_call(
        functools.partial(step_kernel, unroll=unroll, tail=tail, sizes=sizes),
        out_shape=(
            jax.ShapeDtypeStruct((tiles, tops, 3, SUBLANES, LANES), jnp.float32),
            pltpu.SMEM((2, row[1]), jnp.int32),
            pltpu.SMEM((1,), jnp.int32),
        ),
        in_specs=[SMEM] + whole(2) + [HBM] * 3,
        out_specs=whole(1) + [SMEM] * 2,
        scratch_shapes=[
            pltpu.VMEM(rain.shape, jnp.float32),
            pltpu.VMEM(row, jnp.int32),
            pltpu.VMEM(row, jnp.int32),
            pltpu.VMEM((2, row[1]), jnp.int32),
            pltpu.SemaphoreType.DMA((4,)),
        ],
        name="step",
        **params(8 << 20),
    )(zh, state, ground, *in_hbm(rain, counts.reshape(row), slot_map.reshape(row)))


def stepped_tiles(zh, state, rain, ground, counts, slot_map, sizes):
    rows, width = ground.shape
    tiles = width // LANES
    strips = lax.axis_size("row")
    first, last = packed_edges(state, ground)
    count = lax.axis_size(COLUMN)
    forward = [(i, (i + 1) % count) for i in range(count)]
    backward = [(target, source) for source, target in forward]
    top = lax.ppermute(last, COLUMN, forward)
    low = lax.ppermute(first, COLUMN, backward)
    partial, plan, level = partial_step(zh, state, rain, ground, counts, slot_map, sizes)
    strip = lax.axis_index("row").astype(jnp.int32).reshape(1)
    square = (4, tiles, LANES)
    block = pl.pallas_call(
        functools.partial(edge_kernel, strips=strips),
        out_shape=pltpu.VMEM(partial.shape, jnp.float32),
        in_specs=[SMEM] + whole(5),
        out_specs=whole(1)[0],
        scratch_shapes=[pltpu.VMEM((3, tiles, LANES), jnp.float32)] * 2,
        name="edges",
        **params(1 << 20),
    )(strip, first.reshape(square), last.reshape(square), top.reshape(square), low.reshape(square), partial)
    return block, plan, level


SWAP = [(0, 1), (1, 0)]


def blocks_for_slots(plan, block, most):
    held = lax.all_to_all(block, PLANE, split_axis=0, concat_axis=0, tiled=True)
    outgoing = pl.pallas_call(
        outgoing_kernel,
        out_shape=jax.ShapeDtypeStruct((most,) + held.shape[1:], jnp.float32),
        in_specs=[SMEM] + whole(1),
        out_specs=whole(1)[0],
        name="outgoing",
        **params(1 << 20),
    )(plan, held)
    crossed = lax.ppermute(outgoing, "zh", SWAP)
    return pl.pallas_call(
        slots_kernel,
        out_shape=jax.ShapeDtypeStruct(held.shape, jnp.float32),
        in_specs=[SMEM] + whole(2),
        out_specs=whole(1)[0],
        name="slots",
        **params(2 << 20),
    )(plan, held, crossed)


def placed_strip(block, rows, width):
    tiles, tops = block.shape[:2]
    placed = pl.pallas_call(
        place_kernel,
        out_shape=jax.ShapeDtypeStruct((3, tops, tiles, SUBLANES, LANES), jnp.float32),
        in_specs=whole(1),
        out_specs=HBM,
        scratch_shapes=[pltpu.SemaphoreType.DMA((3, tops))],
        name="place",
        **params(2 << 20),
    )(block)
    return placed.transpose(0, 1, 3, 2, 4).reshape(3, 1, rows, width)


PLANE = ("y", "x", "core")
SIZES = (8, 9, 10, 11, 12, 13, 14, 15, 16, 17, 18, 20, 24, 32)


def on_device(state, rain, ground, counts, slot_map):
    rows, width = ground.shape
    zh = lax.axis_index("zh").astype(jnp.int32).reshape(1)
    block, plan, level = stepped_tiles(zh, state, rain, ground, counts, slot_map, SIZES)
    shape = block.shape
    outgoing = block.reshape((lax.axis_size(PLANE), -1) + shape[2:])
    chosen = lax.switch(level[0], [functools.partial(blocks_for_slots, most=size) for size in SIZES], plan, outgoing)
    returned = lax.all_to_all(chosen, PLANE, split_axis=0, concat_axis=0, tiled=True)
    return placed_strip(returned.reshape(shape), rows, width)


def solution(mesh):
    fine = Mesh(mesh.devices.reshape(4, 4, 2, 2, 4), ("y", "x", "zh", "core", "row"))
    dom = ("y", "x", "zh", "core")
    placed = (P(None, dom, "row", None), P(dom, "row", None), P("row", None), P(), P())
    return jax.shard_map(
        on_device,
        mesh=fine,
        in_specs=placed,
        out_specs=P(None, dom, "row", None),
        check_vma=False,
    )
```

```python
import functools

import jax
import jax.numpy as jnp
from jax import lax
from jax.experimental import pallas as pl
from jax.experimental.pallas import tpu as pltpu
from jax.sharding import Mesh, PartitionSpec as P

gravity = 9.81
courant = 0.04
LANES = 128
SUBLANES = 8


def cell_terms(depth, norm, tang):
    vel = norm / depth
    cel = jnp.sqrt(gravity * depth)
    press = 0.5 * gravity * depth * depth
    return depth, norm, tang, norm * vel + press, tang * vel, vel - cel, vel + cel


def interface(left, right):
    depth_l, norm_l, tang_l, fnorm_l, ftang_l, slow_l, fast_l = left
    depth_r, norm_r, tang_r, fnorm_r, ftang_r, slow_r, fast_r = right
    lower = jnp.minimum(jnp.minimum(slow_l, slow_r), 0.0)
    upper = jnp.maximum(jnp.maximum(fast_l, fast_r), 0.0)
    scale = 1.0 / (upper - lower)
    both = upper * lower
    return (
        (upper * norm_l - lower * norm_r + both * (depth_r - depth_l)) * scale,
        (upper * fnorm_l - lower * fnorm_r + both * (norm_r - norm_l)) * scale,
        (upper * ftang_l - lower * ftang_r + both * (tang_r - tang_l)) * scale,
    )


def both_ways(depth, flow_a, flow_b):
    inverse = 1.0 / depth
    cel = jnp.sqrt(gravity * depth)
    press = (0.5 * gravity) * depth * depth
    vel_a = flow_a * inverse
    vel_b = flow_b * inverse
    cross = flow_a * vel_b
    by_row = (depth, flow_a, flow_b, flow_a * vel_a + press, cross, vel_a - cel, vel_a + cel)
    by_col = (depth, flow_b, flow_a, flow_b * vel_b + press, cross, vel_b - cel, vel_b + cel)
    return by_row, by_col


def pack_kernel(state_ref, ground_ref, first_ref, last_ref, sems):
    tops = ground_ref.shape[0]
    copies = []
    for side, (top, row, out_ref) in enumerate(((tops - 1, SUBLANES - 1, last_ref), (0, 0, first_ref))):
        copies.append(pltpu.make_async_copy(state_ref.at[:, top, :, row], out_ref.at[0:3], sems.at[side, 0]))
        copies.append(pltpu.make_async_copy(ground_ref.at[top, :, row], out_ref.at[3], sems.at[side, 1]))
    for copy in copies:
        copy.start()
    for copy in copies:
        copy.wait()


def write_plan(zh, counts, slots, plan_ref, level_ref, sizes):
    total = counts.shape[1]
    square = (total, total)
    i = lax.broadcasted_iota(jnp.int32, square, 0)
    j = lax.broadcasted_iota(jnp.int32, square, 1)

    def over_lanes(values):
        return jnp.sum(values, axis=1, keepdims=True)

    def over_rows(values):
        return jnp.sum(values, axis=0, keepdims=True)

    def half(places):
        return jnp.bitwise_and(jnp.right_shift(places, 1), 1)

    def place(places):
        return 2 * jnp.right_shift(places, 2) + jnp.bitwise_and(places, 1)

    cumul = over_lanes(jnp.where(j <= i, counts, 0))
    ordered = over_rows((cumul <= j).astype(jnp.int32))
    ancestor = over_lanes(jnp.where(slots == i, ordered, 0))
    crossing = jnp.logical_and(ancestor == j, half(i) != half(j))
    needed = (over_rows(crossing.astype(jnp.int32)) > 0).astype(jnp.int32)
    needed_col = over_lanes(jnp.where(i == j, needed, 0))
    earlier = jnp.logical_and(i < j, half(i) == half(j))
    rank = over_rows(jnp.where(earlier, needed_col, 0))
    rank_col = over_lanes(jnp.where(i == j, rank, 0))
    mine = jnp.logical_and(half(i) == zh, jnp.logical_and(needed_col > 0, rank_col == j))
    plan_ref[0:1, :] = over_rows(jnp.where(mine, place(i), 0))
    rank_of = over_lanes(jnp.where(ancestor == j, rank, 0))
    source = jnp.where(half(ancestor) == zh, place(ancestor), total // 2 + rank_of)
    here = jnp.logical_and(half(i) == zh, place(i) == j)
    plan_ref[1:2, :] = over_rows(jnp.where(here, source, 0))
    lower = jnp.sum(jnp.where(half(j[0:1]) == 0, needed, 0))
    most = jnp.maximum(lower, jnp.sum(needed) - lower)
    level_ref[0] = sum((most > size).astype(jnp.int32) for size in sizes[:-1])


def step_kernel(
    zh_ref, state_ref, ground_ref, rain_hbm, counts_hbm, slots_hbm,
    out_ref, plan_smem, level_ref, rain_ref, counts_ref, slots_ref, plan_ref, sems, *, unroll, tail, sizes
):
    rows, width = ground_ref.shape
    copies = [
        pltpu.make_async_copy(counts_hbm, counts_ref, sems.at[0]),
        pltpu.make_async_copy(slots_hbm, slots_ref, sems.at[1]),
        pltpu.make_async_copy(rain_hbm, rain_ref, sems.at[2]),
    ]
    for copy in copies:
        copy.start()
    tiles = width // LANES
    shape = (rows, LANES)
    lane = lax.broadcasted_iota(jnp.int32, shape, 1)
    row = lax.broadcasted_iota(jnp.int32, shape, 0)
    first_lane, last_lane = lane == 0, lane == LANES - 1
    first_row, last_row = row == 0, row == rows - 1

    def columns(tile):
        start = tile * LANES
        return pl.ds(start if isinstance(tile, int) else pl.multiple_of(start, LANES), LANES)

    def load(tile):
        at = columns(tile)
        return state_ref[0, 0, :, at], state_ref[1, 0, :, at], state_ref[2, 0, :, at], ground_ref[:, at]

    def rolled(terms):
        return tuple(pltpu.roll(term, LANES - 1, 1) for term in terms)

    def mirrored(terms):
        depth, norm, tang, fnorm, ftang, slow, fast = terms
        return depth, -norm, tang, fnorm, -ftang, -fast, -slow

    def one(tile, carry, last=False):
        by_row, by_col, bed, cells_r, bed_r, flux_before, bed_before = carry
        depth, flow_a, flow_b = by_row[:3]
        if last:
            n_row, n_col, n_bed = by_row, by_col, bed
            n_rolled, n_bed_r = mirrored(by_col), bed
        else:
            n_depth, n_a, n_b, n_bed = load(tile + 1)
            n_row, n_col = both_ways(n_depth, n_a, n_b)
            n_rolled = rolled(n_col)
            n_bed_r = pltpu.roll(n_bed, LANES - 1, 1)
        right = tuple(jnp.where(last_lane, n, c) for n, c in zip(n_rolled, cells_r))
        bed_next = jnp.where(last_lane, n_bed_r, bed_r)
        flux = interface(by_col, right)
        flux_r = tuple(pltpu.roll(f, 1, 1) for f in flux)
        flux_left = tuple(jnp.where(first_lane, b, f) for b, f in zip(flux_before, flux_r))
        bed_rolled = pltpu.roll(bed, 1, 1)
        bed_left = jnp.where(first_lane, bed_before, bed_rolled)

        above = tuple(pltpu.roll(term, 1, 0) for term in by_row)
        inner = interface(above, by_row)
        inner = tuple(jnp.where(first_row, 0.0, f) for f in inner)
        below = tuple(pltpu.roll(f, rows - 1, 0) for f in inner)
        bed_up = jnp.where(first_row, 0.0, pltpu.roll(bed, 1, 0))
        bed_down = jnp.where(last_row, 0.0, pltpu.roll(bed, rows - 1, 0))

        pull = (0.5 * courant * gravity) * depth
        new_depth = depth - courant * ((below[0] - inner[0]) + (flux[0] - flux_left[0]))
        new_a = flow_a - courant * ((below[1] - inner[1]) + (flux[2] - flux_left[2])) - pull * (bed_down - bed_up)
        new_b = flow_b - courant * ((below[2] - inner[2]) + (flux[1] - flux_left[1])) - pull * (bed_next - bed_left)
        for part, value in enumerate((new_depth, new_a, new_b)):
            for top in range(rows // SUBLANES):
                out_ref[tile, top, part] = value[top * SUBLANES : (top + 1) * SUBLANES]
        return n_row, n_col, n_bed, n_rolled, n_bed_r, flux_r, bed_rolled

    depth, flow_a, flow_b, bed = load(0)
    by_row, by_col = both_ways(depth, flow_a, flow_b)
    edge = interface(mirrored(by_col), by_col)
    carry = (by_row, by_col, bed, rolled(by_col), pltpu.roll(bed, LANES - 1, 1), edge, bed)
    steps = (tiles - max(1, min(tail, tiles))) // unroll

    def some(i, carry):
        for k in range(unroll):
            carry = one(i * unroll + k, carry)
        return carry

    carry = lax.fori_loop(0, steps, some, carry)
    for copy in copies:
        copy.wait()
    write_plan(zh_ref[0], counts_ref[...], slots_ref[...], plan_ref, level_ref, sizes)
    to_scalars = pltpu.make_async_copy(plan_ref, plan_smem, sems.at[3])
    to_scalars.start()
    for tile in range(steps * unroll, tiles):
        carry = one(tile, carry, tile == tiles - 1)
    for tile in range(tiles):
        for top in range(rows // SUBLANES):
            at = slice(top * SUBLANES, (top + 1) * SUBLANES)
            out_ref[tile, top, 0] += rain_ref[0, at, columns(tile)]
    to_scalars.wait()


def edge_kernel(strip_ref, first_ref, last_ref, top_ref, low_ref, part_ref, out_ref, top_sc, low_sc, *, strips):
    strip = strip_ref[0]

    def fluxes(inside, outside, at_wall, upward):
        own = tuple(inside[i] for i in range(4))
        far = tuple(outside[i] for i in range(4))
        depth = jnp.where(at_wall, own[0], far[0])
        norm = jnp.where(at_wall, -own[1], far[1])
        tang = jnp.where(at_wall, own[2], far[2])
        bed = jnp.where(at_wall, own[3], far[3])
        mine = cell_terms(*own[:3])
        other = cell_terms(depth, norm, tang)
        flux = interface(other, mine) if upward else interface(mine, other)
        sign = courant if upward else -courant
        pull = (0.5 * courant * gravity) * own[0] * bed
        return (
            sign * flux[0],
            sign * flux[1] + (pull if upward else -pull),
            sign * flux[2],
        )

    for part, value in enumerate(fluxes(first_ref, top_ref, strip == 0, True)):
        top_sc[part] = value
    for part, value in enumerate(fluxes(last_ref, low_ref, strip == strips - 1, False)):
        low_sc[part] = value
    tiles = out_ref.shape[0]
    tops = out_ref.shape[1]
    out_ref[...] = part_ref[...]
    for tile in range(tiles):
        for part in range(3):
            out_ref[tile, 0, part, 0:1, :] = part_ref[tile, 0, part, 0:1, :] + top_sc[part, tile : tile + 1, :]
            out_ref[tile, tops - 1, part, SUBLANES - 1 : SUBLANES, :] = (
                part_ref[tile, tops - 1, part, SUBLANES - 1 : SUBLANES, :] + low_sc[part, tile : tile + 1, :]
            )


def outgoing_kernel(plan_ref, held_ref, out_ref):
    for k in range(out_ref.shape[0]):
        out_ref[k] = held_ref[plan_ref[0, k]]


def slots_kernel(plan_ref, held_ref, crossed_ref, out_ref):
    held, most = held_ref.shape[0], crossed_ref.shape[0]
    for slot in range(out_ref.shape[0]):
        code = plan_ref[1, slot]
        near = held_ref[jnp.minimum(code, held - 1)]
        far = crossed_ref[jnp.clip(code - held, 0, most - 1)]
        out_ref[slot] = jnp.where(code < held, near, far)


def place_kernel(tiles_ref, out_hbm, sems):
    tops, parts = tiles_ref.shape[1:3]
    copies = [
        pltpu.make_async_copy(tiles_ref.at[:, top, part], out_hbm.at[part, top], sems.at[part, top])
        for part in range(parts)
        for top in range(tops)
    ]
    for copy in copies:
        copy.start()
    for copy in copies:
        copy.wait()


def whole(count):
    return [pl.BlockSpec(memory_space=pltpu.VMEM)] * count


def params(moved):
    return dict(
        compiler_params=pltpu.CompilerParams(vmem_limit_bytes=16 * 1024 * 1024),
        cost_estimate=pl.CostEstimate(flops=moved * 40, bytes_accessed=moved, transcendentals=0),
    )


COLUMN = ("zh", "row")
UNROLL = 8
TAIL = 16
HBM = pl.BlockSpec(memory_space=pltpu.HBM)
SMEM = pl.BlockSpec(memory_space=pltpu.SMEM)


def packed_edges(state, ground):
    rows, width = ground.shape
    tops, tiles = rows // SUBLANES, width // LANES
    shape = pltpu.VMEM((4, tiles, LANES), jnp.float32)
    state = state.reshape(3, tops, SUBLANES, tiles, LANES).transpose(0, 1, 3, 2, 4)
    ground = ground.reshape(tops, SUBLANES, tiles, LANES).transpose(0, 2, 1, 3)
    return pl.pallas_call(
        pack_kernel,
        out_shape=(shape, shape),
        in_specs=[HBM, HBM],
        out_specs=whole(2),
        scratch_shapes=[pltpu.SemaphoreType.DMA((2, 2))],
        name="pack",
        **params(1 << 18),
    )(*in_hbm(state, ground))


def in_hbm(*arrays):
    return [pltpu.with_memory_space_constraint(array, pltpu.HBM) for array in arrays]


def partial_step(zh, state, rain, ground, counts, slot_map, sizes, unroll=UNROLL, tail=TAIL):
    rows, width = ground.shape
    tiles, tops = width // LANES, rows // SUBLANES
    row = (1, counts.shape[0])
    return pl.pallas_call(
        functools.partial(step_kernel, unroll=unroll, tail=tail, sizes=sizes),
        out_shape=(
            jax.ShapeDtypeStruct((tiles, tops, 3, SUBLANES, LANES), jnp.float32),
            pltpu.SMEM((2, row[1]), jnp.int32),
            pltpu.SMEM((1,), jnp.int32),
        ),
        in_specs=[SMEM] + whole(2) + [HBM] * 3,
        out_specs=whole(1) + [SMEM] * 2,
        scratch_shapes=[
            pltpu.VMEM(rain.shape, jnp.float32),
            pltpu.VMEM(row, jnp.int32),
            pltpu.VMEM(row, jnp.int32),
            pltpu.VMEM((2, row[1]), jnp.int32),
            pltpu.SemaphoreType.DMA((4,)),
        ],
        name="step",
        **params(8 << 20),
    )(zh, state, ground, *in_hbm(rain, counts.reshape(row), slot_map.reshape(row)))


def stepped_tiles(zh, state, rain, ground, counts, slot_map, sizes):
    rows, width = ground.shape
    tiles = width // LANES
    strips = lax.axis_size("row")
    first, last = packed_edges(state, ground)
    count = lax.axis_size(COLUMN)
    forward = [(i, (i + 1) % count) for i in range(count)]
    strips_back = [(i, (i + strips - 1) % strips) for i in range(strips)]
    low = lax.ppermute(first, "row", strips_back)
    top = lax.ppermute(last, COLUMN, forward)
    partial, plan, level = partial_step(zh, state, rain, ground, counts, slot_map, sizes)
    strip = lax.axis_index("row").astype(jnp.int32).reshape(1)
    square = (4, tiles, LANES)
    block = pl.pallas_call(
        functools.partial(edge_kernel, strips=strips),
        out_shape=pltpu.VMEM(partial.shape, jnp.float32),
        in_specs=[SMEM] + whole(5),
        out_specs=whole(1)[0],
        scratch_shapes=[pltpu.VMEM((3, tiles, LANES), jnp.float32)] * 2,
        name="edges",
        **params(1 << 20),
    )(strip, first.reshape(square), last.reshape(square), top.reshape(square), low.reshape(square), partial)
    return block, plan, level


SWAP = [(0, 1), (1, 0)]


def blocks_for_slots(plan, block, most):
    held = lax.all_to_all(block, PLANE, split_axis=0, concat_axis=0, tiled=True)
    outgoing = pl.pallas_call(
        outgoing_kernel,
        out_shape=jax.ShapeDtypeStruct((most,) + held.shape[1:], jnp.float32),
        in_specs=[SMEM] + whole(1),
        out_specs=whole(1)[0],
        name="outgoing",
        **params(1 << 20),
    )(plan, held)
    crossed = lax.ppermute(outgoing, "zh", SWAP)
    return pl.pallas_call(
        slots_kernel,
        out_shape=jax.ShapeDtypeStruct(held.shape, jnp.float32),
        in_specs=[SMEM] + whole(2),
        out_specs=whole(1)[0],
        name="slots",
        **params(2 << 20),
    )(plan, held, crossed)


def placed_strip(block, rows, width):
    tiles, tops = block.shape[:2]
    placed = pl.pallas_call(
        place_kernel,
        out_shape=jax.ShapeDtypeStruct((3, tops, tiles, SUBLANES, LANES), jnp.float32),
        in_specs=whole(1),
        out_specs=HBM,
        scratch_shapes=[pltpu.SemaphoreType.DMA((3, tops))],
        name="place",
        **params(2 << 20),
    )(block)
    return placed.transpose(0, 1, 3, 2, 4).reshape(3, 1, rows, width)


PLANE = ("y", "x", "core")
SIZES = (8, 9, 10, 11, 12, 13, 14, 15, 16, 17, 18, 20, 24, 32)


def on_device(state, rain, ground, counts, slot_map):
    rows, width = ground.shape
    zh = lax.axis_index("zh").astype(jnp.int32).reshape(1)
    block, plan, level = stepped_tiles(zh, state, rain, ground, counts, slot_map, SIZES)
    shape = block.shape
    outgoing = block.reshape((lax.axis_size(PLANE), -1) + shape[2:])
    chosen = lax.switch(level[0], [functools.partial(blocks_for_slots, most=size) for size in SIZES], plan, outgoing)
    returned = lax.all_to_all(chosen, PLANE, split_axis=0, concat_axis=0, tiled=True)
    return placed_strip(returned.reshape(shape), rows, width)


def solution(mesh):
    fine = Mesh(mesh.devices.reshape(4, 4, 2, 2, 4), ("y", "x", "zh", "core", "row"))
    dom = ("y", "x", "zh", "core")
    placed = (P(None, dom, "row", None), P(dom, "row", None), P("row", None), P(), P())
    return jax.shard_map(
        on_device,
        mesh=fine,
        in_specs=placed,
        out_specs=P(None, dom, "row", None),
        check_vma=False,
    )
```

```python
import functools

import jax
import jax.numpy as jnp
from jax import lax
from jax.experimental import pallas as pl
from jax.experimental.pallas import tpu as pltpu
from jax.sharding import Mesh, PartitionSpec as P

gravity = 9.81
courant = 0.04
LANES = 128
SUBLANES = 8


def cell_terms(depth, norm, tang):
    vel = norm / depth
    cel = jnp.sqrt(gravity * depth)
    press = 0.5 * gravity * depth * depth
    return depth, norm, tang, norm * vel + press, tang * vel, vel - cel, vel + cel


def interface(left, right):
    depth_l, norm_l, tang_l, fnorm_l, ftang_l, slow_l, fast_l = left
    depth_r, norm_r, tang_r, fnorm_r, ftang_r, slow_r, fast_r = right
    lower = jnp.minimum(jnp.minimum(slow_l, slow_r), 0.0)
    upper = jnp.maximum(jnp.maximum(fast_l, fast_r), 0.0)
    scale = 1.0 / (upper - lower)
    both = upper * lower
    return (
        (upper * norm_l - lower * norm_r + both * (depth_r - depth_l)) * scale,
        (upper * fnorm_l - lower * fnorm_r + both * (norm_r - norm_l)) * scale,
        (upper * ftang_l - lower * ftang_r + both * (tang_r - tang_l)) * scale,
    )


def both_ways(depth, flow_a, flow_b):
    inverse = 1.0 / depth
    cel = jnp.sqrt(gravity * depth)
    press = (0.5 * gravity) * depth * depth
    vel_a = flow_a * inverse
    vel_b = flow_b * inverse
    cross = flow_a * vel_b
    by_row = (depth, flow_a, flow_b, flow_a * vel_a + press, cross, vel_a - cel, vel_a + cel)
    by_col = (depth, flow_b, flow_a, flow_b * vel_b + press, cross, vel_b - cel, vel_b + cel)
    return by_row, by_col


def pack_kernel(state_ref, ground_ref, first_ref, last_ref, sems):
    tops = ground_ref.shape[0]
    copies = []
    for side, (top, row, out_ref) in enumerate(((tops - 1, SUBLANES - 1, last_ref), (0, 0, first_ref))):
        copies.append(pltpu.make_async_copy(state_ref.at[:, top, :, row], out_ref.at[0:3], sems.at[side, 0]))
        copies.append(pltpu.make_async_copy(ground_ref.at[top, :, row], out_ref.at[3], sems.at[side, 1]))
    for copy in copies:
        copy.start()
    for copy in copies:
        copy.wait()


def write_plan(zh, counts, slots, plan_ref, level_ref, sizes):
    total = counts.shape[1]
    square = (total, total)
    i = lax.broadcasted_iota(jnp.int32, square, 0)
    j = lax.broadcasted_iota(jnp.int32, square, 1)

    def over_lanes(values):
        return jnp.sum(values, axis=1, keepdims=True)

    def over_rows(values):
        return jnp.sum(values, axis=0, keepdims=True)

    def half(places):
        return jnp.bitwise_and(jnp.right_shift(places, 1), 1)

    def place(places):
        return 2 * jnp.right_shift(places, 2) + jnp.bitwise_and(places, 1)

    cumul = over_lanes(jnp.where(j <= i, counts, 0))
    ordered = over_rows((cumul <= j).astype(jnp.int32))
    ancestor = over_lanes(jnp.where(slots == i, ordered, 0))
    crossing = jnp.logical_and(ancestor == j, half(i) != half(j))
    needed = (over_rows(crossing.astype(jnp.int32)) > 0).astype(jnp.int32)
    needed_col = over_lanes(jnp.where(i == j, needed, 0))
    earlier = jnp.logical_and(i < j, half(i) == half(j))
    rank = over_rows(jnp.where(earlier, needed_col, 0))
    rank_col = over_lanes(jnp.where(i == j, rank, 0))
    mine = jnp.logical_and(half(i) == zh, jnp.logical_and(needed_col > 0, rank_col == j))
    plan_ref[0:1, :] = over_rows(jnp.where(mine, place(i), 0))
    rank_of = over_lanes(jnp.where(ancestor == j, rank, 0))
    source = jnp.where(half(ancestor) == zh, place(ancestor), total // 2 + rank_of)
    here = jnp.logical_and(half(i) == zh, place(i) == j)
    plan_ref[1:2, :] = over_rows(jnp.where(here, source, 0))
    lower = jnp.sum(jnp.where(half(j[0:1]) == 0, needed, 0))
    most = jnp.maximum(lower, jnp.sum(needed) - lower)
    level_ref[0] = sum((most > size).astype(jnp.int32) for size in sizes[:-1])


def step_kernel(
    zh_ref, state_ref, ground_ref, rain_hbm, counts_hbm, slots_hbm,
    out_ref, plan_smem, level_ref, rain_ref, counts_ref, slots_ref, plan_ref, sems, *, unroll, tail, sizes
):
    rows, width = ground_ref.shape
    copies = [
        pltpu.make_async_copy(counts_hbm, counts_ref, sems.at[0]),
        pltpu.make_async_copy(slots_hbm, slots_ref, sems.at[1]),
        pltpu.make_async_copy(rain_hbm, rain_ref, sems.at[2]),
    ]
    for copy in copies:
        copy.start()
    tiles = width // LANES
    shape = (rows, LANES)
    lane = lax.broadcasted_iota(jnp.int32, shape, 1)
    row = lax.broadcasted_iota(jnp.int32, shape, 0)
    first_lane, last_lane = lane == 0, lane == LANES - 1
    first_row, last_row = row == 0, row == rows - 1

    def columns(tile):
        start = tile * LANES
        return pl.ds(start if isinstance(tile, int) else pl.multiple_of(start, LANES), LANES)

    def load(tile):
        at = columns(tile)
        return state_ref[0, 0, :, at], state_ref[1, 0, :, at], state_ref[2, 0, :, at], ground_ref[:, at]

    def rolled(terms):
        return tuple(pltpu.roll(term, LANES - 1, 1) for term in terms)

    def mirrored(terms):
        depth, norm, tang, fnorm, ftang, slow, fast = terms
        return depth, -norm, tang, fnorm, -ftang, -fast, -slow

    def one(tile, carry, last=False):
        by_row, by_col, bed, cells_r, bed_r, flux_before, bed_before = carry
        depth, flow_a, flow_b = by_row[:3]
        if last:
            n_row, n_col, n_bed = by_row, by_col, bed
            n_rolled, n_bed_r = mirrored(by_col), bed
        else:
            n_depth, n_a, n_b, n_bed = load(tile + 1)
            n_row, n_col = both_ways(n_depth, n_a, n_b)
            n_rolled = rolled(n_col)
            n_bed_r = pltpu.roll(n_bed, LANES - 1, 1)
        right = tuple(jnp.where(last_lane, n, c) for n, c in zip(n_rolled, cells_r))
        bed_next = jnp.where(last_lane, n_bed_r, bed_r)
        flux = interface(by_col, right)
        flux_r = tuple(pltpu.roll(f, 1, 1) for f in flux)
        flux_left = tuple(jnp.where(first_lane, b, f) for b, f in zip(flux_before, flux_r))
        bed_rolled = pltpu.roll(bed, 1, 1)
        bed_left = jnp.where(first_lane, bed_before, bed_rolled)

        above = tuple(pltpu.roll(term, 1, 0) for term in by_row)
        inner = interface(above, by_row)
        inner = tuple(jnp.where(first_row, 0.0, f) for f in inner)
        below = tuple(pltpu.roll(f, rows - 1, 0) for f in inner)
        bed_up = jnp.where(first_row, 0.0, pltpu.roll(bed, 1, 0))
        bed_down = jnp.where(last_row, 0.0, pltpu.roll(bed, rows - 1, 0))

        pull = (0.5 * courant * gravity) * depth
        new_depth = depth - courant * ((below[0] - inner[0]) + (flux[0] - flux_left[0]))
        new_a = flow_a - courant * ((below[1] - inner[1]) + (flux[2] - flux_left[2])) - pull * (bed_down - bed_up)
        new_b = flow_b - courant * ((below[2] - inner[2]) + (flux[1] - flux_left[1])) - pull * (bed_next - bed_left)
        for part, value in enumerate((new_depth, new_a, new_b)):
            for top in range(rows // SUBLANES):
                out_ref[tile, top, part] = value[top * SUBLANES : (top + 1) * SUBLANES]
        return n_row, n_col, n_bed, n_rolled, n_bed_r, flux_r, bed_rolled

    depth, flow_a, flow_b, bed = load(0)
    by_row, by_col = both_ways(depth, flow_a, flow_b)
    edge = interface(mirrored(by_col), by_col)
    carry = (by_row, by_col, bed, rolled(by_col), pltpu.roll(bed, LANES - 1, 1), edge, bed)
    steps = (tiles - max(1, min(tail, tiles))) // unroll

    def some(i, carry):
        for k in range(unroll):
            carry = one(i * unroll + k, carry)
        return carry

    carry = lax.fori_loop(0, steps, some, carry)
    for copy in copies:
        copy.wait()
    write_plan(zh_ref[0], counts_ref[...], slots_ref[...], plan_ref, level_ref, sizes)
    to_scalars = pltpu.make_async_copy(plan_ref, plan_smem, sems.at[3])
    to_scalars.start()
    for tile in range(steps * unroll, tiles):
        carry = one(tile, carry, tile == tiles - 1)
    for tile in range(tiles):
        for top in range(rows // SUBLANES):
            at = slice(top * SUBLANES, (top + 1) * SUBLANES)
            out_ref[tile, top, 0] += rain_ref[0, at, columns(tile)]
    to_scalars.wait()


def edge_kernel(strip_ref, last_ref, first_ref, low_ref, top_ref, part_ref, out_ref, top_sc, low_sc, *, strips):
    strip = strip_ref[0]

    def fluxes(inside, outside, at_wall, upward):
        own = tuple(inside[i] for i in range(4))
        far = tuple(outside[i] for i in range(4))
        depth = jnp.where(at_wall, own[0], far[0])
        norm = jnp.where(at_wall, -own[1], far[1])
        tang = jnp.where(at_wall, own[2], far[2])
        bed = jnp.where(at_wall, own[3], far[3])
        mine = cell_terms(*own[:3])
        other = cell_terms(depth, norm, tang)
        flux = interface(other, mine) if upward else interface(mine, other)
        sign = courant if upward else -courant
        pull = (0.5 * courant * gravity) * own[0] * bed
        return (
            sign * flux[0],
            sign * flux[1] + (pull if upward else -pull),
            sign * flux[2],
        )

    for part, value in enumerate(fluxes(first_ref, top_ref, strip == 0, True)):
        top_sc[part] = value
    for part, value in enumerate(fluxes(last_ref, low_ref, strip == strips - 1, False)):
        low_sc[part] = value
    tiles = out_ref.shape[0]
    tops = out_ref.shape[1]
    out_ref[...] = part_ref[...]
    for tile in range(tiles):
        for part in range(3):
            out_ref[tile, 0, part, 0:1, :] = part_ref[tile, 0, part, 0:1, :] + top_sc[part, tile : tile + 1, :]
            out_ref[tile, tops - 1, part, SUBLANES - 1 : SUBLANES, :] = (
                part_ref[tile, tops - 1, part, SUBLANES - 1 : SUBLANES, :] + low_sc[part, tile : tile + 1, :]
            )


def outgoing_kernel(plan_ref, held_ref, out_ref):
    for k in range(out_ref.shape[0]):
        out_ref[k] = held_ref[plan_ref[0, k]]


def slots_kernel(plan_ref, held_ref, crossed_ref, out_ref):
    held, most = held_ref.shape[0], crossed_ref.shape[0]
    for slot in range(out_ref.shape[0]):
        code = plan_ref[1, slot]
        near = held_ref[jnp.minimum(code, held - 1)]
        far = crossed_ref[jnp.clip(code - held, 0, most - 1)]
        out_ref[slot] = jnp.where(code < held, near, far)


def place_kernel(tiles_ref, out_hbm, sems):
    tops, parts = tiles_ref.shape[1:3]
    copies = [
        pltpu.make_async_copy(tiles_ref.at[:, top, part], out_hbm.at[part, top], sems.at[part, top])
        for part in range(parts)
        for top in range(tops)
    ]
    for copy in copies:
        copy.start()
    for copy in copies:
        copy.wait()


def whole(count):
    return [pl.BlockSpec(memory_space=pltpu.VMEM)] * count


def params(moved):
    return dict(
        compiler_params=pltpu.CompilerParams(vmem_limit_bytes=16 * 1024 * 1024),
        cost_estimate=pl.CostEstimate(flops=moved * 40, bytes_accessed=moved, transcendentals=0),
    )


COLUMN = ("zh", "row")
UNROLL = 8
TAIL = 16
HBM = pl.BlockSpec(memory_space=pltpu.HBM)
SMEM = pl.BlockSpec(memory_space=pltpu.SMEM)


def packed_edges(state, ground):
    rows, width = ground.shape
    tops, tiles = rows // SUBLANES, width // LANES
    shape = pltpu.VMEM((4, tiles, LANES), jnp.float32)
    state = state.reshape(3, tops, SUBLANES, tiles, LANES).transpose(0, 1, 3, 2, 4)
    ground = ground.reshape(tops, SUBLANES, tiles, LANES).transpose(0, 2, 1, 3)
    return pl.pallas_call(
        pack_kernel,
        out_shape=(shape, shape),
        in_specs=[HBM, HBM],
        out_specs=whole(2),
        scratch_shapes=[pltpu.SemaphoreType.DMA((2, 2))],
        name="pack",
        **params(1 << 18),
    )(*in_hbm(state, ground))


def in_hbm(*arrays):
    return [pltpu.with_memory_space_constraint(array, pltpu.HBM) for array in arrays]


def partial_step(zh, state, rain, ground, counts, slot_map, sizes, unroll=UNROLL, tail=TAIL):
    rows, width = ground.shape
    tiles, tops = width // LANES, rows // SUBLANES
    row = (1, counts.shape[0])
    return pl.pallas_call(
        functools.partial(step_kernel, unroll=unroll, tail=tail, sizes=sizes),
        out_shape=(
            jax.ShapeDtypeStruct((tiles, tops, 3, SUBLANES, LANES), jnp.float32),
            pltpu.SMEM((2, row[1]), jnp.int32),
            pltpu.SMEM((1,), jnp.int32),
        ),
        in_specs=[SMEM] + whole(2) + [HBM] * 3,
        out_specs=whole(1) + [SMEM] * 2,
        scratch_shapes=[
            pltpu.VMEM(rain.shape, jnp.float32),
            pltpu.VMEM(row, jnp.int32),
            pltpu.VMEM(row, jnp.int32),
            pltpu.VMEM((2, row[1]), jnp.int32),
            pltpu.SemaphoreType.DMA((4,)),
        ],
        name="step",
        **params(8 << 20),
    )(zh, state, ground, *in_hbm(rain, counts.reshape(row), slot_map.reshape(row)))


def stepped_tiles(zh, state, rain, ground, counts, slot_map, sizes):
    rows, width = ground.shape
    tiles = width // LANES
    strips = lax.axis_size("row")
    first, last = packed_edges(state, ground)
    count = lax.axis_size(COLUMN)
    forward = [(i, (i + 1) % count) for i in range(count)]
    backward = [(target, source) for source, target in forward]
    top = lax.ppermute(last, COLUMN, forward)
    low = lax.ppermute(first, COLUMN, backward)
    partial, plan, level = partial_step(zh, state, rain, ground, counts, slot_map, sizes)
    strip = lax.axis_index("row").astype(jnp.int32).reshape(1)
    square = (4, tiles, LANES)
    block = pl.pallas_call(
        functools.partial(edge_kernel, strips=strips),
        out_shape=pltpu.VMEM(partial.shape, jnp.float32),
        in_specs=[SMEM] + whole(5),
        out_specs=whole(1)[0],
        scratch_shapes=[pltpu.VMEM((3, tiles, LANES), jnp.float32)] * 2,
        name="edges",
        **params(1 << 20),
    )(strip, last.reshape(square), first.reshape(square), low.reshape(square), top.reshape(square), partial)
    return block, plan, level


SWAP = [(0, 1), (1, 0)]


def blocks_for_slots(plan, block, most):
    held = lax.all_to_all(block, PLANE, split_axis=0, concat_axis=0, tiled=True)
    outgoing = pl.pallas_call(
        outgoing_kernel,
        out_shape=jax.ShapeDtypeStruct((most,) + held.shape[1:], jnp.float32),
        in_specs=[SMEM] + whole(1),
        out_specs=whole(1)[0],
        name="outgoing",
        **params(1 << 20),
    )(plan, held)
    crossed = lax.ppermute(outgoing, "zh", SWAP)
    return pl.pallas_call(
        slots_kernel,
        out_shape=jax.ShapeDtypeStruct(held.shape, jnp.float32),
        in_specs=[SMEM] + whole(2),
        out_specs=whole(1)[0],
        name="slots",
        **params(2 << 20),
    )(plan, held, crossed)


def placed_strip(block, rows, width):
    tiles, tops = block.shape[:2]
    placed = pl.pallas_call(
        place_kernel,
        out_shape=jax.ShapeDtypeStruct((3, tops, tiles, SUBLANES, LANES), jnp.float32),
        in_specs=whole(1),
        out_specs=HBM,
        scratch_shapes=[pltpu.SemaphoreType.DMA((3, tops))],
        name="place",
        **params(2 << 20),
    )(block)
    return placed.transpose(0, 1, 3, 2, 4).reshape(3, 1, rows, width)


PLANE = ("y", "x", "core")
SIZES = (8, 9, 10, 11, 12, 13, 14, 15, 16, 17, 18, 20, 24, 32)


def on_device(state, rain, ground, counts, slot_map):
    rows, width = ground.shape
    zh = lax.axis_index("zh").astype(jnp.int32).reshape(1)
    block, plan, level = stepped_tiles(zh, state, rain, ground, counts, slot_map, SIZES)
    shape = block.shape
    outgoing = block.reshape((lax.axis_size(PLANE), -1) + shape[2:])
    chosen = lax.switch(level[0], [functools.partial(blocks_for_slots, most=size) for size in SIZES], plan, outgoing)
    returned = lax.all_to_all(chosen, PLANE, split_axis=0, concat_axis=0, tiled=True)
    return placed_strip(returned.reshape(shape), rows, width)


def solution(mesh):
    fine = Mesh(mesh.devices.reshape(4, 4, 2, 2, 4), ("y", "x", "zh", "core", "row"))
    dom = ("y", "x", "zh", "core")
    placed = (P(None, dom, "row", None), P(dom, "row", None), P("row", None), P(), P())
    return jax.shard_map(
        on_device,
        mesh=fine,
        in_specs=placed,
        out_specs=P(None, dom, "row", None),
        check_vma=False,
    )
```

```python
import functools

import jax
import jax.numpy as jnp
from jax import lax
from jax.experimental import pallas as pl
from jax.experimental.pallas import tpu as pltpu
from jax.sharding import Mesh, PartitionSpec as P

gravity = 9.81
courant = 0.04
LANES = 128
SUBLANES = 8


def cell_terms(depth, norm, tang):
    vel = norm / depth
    cel = jnp.sqrt(gravity * depth)
    press = 0.5 * gravity * depth * depth
    return depth, norm, tang, norm * vel + press, tang * vel, vel - cel, vel + cel


def interface(left, right):
    depth_l, norm_l, tang_l, fnorm_l, ftang_l, slow_l, fast_l = left
    depth_r, norm_r, tang_r, fnorm_r, ftang_r, slow_r, fast_r = right
    lower = jnp.minimum(jnp.minimum(slow_l, slow_r), 0.0)
    upper = jnp.maximum(jnp.maximum(fast_l, fast_r), 0.0)
    scale = 1.0 / (upper - lower)
    both = upper * lower
    return (
        (upper * norm_l - lower * norm_r + both * (depth_r - depth_l)) * scale,
        (upper * fnorm_l - lower * fnorm_r + both * (norm_r - norm_l)) * scale,
        (upper * ftang_l - lower * ftang_r + both * (tang_r - tang_l)) * scale,
    )


def both_ways(depth, flow_a, flow_b):
    inverse = 1.0 / depth
    cel = jnp.sqrt(gravity * depth)
    press = (0.5 * gravity) * depth * depth
    vel_a = flow_a * inverse
    vel_b = flow_b * inverse
    cross = flow_a * vel_b
    by_row = (depth, flow_a, flow_b, flow_a * vel_a + press, cross, vel_a - cel, vel_a + cel)
    by_col = (depth, flow_b, flow_a, flow_b * vel_b + press, cross, vel_b - cel, vel_b + cel)
    return by_row, by_col


def pack_kernel(state_ref, ground_ref, first_ref, last_ref, sems):
    tops = ground_ref.shape[0]
    copies = []
    for side, (top, row, out_ref) in enumerate(((tops - 1, SUBLANES - 1, last_ref), (0, 0, first_ref))):
        copies.append(pltpu.make_async_copy(state_ref.at[:, top, :, row], out_ref.at[0:3], sems.at[side, 0]))
        copies.append(pltpu.make_async_copy(ground_ref.at[top, :, row], out_ref.at[3], sems.at[side, 1]))
    for copy in copies:
        copy.start()
    for copy in copies:
        copy.wait()


def write_plan(zh, counts, slots, plan_ref, level_ref, sizes):
    total = counts.shape[1]
    square = (total, total)
    i = lax.broadcasted_iota(jnp.int32, square, 0)
    j = lax.broadcasted_iota(jnp.int32, square, 1)

    def over_lanes(values):
        return jnp.sum(values, axis=1, keepdims=True)

    def over_rows(values):
        return jnp.sum(values, axis=0, keepdims=True)

    def half(places):
        return jnp.bitwise_and(jnp.right_shift(places, 1), 1)

    def place(places):
        return 2 * jnp.right_shift(places, 2) + jnp.bitwise_and(places, 1)

    cumul = over_lanes(jnp.where(j <= i, counts, 0))
    ordered = over_rows((cumul <= j).astype(jnp.int32))
    ancestor = over_lanes(jnp.where(slots == i, ordered, 0))
    crossing = jnp.logical_and(ancestor == j, half(i) != half(j))
    needed = (over_rows(crossing.astype(jnp.int32)) > 0).astype(jnp.int32)
    needed_col = over_lanes(jnp.where(i == j, needed, 0))
    earlier = jnp.logical_and(i < j, half(i) == half(j))
    rank = over_rows(jnp.where(earlier, needed_col, 0))
    rank_col = over_lanes(jnp.where(i == j, rank, 0))
    mine = jnp.logical_and(half(i) == zh, jnp.logical_and(needed_col > 0, rank_col == j))
    plan_ref[0:1, :] = over_rows(jnp.where(mine, place(i), 0))
    rank_of = over_lanes(jnp.where(ancestor == j, rank, 0))
    source = jnp.where(half(ancestor) == zh, place(ancestor), total // 2 + rank_of)
    here = jnp.logical_and(half(i) == zh, place(i) == j)
    plan_ref[1:2, :] = over_rows(jnp.where(here, source, 0))
    lower = jnp.sum(jnp.where(half(j[0:1]) == 0, needed, 0))
    most = jnp.maximum(lower, jnp.sum(needed) - lower)
    level_ref[0] = sum((most > size).astype(jnp.int32) for size in sizes[:-1])


def step_kernel(
    zh_ref, state_ref, ground_ref, rain_hbm, counts_hbm, slots_hbm,
    out_ref, plan_smem, level_ref, rain_ref, counts_ref, slots_ref, plan_ref, sems, *, unroll, tail, sizes
):
    rows, width = ground_ref.shape
    copies = [
        pltpu.make_async_copy(counts_hbm, counts_ref, sems.at[0]),
        pltpu.make_async_copy(slots_hbm, slots_ref, sems.at[1]),
        pltpu.make_async_copy(rain_hbm, rain_ref, sems.at[2]),
    ]
    for copy in copies:
        copy.start()
    tiles = width // LANES
    shape = (rows, LANES)
    lane = lax.broadcasted_iota(jnp.int32, shape, 1)
    row = lax.broadcasted_iota(jnp.int32, shape, 0)
    first_lane, last_lane = lane == 0, lane == LANES - 1
    first_row, last_row = row == 0, row == rows - 1

    def columns(tile):
        start = tile * LANES
        return pl.ds(start if isinstance(tile, int) else pl.multiple_of(start, LANES), LANES)

    def load(tile):
        at = columns(tile)
        return state_ref[0, 0, :, at], state_ref[1, 0, :, at], state_ref[2, 0, :, at], ground_ref[:, at]

    def rolled(terms):
        return tuple(pltpu.roll(term, LANES - 1, 1) for term in terms)

    def mirrored(terms):
        depth, norm, tang, fnorm, ftang, slow, fast = terms
        return depth, -norm, tang, fnorm, -ftang, -fast, -slow

    def one(tile, carry, last=False):
        by_row, by_col, bed, cells_r, bed_r, flux_before, bed_before = carry
        depth, flow_a, flow_b = by_row[:3]
        if last:
            n_row, n_col, n_bed = by_row, by_col, bed
            n_rolled, n_bed_r = mirrored(by_col), bed
        else:
            n_depth, n_a, n_b, n_bed = load(tile + 1)
            n_row, n_col = both_ways(n_depth, n_a, n_b)
            n_rolled = rolled(n_col)
            n_bed_r = pltpu.roll(n_bed, LANES - 1, 1)
        right = tuple(jnp.where(last_lane, n, c) for n, c in zip(n_rolled, cells_r))
        bed_next = jnp.where(last_lane, n_bed_r, bed_r)
        flux = interface(by_col, right)
        flux_r = tuple(pltpu.roll(f, 1, 1) for f in flux)
        flux_left = tuple(jnp.where(first_lane, b, f) for b, f in zip(flux_before, flux_r))
        bed_rolled = pltpu.roll(bed, 1, 1)
        bed_left = jnp.where(first_lane, bed_before, bed_rolled)

        above = tuple(pltpu.roll(term, 1, 0) for term in by_row)
        inner = interface(above, by_row)
        inner = tuple(jnp.where(first_row, 0.0, f) for f in inner)
        below = tuple(pltpu.roll(f, rows - 1, 0) for f in inner)
        bed_up = jnp.where(first_row, 0.0, pltpu.roll(bed, 1, 0))
        bed_down = jnp.where(last_row, 0.0, pltpu.roll(bed, rows - 1, 0))

        pull = (0.5 * courant * gravity) * depth
        new_depth = depth - courant * ((below[0] - inner[0]) + (flux[0] - flux_left[0]))
        new_a = flow_a - courant * ((below[1] - inner[1]) + (flux[2] - flux_left[2])) - pull * (bed_down - bed_up)
        new_b = flow_b - courant * ((below[2] - inner[2]) + (flux[1] - flux_left[1])) - pull * (bed_next - bed_left)
        for part, value in enumerate((new_depth, new_a, new_b)):
            for top in range(rows // SUBLANES):
                out_ref[tile, top, part] = value[top * SUBLANES : (top + 1) * SUBLANES]
        return n_row, n_col, n_bed, n_rolled, n_bed_r, flux_r, bed_rolled

    depth, flow_a, flow_b, bed = load(0)
    by_row, by_col = both_ways(depth, flow_a, flow_b)
    edge = interface(mirrored(by_col), by_col)
    carry = (by_row, by_col, bed, rolled(by_col), pltpu.roll(bed, LANES - 1, 1), edge, bed)
    steps = (tiles - max(1, min(tail, tiles))) // unroll

    def some(i, carry):
        for k in range(unroll):
            carry = one(i * unroll + k, carry)
        return carry

    carry = lax.fori_loop(0, steps, some, carry)
    for copy in copies:
        copy.wait()
    write_plan(zh_ref[0], counts_ref[...], slots_ref[...], plan_ref, level_ref, sizes)
    to_scalars = pltpu.make_async_copy(plan_ref, plan_smem, sems.at[3])
    to_scalars.start()
    for tile in range(steps * unroll, tiles):
        carry = one(tile, carry, tile == tiles - 1)
    for tile in range(tiles):
        for top in range(rows // SUBLANES):
            at = slice(top * SUBLANES, (top + 1) * SUBLANES)
            out_ref[tile, top, 0] += rain_ref[0, at, columns(tile)]
    to_scalars.wait()


def edge_kernel(strip_ref, last_ref, first_ref, low_ref, top_ref, part_ref, out_ref, top_sc, low_sc, *, strips):
    strip = strip_ref[0]

    def fluxes(inside, outside, at_wall, upward):
        own = tuple(inside[i] for i in range(4))
        far = tuple(outside[i] for i in range(4))
        depth = jnp.where(at_wall, own[0], far[0])
        norm = jnp.where(at_wall, -own[1], far[1])
        tang = jnp.where(at_wall, own[2], far[2])
        bed = jnp.where(at_wall, own[3], far[3])
        mine = cell_terms(*own[:3])
        other = cell_terms(depth, norm, tang)
        flux = interface(other, mine) if upward else interface(mine, other)
        sign = courant if upward else -courant
        pull = (0.5 * courant * gravity) * own[0] * bed
        return (
            sign * flux[0],
            sign * flux[1] + (pull if upward else -pull),
            sign * flux[2],
        )

    for part, value in enumerate(fluxes(first_ref, top_ref, strip == 0, True)):
        top_sc[part] = value
    for part, value in enumerate(fluxes(last_ref, low_ref, strip == strips - 1, False)):
        low_sc[part] = value
    tiles = out_ref.shape[0]
    tops = out_ref.shape[1]
    out_ref[...] = part_ref[...]
    for tile in range(tiles):
        for part in range(3):
            out_ref[tile, 0, part, 0:1, :] = part_ref[tile, 0, part, 0:1, :] + top_sc[part, tile : tile + 1, :]
            out_ref[tile, tops - 1, part, SUBLANES - 1 : SUBLANES, :] = (
                part_ref[tile, tops - 1, part, SUBLANES - 1 : SUBLANES, :] + low_sc[part, tile : tile + 1, :]
            )


def outgoing_kernel(plan_ref, held_ref, out_ref):
    for k in range(out_ref.shape[0]):
        out_ref[k] = held_ref[plan_ref[0, k]]


def slots_kernel(plan_ref, held_ref, crossed_ref, out_ref):
    held, most = held_ref.shape[0], crossed_ref.shape[0]
    for slot in range(out_ref.shape[0]):
        code = plan_ref[1, slot]
        near = held_ref[jnp.minimum(code, held - 1)]
        far = crossed_ref[jnp.clip(code - held, 0, most - 1)]
        out_ref[slot] = jnp.where(code < held, near, far)


def place_kernel(tiles_ref, out_hbm, sems):
    tops, parts = tiles_ref.shape[1:3]
    copies = [
        pltpu.make_async_copy(tiles_ref.at[:, top, part], out_hbm.at[part, top], sems.at[part, top])
        for part in range(parts)
        for top in range(tops)
    ]
    for copy in copies:
        copy.start()
    for copy in copies:
        copy.wait()


def whole(count):
    return [pl.BlockSpec(memory_space=pltpu.VMEM)] * count


def params(moved):
    return dict(
        compiler_params=pltpu.CompilerParams(vmem_limit_bytes=16 * 1024 * 1024),
        cost_estimate=pl.CostEstimate(flops=moved * 40, bytes_accessed=moved, transcendentals=0),
    )


COLUMN = ("zh", "row")
UNROLL = 8
TAIL = 16
HBM = pl.BlockSpec(memory_space=pltpu.HBM)
SMEM = pl.BlockSpec(memory_space=pltpu.SMEM)


def packed_edges(state, ground):
    rows, width = ground.shape
    tops, tiles = rows // SUBLANES, width // LANES
    shape = pltpu.VMEM((4, tiles, LANES), jnp.float32)
    state = state.reshape(3, tops, SUBLANES, tiles, LANES).transpose(0, 1, 3, 2, 4)
    ground = ground.reshape(tops, SUBLANES, tiles, LANES).transpose(0, 2, 1, 3)
    return pl.pallas_call(
        pack_kernel,
        out_shape=(shape, shape),
        in_specs=[HBM, HBM],
        out_specs=whole(2),
        scratch_shapes=[pltpu.SemaphoreType.DMA((2, 2))],
        name="pack",
        **params(1 << 18),
    )(*in_hbm(state, ground))


def in_hbm(*arrays):
    return [pltpu.with_memory_space_constraint(array, pltpu.HBM) for array in arrays]


def partial_step(zh, state, rain, ground, counts, slot_map, sizes, unroll=UNROLL, tail=TAIL):
    rows, width = ground.shape
    tiles, tops = width // LANES, rows // SUBLANES
    row = (1, counts.shape[0])
    return pl.pallas_call(
        functools.partial(step_kernel, unroll=unroll, tail=tail, sizes=sizes),
        out_shape=(
            jax.ShapeDtypeStruct((tiles, tops, 3, SUBLANES, LANES), jnp.float32),
            pltpu.SMEM((2, row[1]), jnp.int32),
            pltpu.SMEM((1,), jnp.int32),
        ),
        in_specs=[SMEM] + whole(2) + [HBM] * 3,
        out_specs=whole(1) + [SMEM] * 2,
        scratch_shapes=[
            pltpu.VMEM(rain.shape, jnp.float32),
            pltpu.VMEM(row, jnp.int32),
            pltpu.VMEM(row, jnp.int32),
            pltpu.VMEM((2, row[1]), jnp.int32),
            pltpu.SemaphoreType.DMA((4,)),
        ],
        name="step",
        **params(8 << 20),
    )(zh, state, ground, *in_hbm(rain, counts.reshape(row), slot_map.reshape(row)))


def stepped_tiles(zh, state, rain, ground, counts, slot_map, sizes):
    rows, width = ground.shape
    tiles = width // LANES
    strips = lax.axis_size("row")
    first, last = packed_edges(state, ground)
    count = lax.axis_size(COLUMN)
    forward = [(i, (i + 1) % count) for i in range(count)]
    backward = [(i, (i + strips - 1) % strips) for i in range(strips)]
    top = lax.ppermute(last, COLUMN, forward)
    low = lax.ppermute(first, "row", backward)
    partial, plan, level = partial_step(zh, state, rain, ground, counts, slot_map, sizes)
    strip = lax.axis_index("row").astype(jnp.int32).reshape(1)
    square = (4, tiles, LANES)
    block = pl.pallas_call(
        functools.partial(edge_kernel, strips=strips),
        out_shape=pltpu.VMEM(partial.shape, jnp.float32),
        in_specs=[SMEM] + whole(5),
        out_specs=whole(1)[0],
        scratch_shapes=[pltpu.VMEM((3, tiles, LANES), jnp.float32)] * 2,
        name="edges",
        **params(1 << 20),
    )(strip, last.reshape(square), first.reshape(square), low.reshape(square), top.reshape(square), partial)
    return block, plan, level


SWAP = [(0, 1), (1, 0)]


def blocks_for_slots(plan, block, most):
    held = lax.all_to_all(block, PLANE, split_axis=0, concat_axis=0, tiled=True)
    outgoing = pl.pallas_call(
        outgoing_kernel,
        out_shape=jax.ShapeDtypeStruct((most,) + held.shape[1:], jnp.float32),
        in_specs=[SMEM] + whole(1),
        out_specs=whole(1)[0],
        name="outgoing",
        **params(1 << 20),
    )(plan, held)
    crossed = lax.ppermute(outgoing, "zh", SWAP)
    return pl.pallas_call(
        slots_kernel,
        out_shape=jax.ShapeDtypeStruct(held.shape, jnp.float32),
        in_specs=[SMEM] + whole(2),
        out_specs=whole(1)[0],
        name="slots",
        **params(2 << 20),
    )(plan, held, crossed)


def placed_strip(block, rows, width):
    tiles, tops = block.shape[:2]
    placed = pl.pallas_call(
        place_kernel,
        out_shape=jax.ShapeDtypeStruct((3, tops, tiles, SUBLANES, LANES), jnp.float32),
        in_specs=whole(1),
        out_specs=HBM,
        scratch_shapes=[pltpu.SemaphoreType.DMA((3, tops))],
        name="place",
        **params(2 << 20),
    )(block)
    return placed.transpose(0, 1, 3, 2, 4).reshape(3, 1, rows, width)


PLANE = ("y", "x", "core")
SIZES = (8, 9, 10, 11, 12, 13, 14, 15, 16, 17, 18, 20, 24, 32)


def on_device(state, rain, ground, counts, slot_map):
    rows, width = ground.shape
    zh = lax.axis_index("zh").astype(jnp.int32).reshape(1)
    block, plan, level = stepped_tiles(zh, state, rain, ground, counts, slot_map, SIZES)
    shape = block.shape
    outgoing = block.reshape((lax.axis_size(PLANE), -1) + shape[2:])
    chosen = lax.switch(level[0], [functools.partial(blocks_for_slots, most=size) for size in SIZES], plan, outgoing)
    returned = lax.all_to_all(chosen, PLANE, split_axis=0, concat_axis=0, tiled=True)
    return placed_strip(returned.reshape(shape), rows, width)


def solution(mesh):
    fine = Mesh(mesh.devices.reshape(4, 4, 2, 2, 4), ("y", "x", "zh", "core", "row"))
    dom = ("y", "x", "zh", "core")
    placed = (P(None, dom, "row", None), P(dom, "row", None), P("row", None), P(), P())
    return jax.shard_map(
        on_device,
        mesh=fine,
        in_specs=placed,
        out_specs=P(None, dom, "row", None),
        check_vma=False,
    )
```

```python
import functools

import jax
import jax.numpy as jnp
from jax import lax
from jax.experimental import pallas as pl
from jax.experimental.pallas import tpu as pltpu
from jax.sharding import Mesh, PartitionSpec as P

gravity = 9.81
courant = 0.04
LANES = 128
SUBLANES = 8


def cell_terms(depth, norm, tang):
    vel = norm / depth
    cel = jnp.sqrt(gravity * depth)
    press = 0.5 * gravity * depth * depth
    return depth, norm, tang, norm * vel + press, tang * vel, vel - cel, vel + cel


def interface(left, right):
    depth_l, norm_l, tang_l, fnorm_l, ftang_l, slow_l, fast_l = left
    depth_r, norm_r, tang_r, fnorm_r, ftang_r, slow_r, fast_r = right
    lower = jnp.minimum(jnp.minimum(slow_l, slow_r), 0.0)
    upper = jnp.maximum(jnp.maximum(fast_l, fast_r), 0.0)
    scale = 1.0 / (upper - lower)
    both = upper * lower
    return (
        (upper * norm_l - lower * norm_r + both * (depth_r - depth_l)) * scale,
        (upper * fnorm_l - lower * fnorm_r + both * (norm_r - norm_l)) * scale,
        (upper * ftang_l - lower * ftang_r + both * (tang_r - tang_l)) * scale,
    )


def both_ways(depth, flow_a, flow_b):
    inverse = 1.0 / depth
    cel = jnp.sqrt(gravity * depth)
    press = (0.5 * gravity) * depth * depth
    vel_a = flow_a * inverse
    vel_b = flow_b * inverse
    cross = flow_a * vel_b
    by_row = (depth, flow_a, flow_b, flow_a * vel_a + press, cross, vel_a - cel, vel_a + cel)
    by_col = (depth, flow_b, flow_a, flow_b * vel_b + press, cross, vel_b - cel, vel_b + cel)
    return by_row, by_col


def pack_kernel(state_ref, ground_ref, first_ref, last_ref, sems):
    tops = ground_ref.shape[0]
    copies = []
    for side, (top, row, out_ref) in enumerate(((tops - 1, SUBLANES - 1, last_ref), (0, 0, first_ref))):
        copies.append(pltpu.make_async_copy(state_ref.at[:, top, :, row], out_ref.at[0:3], sems.at[side, 0]))
        copies.append(pltpu.make_async_copy(ground_ref.at[top, :, row], out_ref.at[3], sems.at[side, 1]))
    for copy in copies:
        copy.start()
    for copy in copies:
        copy.wait()


def write_plan(zh, counts, slots, plan_ref, level_ref, sizes):
    total = counts.shape[1]
    square = (total, total)
    i = lax.broadcasted_iota(jnp.int32, square, 0)
    j = lax.broadcasted_iota(jnp.int32, square, 1)

    def over_lanes(values):
        return jnp.sum(values, axis=1, keepdims=True)

    def over_rows(values):
        return jnp.sum(values, axis=0, keepdims=True)

    def half(places):
        return jnp.bitwise_and(jnp.right_shift(places, 1), 1)

    def place(places):
        return 2 * jnp.right_shift(places, 2) + jnp.bitwise_and(places, 1)

    cumul = over_lanes(jnp.where(j <= i, counts, 0))
    ordered = over_rows((cumul <= j).astype(jnp.int32))
    ancestor = over_lanes(jnp.where(slots == i, ordered, 0))
    crossing = jnp.logical_and(ancestor == j, half(i) != half(j))
    needed = (over_rows(crossing.astype(jnp.int32)) > 0).astype(jnp.int32)
    needed_col = over_lanes(jnp.where(i == j, needed, 0))
    earlier = jnp.logical_and(i < j, half(i) == half(j))
    rank = over_rows(jnp.where(earlier, needed_col, 0))
    rank_col = over_lanes(jnp.where(i == j, rank, 0))
    mine = jnp.logical_and(half(i) == zh, jnp.logical_and(needed_col > 0, rank_col == j))
    plan_ref[0:1, :] = over_rows(jnp.where(mine, place(i), 0))
    rank_of = over_lanes(jnp.where(ancestor == j, rank, 0))
    source = jnp.where(half(ancestor) == zh, place(ancestor), total // 2 + rank_of)
    here = jnp.logical_and(half(i) == zh, place(i) == j)
    plan_ref[1:2, :] = over_rows(jnp.where(here, source, 0))
    lower = jnp.sum(jnp.where(half(j[0:1]) == 0, needed, 0))
    most = jnp.maximum(lower, jnp.sum(needed) - lower)
    level_ref[0] = sum((most > size).astype(jnp.int32) for size in sizes[:-1])


def step_kernel(
    zh_ref, state_ref, ground_ref, rain_hbm, counts_hbm, slots_hbm,
    out_ref, plan_smem, level_ref, rain_ref, counts_ref, slots_ref, plan_ref, sems, *, unroll, tail, sizes
):
    rows, width = ground_ref.shape
    copies = [
        pltpu.make_async_copy(counts_hbm, counts_ref, sems.at[0]),
        pltpu.make_async_copy(slots_hbm, slots_ref, sems.at[1]),
        pltpu.make_async_copy(rain_hbm, rain_ref, sems.at[2]),
    ]
    for copy in copies:
        copy.start()
    tiles = width // LANES
    shape = (rows, LANES)
    lane = lax.broadcasted_iota(jnp.int32, shape, 1)
    row = lax.broadcasted_iota(jnp.int32, shape, 0)
    first_lane, last_lane = lane == 0, lane == LANES - 1
    first_row, last_row = row == 0, row == rows - 1

    def columns(tile):
        start = tile * LANES
        return pl.ds(start if isinstance(tile, int) else pl.multiple_of(start, LANES), LANES)

    def load(tile):
        at = columns(tile)
        return state_ref[0, 0, :, at], state_ref[1, 0, :, at], state_ref[2, 0, :, at], ground_ref[:, at]

    def rolled(terms):
        return tuple(pltpu.roll(term, LANES - 1, 1) for term in terms)

    def mirrored(terms):
        depth, norm, tang, fnorm, ftang, slow, fast = terms
        return depth, -norm, tang, fnorm, -ftang, -fast, -slow

    def one(tile, carry, last=False):
        by_row, by_col, bed, cells_r, bed_r, flux_before, bed_before = carry
        depth, flow_a, flow_b = by_row[:3]
        if last:
            n_row, n_col, n_bed = by_row, by_col, bed
            n_rolled, n_bed_r = mirrored(by_col), bed
        else:
            n_depth, n_a, n_b, n_bed = load(tile + 1)
            n_row, n_col = both_ways(n_depth, n_a, n_b)
            n_rolled = rolled(n_col)
            n_bed_r = pltpu.roll(n_bed, LANES - 1, 1)
        right = tuple(jnp.where(last_lane, n, c) for n, c in zip(n_rolled, cells_r))
        bed_next = jnp.where(last_lane, n_bed_r, bed_r)
        flux = interface(by_col, right)
        flux_r = tuple(pltpu.roll(f, 1, 1) for f in flux)
        flux_left = tuple(jnp.where(first_lane, b, f) for b, f in zip(flux_before, flux_r))
        bed_rolled = pltpu.roll(bed, 1, 1)
        bed_left = jnp.where(first_lane, bed_before, bed_rolled)

        above = tuple(pltpu.roll(term, 1, 0) for term in by_row)
        inner = interface(above, by_row)
        inner = tuple(jnp.where(first_row, 0.0, f) for f in inner)
        below = tuple(pltpu.roll(f, rows - 1, 0) for f in inner)
        bed_up = jnp.where(first_row, 0.0, pltpu.roll(bed, 1, 0))
        bed_down = jnp.where(last_row, 0.0, pltpu.roll(bed, rows - 1, 0))

        pull = (0.5 * courant * gravity) * depth
        new_depth = depth - courant * ((below[0] - inner[0]) + (flux[0] - flux_left[0]))
        new_a = flow_a - courant * ((below[1] - inner[1]) + (flux[2] - flux_left[2])) - pull * (bed_down - bed_up)
        new_b = flow_b - courant * ((below[2] - inner[2]) + (flux[1] - flux_left[1])) - pull * (bed_next - bed_left)
        for part, value in enumerate((new_depth, new_a, new_b)):
            for top in range(rows // SUBLANES):
                out_ref[tile, top, part] = value[top * SUBLANES : (top + 1) * SUBLANES]
        return n_row, n_col, n_bed, n_rolled, n_bed_r, flux_r, bed_rolled

    depth, flow_a, flow_b, bed = load(0)
    by_row, by_col = both_ways(depth, flow_a, flow_b)
    edge = interface(mirrored(by_col), by_col)
    carry = (by_row, by_col, bed, rolled(by_col), pltpu.roll(bed, LANES - 1, 1), edge, bed)
    steps = (tiles - max(1, min(tail, tiles))) // unroll

    def some(i, carry):
        for k in range(unroll):
            carry = one(i * unroll + k, carry)
        return carry

    carry = lax.fori_loop(0, steps, some, carry)
    for copy in copies:
        copy.wait()
    write_plan(zh_ref[0], counts_ref[...], slots_ref[...], plan_ref, level_ref, sizes)
    to_scalars = pltpu.make_async_copy(plan_ref, plan_smem, sems.at[3])
    to_scalars.start()
    for tile in range(steps * unroll, tiles):
        carry = one(tile, carry, tile == tiles - 1)
    for tile in range(tiles):
        for top in range(rows // SUBLANES):
            at = slice(top * SUBLANES, (top + 1) * SUBLANES)
            out_ref[tile, top, 0] += rain_ref[0, at, columns(tile)]
    to_scalars.wait()


def edge_kernel(strip_ref, last_ref, first_ref, low_ref, top_ref, part_ref, out_ref, top_sc, low_sc, *, strips):
    strip = strip_ref[0]

    def fluxes(inside, outside, at_wall, upward):
        own = tuple(inside[i] for i in range(4))
        far = tuple(outside[i] for i in range(4))
        depth = jnp.where(at_wall, own[0], far[0])
        norm = jnp.where(at_wall, -own[1], far[1])
        tang = jnp.where(at_wall, own[2], far[2])
        bed = jnp.where(at_wall, own[3], far[3])
        mine = cell_terms(*own[:3])
        other = cell_terms(depth, norm, tang)
        flux = interface(other, mine) if upward else interface(mine, other)
        sign = courant if upward else -courant
        pull = (0.5 * courant * gravity) * own[0] * bed
        return (
            sign * flux[0],
            sign * flux[1] + (pull if upward else -pull),
            sign * flux[2],
        )

    for part, value in enumerate(fluxes(first_ref, top_ref, strip == 0, True)):
        top_sc[part] = value
    for part, value in enumerate(fluxes(last_ref, low_ref, strip == strips - 1, False)):
        low_sc[part] = value
    tiles = out_ref.shape[0]
    tops = out_ref.shape[1]
    out_ref[...] = part_ref[...]
    for tile in range(tiles):
        for part in range(3):
            out_ref[tile, 0, part, 0:1, :] = part_ref[tile, 0, part, 0:1, :] + top_sc[part, tile : tile + 1, :]
            out_ref[tile, tops - 1, part, SUBLANES - 1 : SUBLANES, :] = (
                part_ref[tile, tops - 1, part, SUBLANES - 1 : SUBLANES, :] + low_sc[part, tile : tile + 1, :]
            )


def outgoing_kernel(plan_ref, held_ref, out_ref):
    for k in range(out_ref.shape[0]):
        out_ref[k] = held_ref[plan_ref[0, k]]


def slots_kernel(plan_ref, held_ref, crossed_ref, out_ref):
    held, most = held_ref.shape[0], crossed_ref.shape[0]
    for slot in range(out_ref.shape[0]):
        code = plan_ref[1, slot]
        near = held_ref[jnp.minimum(code, held - 1)]
        far = crossed_ref[jnp.clip(code - held, 0, most - 1)]
        out_ref[slot] = jnp.where(code < held, near, far)


def place_kernel(tiles_ref, out_hbm, sems):
    tops, parts = tiles_ref.shape[1:3]
    copies = [
        pltpu.make_async_copy(tiles_ref.at[:, top, part], out_hbm.at[part, top], sems.at[part, top])
        for part in range(parts)
        for top in range(tops)
    ]
    for copy in copies:
        copy.start()
    for copy in copies:
        copy.wait()


def whole(count):
    return [pl.BlockSpec(memory_space=pltpu.VMEM)] * count


def params(moved):
    return dict(
        compiler_params=pltpu.CompilerParams(vmem_limit_bytes=16 * 1024 * 1024),
        cost_estimate=pl.CostEstimate(flops=moved * 40, bytes_accessed=moved, transcendentals=0),
    )


COLUMN = ("zh", "row")
UNROLL = 8
TAIL = 16
HBM = pl.BlockSpec(memory_space=pltpu.HBM)
SMEM = pl.BlockSpec(memory_space=pltpu.SMEM)


def packed_edges(state, ground):
    rows, width = ground.shape
    tops, tiles = rows // SUBLANES, width // LANES
    shape = pltpu.VMEM((4, tiles, LANES), jnp.float32)
    state = state.reshape(3, tops, SUBLANES, tiles, LANES).transpose(0, 1, 3, 2, 4)
    ground = ground.reshape(tops, SUBLANES, tiles, LANES).transpose(0, 2, 1, 3)
    return pl.pallas_call(
        pack_kernel,
        out_shape=(shape, shape),
        in_specs=[HBM, HBM],
        out_specs=whole(2),
        scratch_shapes=[pltpu.SemaphoreType.DMA((2, 2))],
        name="pack",
        **params(1 << 18),
    )(*in_hbm(state, ground))


def in_hbm(*arrays):
    return [pltpu.with_memory_space_constraint(array, pltpu.HBM) for array in arrays]


def partial_step(zh, state, rain, ground, counts, slot_map, sizes, unroll=UNROLL, tail=TAIL):
    rows, width = ground.shape
    tiles, tops = width // LANES, rows // SUBLANES
    row = (1, counts.shape[0])
    return pl.pallas_call(
        functools.partial(step_kernel, unroll=unroll, tail=tail, sizes=sizes),
        out_shape=(
            jax.ShapeDtypeStruct((tiles, tops, 3, SUBLANES, LANES), jnp.float32),
            pltpu.SMEM((2, row[1]), jnp.int32),
            pltpu.SMEM((1,), jnp.int32),
        ),
        in_specs=[SMEM] + whole(2) + [HBM] * 3,
        out_specs=whole(1) + [SMEM] * 2,
        scratch_shapes=[
            pltpu.VMEM(rain.shape, jnp.float32),
            pltpu.VMEM(row, jnp.int32),
            pltpu.VMEM(row, jnp.int32),
            pltpu.VMEM((2, row[1]), jnp.int32),
            pltpu.SemaphoreType.DMA((4,)),
        ],
        name="step",
        **params(8 << 20),
    )(zh, state, ground, *in_hbm(rain, counts.reshape(row), slot_map.reshape(row)))


def stepped_tiles(zh, state, rain, ground, counts, slot_map, sizes):
    rows, width = ground.shape
    tiles = width // LANES
    strips = lax.axis_size("row")
    first, last = packed_edges(state, ground)
    count = lax.axis_size(COLUMN)
    forward = [(i, (i + 1) % strips) for i in range(strips)]
    backward = [((i + 1) % count, i) for i in range(count)]
    top = lax.ppermute(last, "row", forward)
    low = lax.ppermute(first, COLUMN, backward)
    partial, plan, level = partial_step(zh, state, rain, ground, counts, slot_map, sizes)
    strip = lax.axis_index("row").astype(jnp.int32).reshape(1)
    square = (4, tiles, LANES)
    block = pl.pallas_call(
        functools.partial(edge_kernel, strips=strips),
        out_shape=pltpu.VMEM(partial.shape, jnp.float32),
        in_specs=[SMEM] + whole(5),
        out_specs=whole(1)[0],
        scratch_shapes=[pltpu.VMEM((3, tiles, LANES), jnp.float32)] * 2,
        name="edges",
        **params(1 << 20),
    )(strip, last.reshape(square), first.reshape(square), low.reshape(square), top.reshape(square), partial)
    return block, plan, level


SWAP = [(0, 1), (1, 0)]


def blocks_for_slots(plan, block, most):
    held = lax.all_to_all(block, PLANE, split_axis=0, concat_axis=0, tiled=True)
    outgoing = pl.pallas_call(
        outgoing_kernel,
        out_shape=jax.ShapeDtypeStruct((most,) + held.shape[1:], jnp.float32),
        in_specs=[SMEM] + whole(1),
        out_specs=whole(1)[0],
        name="outgoing",
        **params(1 << 20),
    )(plan, held)
    crossed = lax.ppermute(outgoing, "zh", SWAP)
    return pl.pallas_call(
        slots_kernel,
        out_shape=jax.ShapeDtypeStruct(held.shape, jnp.float32),
        in_specs=[SMEM] + whole(2),
        out_specs=whole(1)[0],
        name="slots",
        **params(2 << 20),
    )(plan, held, crossed)


def placed_strip(block, rows, width):
    tiles, tops = block.shape[:2]
    placed = pl.pallas_call(
        place_kernel,
        out_shape=jax.ShapeDtypeStruct((3, tops, tiles, SUBLANES, LANES), jnp.float32),
        in_specs=whole(1),
        out_specs=HBM,
        scratch_shapes=[pltpu.SemaphoreType.DMA((3, tops))],
        name="place",
        **params(2 << 20),
    )(block)
    return placed.transpose(0, 1, 3, 2, 4).reshape(3, 1, rows, width)


PLANE = ("y", "x", "core")
SIZES = (8, 9, 10, 11, 12, 13, 14, 15, 16, 17, 18, 20, 24, 32)


def on_device(state, rain, ground, counts, slot_map):
    rows, width = ground.shape
    zh = lax.axis_index("zh").astype(jnp.int32).reshape(1)
    block, plan, level = stepped_tiles(zh, state, rain, ground, counts, slot_map, SIZES)
    shape = block.shape
    outgoing = block.reshape((lax.axis_size(PLANE), -1) + shape[2:])
    chosen = lax.switch(level[0], [functools.partial(blocks_for_slots, most=size) for size in SIZES], plan, outgoing)
    returned = lax.all_to_all(chosen, PLANE, split_axis=0, concat_axis=0, tiled=True)
    return placed_strip(returned.reshape(shape), rows, width)


def solution(mesh):
    fine = Mesh(mesh.devices.reshape(4, 4, 2, 2, 4), ("y", "x", "zh", "core", "row"))
    dom = ("y", "x", "zh", "core")
    placed = (P(None, dom, "row", None), P(dom, "row", None), P("row", None), P(), P())
    return jax.shard_map(
        on_device,
        mesh=fine,
        in_specs=placed,
        out_specs=P(None, dom, "row", None),
        check_vma=False,
    )
```
